32 devices in a mesh: seq: 8 (over z, y), ch: 4 (over x, core).
Axes of the slice: x: 2, y: 2, z: 4, core: 2. Of those that a mesh axis runs over, the one named last changes fastest.
Arguments:
- block_in: bfloat16 [49152, 768], P(('seq', 'ch')), may hold values from -24 to 24
- cotangent: bfloat16 [49152, 768], P(('seq', 'ch')), may hold values from -6 to 6
- lengths: int32 [48], replicated, may hold values from 256 to 1024, as said below
- gain_one: bfloat16 [768], replicated, may hold values from 0.099609375 to 1.8984375
- shift_one: bfloat16 [768], replicated, may hold values from -3 to 3
- dilated_w: bfloat16 [384, 3, 768], P('ch'), may hold values from -0.125 to 0.125
- gain_two: bfloat16 [384], P('ch'), may hold values from 0.099609375 to 1.8984375
- shift_two: bfloat16 [384], P('ch'), may hold values from -3 to 3
- point_w: bfloat16 [384, 768], P('ch'), may hold values from -0.3125 to 0.3125
Outputs:
- output: bfloat16 [49152, 768], P(('seq', 'ch'))
- input_grad: bfloat16 [49152, 768], P(('seq', 'ch'))
- gain_one_grad: float32 [768], replicated
- shift_one_grad: float32 [768], replicated
- dilated_grad: float32 [384, 3, 768], P('ch')
- gain_two_grad: float32 [384], P('ch')
- shift_two_grad: float32 [384], P('ch')
- point_grad: float32 [384, 768], P('ch')
The draws below stay inside these ranges and needn't reach their ends.
Inputs may be any that keep to these rules, and one draw needn't show every extreme that they name: lengths[w] counts the valid bins at the start of window w; some window is full.
All inputs are finite; a program needn't handle non-finite values.
Results may differ from the reference program's by a relative error of at most 0.0082.
Values may be sent and summed in bfloat16 or wider, within the bound.
A program may use at most 192 MiB of HBM per device.

```python
import jax
import jax.numpy as jnp
from jax import lax

C = 768
F = 384
DILATION_STEP = 17
WIN = 1024
BINS_PER_UNIT = 1536
BINS = 49152
WINDOWS = 48


def draw_block_in(key, part):
    key = jax.random.fold_in(key, 11)
    key_rows, key_cols, key_shift, key_noise = jax.random.split(key, 4)
    position_ramp = jnp.arange(BINS, dtype=jnp.float32) / BINS
    row_rough = jax.random.uniform(key_rows, (BINS,), jnp.float32)
    row_scale = 0.3 * jnp.exp(jnp.log(10.0) * (0.5 * position_ramp + 0.5 * row_rough))
    col_scale = jnp.exp(jax.random.uniform(key_cols, (C,), jnp.float32, -0.5, 0.5))
    col_shift = 0.3 * jnp.clip(jax.random.normal(key_shift, (C,), jnp.float32), -3.0, 3.0)
    noise_draw = jnp.clip(jax.random.normal(key_noise, (BINS, C), jnp.float32), -4.0, 4.0)
    drawn = col_shift[None, :] + row_scale[:, None] * col_scale[None, :] * noise_draw
    return drawn.astype(jnp.bfloat16)


def draw_lengths(key, part):
    key = jax.random.fold_in(key, 7)
    key_len, key_full = jax.random.split(key)
    drawn = jax.random.randint(key_len, (WINDOWS,), WIN // 4, WIN + 1, dtype=jnp.int32)
    full_index = jax.random.randint(key_full, (), 0, WINDOWS, dtype=jnp.int32)
    return drawn.at[full_index].set(WIN).astype(jnp.int32)


def level_of(own_key, shape, cuts, least, top_value):
    factor_of, own = 1.0, jax.random.fold_in(own_key, 6)
    for axis_at, blocks in cuts:
        heights = jnp.exp(jax.random.uniform(jax.random.fold_in(own, axis_at), (blocks,), jnp.float32, least / len(cuts), top_value / len(cuts)))
        factor_of = factor_of * jnp.repeat(heights, shape[axis_at] // blocks).reshape([-1 if axis == axis_at else 1 for axis in range(len(shape))])
    return factor_of


def centred(stream_key, extent, deviation, limit, cuts=(), held_as=jnp.bfloat16):
    values = deviation * jax.random.normal(stream_key, extent, jnp.float32)
    if cuts:
        values = values * level_of(stream_key, extent, cuts, -0.22, 0.18)
    return jnp.clip(values, -limit, limit).astype(held_as)


def setup_inputs(seed: int = 0) -> dict:
    arg_keys = jax.random.split(jax.random.key(seed), 10)
    block_in = draw_block_in(jax.random.fold_in(arg_keys[9], 71), 0)
    cotangent = centred(arg_keys[1], (BINS, C), 1.0, 6.0, ((0, 32),))
    lengths = draw_lengths(jax.random.fold_in(arg_keys[9], 71), 0)
    gain_one = jnp.clip(1.0 + 0.18 * jax.random.normal(arg_keys[3], (C,), jnp.float32), 0.099609375, 1.8984375).astype(jnp.bfloat16)
    shift_one = centred(arg_keys[4], (C,), 0.5, 3.0)
    dilated_w = centred(arg_keys[5], (F, 3, C), (3 * C) ** -0.5, 0.125, ((0, 4),))
    gain_two = jnp.clip(1.0 + 0.18 * jax.random.normal(arg_keys[6], (F,), jnp.float32), 0.099609375, 1.8984375).astype(jnp.bfloat16)
    shift_two = centred(arg_keys[7], (F,), 0.5, 3.0, ((0, 4),))
    point_w = centred(arg_keys[8], (F, C), F ** -0.5, 0.3125, ((0, 4),))
    return dict(block_in=block_in, cotangent=cotangent, lengths=lengths, gain_one=gain_one, shift_one=shift_one, dilated_w=dilated_w, gain_two=gain_two, shift_two=shift_two, point_w=point_w)


EPS = 0.001
EXACT_PRECISION = lax.Precision.HIGHEST

@jax.custom_vjp
def low(v):
    return lax.optimization_barrier(v.astype(jnp.bfloat16)).astype(jnp.float32)

@jax.custom_vjp
def low_back(v):
    return v

def low_keep(v):
    return (low(v), None)

def low_pass(kept, grad):
    return (grad,)

def back_keep(v):
    return (v, None)

def back_low(kept, grad):
    return (low(grad),)
low.defvjp(low_keep, low_pass)
low_back.defvjp(back_keep, back_low)

def gelu_tanh(inputs_v):
    return jax.nn.gelu(inputs_v, approximate=True)

def reference(block_in, cotangent, lengths, gain_one, shift_one, dilated_w, gain_two, shift_two, point_w):
    places = jnp.arange(BINS, dtype=jnp.int32)
    window_ids = jnp.floor_divide(places, WIN)
    live_flat = (places - window_ids * WIN < lengths[window_ids]).astype(jnp.float32)
    bin_count = jnp.sum(lengths).astype(jnp.float32)
    block_total = BINS // BINS_PER_UNIT
    live_blocks = live_flat.reshape(block_total, BINS_PER_UNIT)
    block_ids = jnp.arange(block_total, dtype=jnp.int32)
    x_float = block_in.astype(jnp.float32)

    def masked_stats(pair_in):
        act_block, live_block = pair_in
        act_value = gelu_tanh(act_block)
        return (lax.optimization_barrier(jnp.sum(live_block[:, None] * act_value, 0)), lax.optimization_barrier(jnp.sum(live_block[:, None] * act_value * act_value, 0)))

    def whole_block(input_complete, gain_a, shift_a, first_weight, gain_b, shift_b, weight_b):
        x_blocks = input_complete.reshape(block_total, BINS_PER_UNIT, C)
        act_sums, squares = lax.map(jax.checkpoint(masked_stats), (x_blocks, live_blocks))
        mean_a = lax.optimization_barrier(jnp.sum(act_sums, 0)) / bin_count
        inv_a = lax.rsqrt(lax.optimization_barrier(jnp.sum(squares, 0)) / bin_count - mean_a * mean_a + EPS)
        input_with_margin = jnp.pad(input_complete, ((DILATION_STEP, DILATION_STEP), (0, 0)))

        def conv_part(block_number):
            sequence_segment = lax.dynamic_slice_in_dim(input_with_margin, block_number * BINS_PER_UNIT, BINS_PER_UNIT + 2 * DILATION_STEP, 0)
            normalized_rows = low(gain_a * ((gelu_tanh(sequence_segment) - mean_a) * inv_a) + shift_a)
            rows = block_number * BINS_PER_UNIT + jnp.arange(BINS_PER_UNIT, dtype=jnp.int32)
            result = jnp.zeros((BINS_PER_UNIT, F), jnp.float32)
            for kernel_tap_index in range(3):
                kernel_tap_offset = (kernel_tap_index - 1) * DILATION_STEP
                keep_mask = (jnp.floor_divide(rows, WIN) == jnp.floor_divide(rows + kernel_tap_offset, WIN)).astype(jnp.float32)
                matrix_product = lax.dot_general(normalized_rows[kernel_tap_index * DILATION_STEP:kernel_tap_index * DILATION_STEP + BINS_PER_UNIT], first_weight[:, kernel_tap_index, :], (((1,), (1,)), ((), ())), precision=EXACT_PRECISION, preferred_element_type=jnp.float32)
                result = result + keep_mask[:, None] * matrix_product
            return result
        hidden = low_back(lax.map(jax.checkpoint(conv_part), block_ids))
        sums_b, squares_b = lax.map(jax.checkpoint(masked_stats), (hidden, live_blocks))
        mean_b = lax.optimization_barrier(jnp.sum(sums_b, 0)) / bin_count
        inv_b = lax.rsqrt(lax.optimization_barrier(jnp.sum(squares_b, 0)) / bin_count - mean_b * mean_b + EPS)

        def point_part(pair_in):
            x_block, h_block = pair_in
            normalized_rows = low(gain_b * ((gelu_tanh(h_block) - mean_b) * inv_b) + shift_b)
            return x_block + low_back(jnp.dot(normalized_rows, weight_b, precision=EXACT_PRECISION, preferred_element_type=jnp.float32))
        return lax.map(jax.checkpoint(point_part), (x_blocks, hidden))
    result, pullback = jax.vjp(whole_block, x_float, gain_one.astype(jnp.float32), shift_one.astype(jnp.float32), dilated_w.astype(jnp.float32), gain_two.astype(jnp.float32), shift_two.astype(jnp.float32), point_w.astype(jnp.float32))
    all_grads = pullback(cotangent.astype(jnp.float32).reshape(block_total, BINS_PER_UNIT, C) * live_blocks[:, :, None])
    return (result.reshape(BINS, C).astype(jnp.bfloat16), all_grads[0].astype(jnp.bfloat16), all_grads[1], all_grads[2], all_grads[3], all_grads[4], all_grads[5], all_grads[6])
```

```python
import functools
import types

import jax
import jax.numpy as jnp
from jax import lax
from jax.experimental import pallas as pl
from jax.experimental.pallas import tpu as pltpu
from jax.sharding import PartitionSpec as P

DILATION = 17
EPS = 0.001
HALO = 48
PAD = 24
LANES = 128
SPLIT = 4
MESH = pl.DeviceIdType.MESH
F32 = jnp.float32
BF16 = jnp.bfloat16
NT = (((1,), (1,)), ((), ()))
TN = (((0,), (0,)), ((), ()))
GELU_A = 0.7978845608028654
GELU_B = GELU_A * 0.044715


def gelu_half(v):
    square = v * v
    half = 0.5 + 0.5 * jnp.tanh(v * (GELU_A + GELU_B * square))
    return half, square


def gelu_slope(v, half, square):
    return half + (2.0 * v) * (half * (1.0 - half)) * (GELU_A + 3.0 * GELU_B * square)


def wide(mask, width):
    return jnp.concatenate([mask] * (width // LANES), axis=1)


def fold(value):
    rows, width = value.shape
    return jnp.sum(value.reshape(rows // 8, 8, width), axis=0)


def rows_at(start, size, step=8):
    return pl.ds(pl.multiple_of(start, step), size)


def plan(n_seq, n_ch, bins, channels, mid, n_windows):
    z = types.SimpleNamespace()
    z.n_seq, z.n_ch = n_seq, n_ch
    z.bins, z.c, z.f, z.n_windows = bins, channels, mid, n_windows
    z.share = mid // n_ch
    z.n_x = n_ch // 2
    z.n_chips = n_seq * z.n_x
    z.window = bins * n_ch * n_seq // n_windows
    z.pair_windows = 2 * bins // z.window
    z.n_lo = SPLIT
    z.n_hi = n_seq // (2 * SPLIT)
    z.ext = bins + HALO
    assert n_ch % 2 == 0 and n_seq % (2 * SPLIT) == 0
    assert 2 * bins % z.window == 0 and HALO >= 2 * DILATION
    z.ext_step = z.ext // 9
    z.ext_block = z.ext // 3
    z.own_step = bins // 8
    z.own_block = bins // 3
    assert z.ext_step % 16 == 0 and z.own_step % 16 == 0
    z.half = channels // 2
    z.piece = 2 * z.share // SPLIT
    return z


def scratch_of(z):
    dma = pltpu.SemaphoreType.DMA
    vmem = pltpu.VMEM
    return dict(
        x=vmem((z.ext, z.c), BF16),
        u=vmem((z.ext, z.c), BF16),
        x_edge=vmem((HALO, z.c), BF16),
        u_edge=vmem((HALO, z.c), BF16),
        act=vmem((z.ext, z.c), F32),
        slope=vmem((z.bins, z.c), BF16),
        normed=vmem((z.ext, z.c), BF16),
        w=vmem((4, z.f, z.c), BF16),
        taps=vmem((z.ext + 2 * PAD, 3 * z.f), F32),
        grad_two=vmem((z.ext, z.f), F32),
        act_two=vmem((z.ext, z.f), F32),
        slope_two=vmem((z.ext, z.f), F32),
        normed_two=vmem((z.ext, z.f), BF16),
        shifted=vmem((z.bins, 3 * z.f), BF16),
        live=vmem((z.ext, LANES), F32),
        live_own=vmem((z.ext, LANES), F32),
        not_first=vmem((z.ext, LANES), F32),
        not_last=vmem((z.ext, LANES), F32),
        gains=vmem((z.n_ch, 8, z.f), F32),
        **{f"own_sum_{i}": vmem((2, z.c), F32) for i in range(3)},
        **{f"pair_sum_{i}": vmem((2, z.c), F32) for i in range(3)},
        **{f"chip_sum_{i}": vmem((z.n_chips, 2, z.c), F32) for i in range(3)},
        part=vmem((4, z.f, z.c), BF16),
        **{f"from_core_{p}": vmem((z.n_x, z.share, z.c), BF16) for p in range(4)},
        from_x=vmem((4, z.n_x - 1, z.share, z.c), BF16),
        to_y=vmem((4, 2, z.share, z.half), BF16),
        from_y=vmem((4, z.share, z.half), BF16),
        to_z=vmem((4 * z.share, z.half), BF16),
        from_z=vmem((2, z.n_lo - 1, z.piece, z.half), BF16),
        hi=vmem((2, z.n_hi, z.piece, z.half), BF16),
        to_x=vmem((4, z.n_x - 1, z.share, z.c), BF16),
        mine=vmem((2, z.n_lo, z.piece, z.half), BF16),
        other=vmem((2, z.n_lo, z.piece, z.half), BF16),
        local_sem=dma((8,)),
        halo_send=dma((2,)),
        halo_recv=dma((2,)),
        gain_send=dma((z.n_ch,)),
        gain_recv=dma((z.n_ch,)),
        w_send=dma((2, z.n_x, 4)),
        w_recv=dma((z.n_ch, 4)),
        pair_send=dma((3,)),
        pair_recv=dma((3,)),
        chip_send=dma((3, z.n_chips)),
        chip_recv=dma((3, z.n_chips)),
        core_send=dma((4, z.n_x)),
        core_recv=dma((4, z.n_x)),
        x_send=dma((4, z.n_x)),
        x_recv=dma((4, z.n_x)),
        y_send=dma((4,)),
        y_recv=dma((4,)),
        z_send=dma((2, z.n_lo)),
        z_recv=dma((2, z.n_lo)),
        hi_send=dma((2, z.n_hi)),
        hi_recv=dma((2, z.n_hi)),
        zback_send=dma((2, z.n_lo)),
        zback_recv=dma((2, z.n_lo)),
        yback_send=dma((2,)),
        yback_recv=dma((2,)),
    )


def kernel(z, names, x_hbm, cot_hbm, lengths, params, w_hbm, out_hbm, grad_hbm, stats, w_grad, *scratch):
    s = types.SimpleNamespace(**dict(zip(names, scratch)))
    seq, ch = lax.axis_index("seq"), lax.axis_index("ch")
    x_at, core = ch // 2, ch % 2
    slow, y_at = seq // 2, seq % 2
    z_hi, z_lo = slow // z.n_lo, slow % z.n_lo
    chip = seq * z.n_x + x_at
    partner = (seq, x_at * 2 + 1 - core)
    y_peer = (slow * 2 + 1 - y_at, ch)
    own0 = core * HALO
    pending = []
    own_sum = (s.own_sum_0, s.own_sum_1, s.own_sum_2)
    pair_sum = (s.pair_sum_0, s.pair_sum_1, s.pair_sum_2)
    chip_sum = (s.chip_sum_0, s.chip_sum_1, s.chip_sum_2)
    from_core = (s.from_core_0, s.from_core_1, s.from_core_2, s.from_core_3)

    def remote(src, dst, send_sem, recv_sem, device):
        return pltpu.make_async_remote_copy(
            src_ref=src,
            dst_ref=dst,
            send_sem=send_sem,
            recv_sem=recv_sem,
            device_id=device,
            device_id_type=MESH,
        )

    def send(*copy):
        made = remote(*copy)
        made.start()
        pending.append(made)

    def chip_device(q):
        return (q // z.n_x, (q % z.n_x) * 2 + core)

    def other_chip(j):
        return (chip + 1 + j) % z.n_chips

    def own(j, size):
        return rows_at(own0 + j * size, size, 16)

    load_x = pltpu.make_async_copy(x_hbm, s.x.at[rows_at(own0, z.bins, 16)], s.local_sem.at[0])
    load_x.start()
    load_u = pltpu.make_async_copy(cot_hbm, s.u.at[rows_at(own0, z.bins, 16)], s.local_sem.at[1])
    load_u.start()
    own_rows = rows_at(ch * z.share, z.share, 16)
    load_w = [
        pltpu.make_async_copy(w_hbm.at[p], s.w.at[p, own_rows], s.local_sem.at[2 + p]) for p in range(4)
    ]
    for made in load_w:
        made.start()

    barrier = pltpu.get_barrier_semaphore()

    def greet(j, carry):
        pl.semaphore_signal(barrier, inc=1, device_id=chip_device(other_chip(j)), device_id_type=MESH)
        return carry

    for i in range(z.n_x):
        across = (seq, ((x_at + i) % z.n_x) * 2 + 1 - core)
        pl.semaphore_signal(barrier, inc=1, device_id=across, device_id_type=MESH)
    lax.fori_loop(0, z.n_chips - 1, greet, 0)

    pair = (seq * z.n_ch + ch) // 2
    window_lengths = [lengths[pair * z.pair_windows + i] for i in range(z.pair_windows)]

    def make_masks(j, carry):
        rows = rows_at(j * z.ext_step, z.ext_step, 16)
        at = lax.broadcasted_iota(jnp.int32, (z.ext_step, LANES), 0) + j * z.ext_step
        place = at + core * (z.bins - HALO)
        inside, limit = place, jnp.full(place.shape, window_lengths[0], jnp.int32)
        for i in range(1, z.pair_windows):
            past = place >= i * z.window
            inside = jnp.where(past, place - i * z.window, inside)
            limit = jnp.where(past, window_lengths[i], limit)
        live = (inside < limit).astype(F32)
        mine = ((at >= own0) & (at < own0 + z.bins)).astype(F32)
        s.live[rows] = live
        s.live_own[rows] = live * mine
        s.not_first[rows] = (inside >= DILATION).astype(F32)
        s.not_last[rows] = (inside < z.window - DILATION).astype(F32)
        return carry

    lax.fori_loop(0, z.ext // z.ext_step, make_masks, 0)
    bin_total = lax.fori_loop(0, z.n_windows, lambda i, t: t + lengths[i], jnp.int32(0))
    count = jnp.full((1, z.c), bin_total, jnp.int32).astype(F32)
    count_two = count[:, : z.f]
    s.taps[0:PAD] = jnp.zeros((PAD, 3 * z.f), F32)
    s.taps[PAD + z.ext : 2 * PAD + z.ext] = jnp.zeros((PAD, 3 * z.f), F32)

    chosen = lax.broadcasted_iota(jnp.int32, (LANES, z.f), 1) == (
        lax.broadcasted_iota(jnp.int32, (LANES, z.f), 0) + ch * z.share
    )
    placed = jnp.dot(params[0:16, 0:LANES].astype(BF16), chosen.astype(BF16), preferred_element_type=F32)
    s.gains[pl.ds(ch, 1)] = placed[0:8].reshape(1, 8, z.f)

    pl.semaphore_wait(barrier, z.n_chips - 1 + z.n_x)

    away = (1 - core) * (z.bins - HALO)
    halo_copies = [
        remote(src.at[rows_at(away, HALO, 16)], dst, s.halo_send.at[i], s.halo_recv.at[i], partner)
        for i, (src, dst) in enumerate(((x_hbm, s.x_edge), (cot_hbm, s.u_edge)))
    ]
    for made in halo_copies:
        made.start()
        pending.append(made)
    for p in range(4):
        for i in range(1, z.n_x):
            to = (seq, ((x_at + i) % z.n_x) * 2 + core)
            send(w_hbm.at[p], s.w.at[p, own_rows], s.w_send.at[0, i, p], s.w_recv.at[ch, p], to)
        send(w_hbm.at[p], s.w.at[p, own_rows], s.w_send.at[0, 0, p], s.w_recv.at[ch, p], partner)
    for i in range(1, z.n_ch):
        send(
            s.gains.at[pl.ds(ch, 1)],
            s.gains.at[pl.ds(ch, 1)],
            s.gain_send.at[i],
            s.gain_recv.at[ch],
            (seq, (ch + i) % z.n_ch),
        )

    def reduce_start(i):
        send(own_sum[i], pair_sum[i], s.pair_send.at[i], s.pair_recv.at[i], partner)

    def chip_copy(i, slot, j):
        return remote(
            chip_sum[i].at[slot],
            chip_sum[i].at[slot],
            s.chip_send.at[i, j],
            s.chip_recv.at[i, slot],
            chip_device(other_chip(j)),
        )

    def reduce_spread(i):
        remote(own_sum[i], pair_sum[i], s.pair_send.at[i], s.pair_recv.at[i], partner).wait_recv()
        chip_sum[i][pl.ds(chip, 1)] = (own_sum[i][...] + pair_sum[i][...]).reshape(1, 2, z.c)

        for j in range(z.n_chips - 1):
            made = chip_copy(i, chip, j)
            made.start()
            pending.append(made)

    def reduce_finish(i):
        for j in range(z.n_chips - 1):
            chip_copy(i, other_chip(j), j).wait_recv()
        return jnp.sum(chip_sum[i][...], axis=0)

    load_x.wait()

    def first_act(j, carry):
        rows = own(j, z.own_step)
        v = s.x[rows].astype(F32)
        half, _ = gelu_half(v)
        act = v * half
        s.act[rows] = act
        masked = wide(s.live[rows], z.c) * act
        return carry[0] + fold(masked), carry[1] + fold(masked * act)

    zero = jnp.zeros((8, z.c), F32)
    sums = lax.fori_loop(0, z.bins // z.own_step, first_act, (zero, zero))
    own_sum[0][0:1] = jnp.sum(sums[0], axis=0, keepdims=True)
    own_sum[0][1:2] = jnp.sum(sums[1], axis=0, keepdims=True)
    reduce_start(0)

    load_u.wait()

    def first_slope(j, carry):
        rows = own(j, z.own_step)
        v = s.x[rows].astype(F32)
        half, square = gelu_half(v)
        s.slope[rows_at(j * z.own_step, z.own_step, 16)] = gelu_slope(v, half, square).astype(BF16)
        s.u[rows] = (s.u[rows].astype(F32) * wide(s.live[rows], z.c)).astype(BF16)
        return carry

    def halo_rows():
        return rows_at((1 - core) * z.bins, HALO, 16)

    reduce_spread(0)
    lax.fori_loop(0, z.bins // z.own_step, first_slope, 0)
    for made in halo_copies:
        made.wait_recv()
    edge = s.x_edge[...].astype(F32)
    s.act[halo_rows()] = edge * gelu_half(edge)[0]
    s.u[halo_rows()] = (s.u_edge[...].astype(F32) * wide(s.live[halo_rows()], z.c)).astype(BF16)

    def w_copy(slot, i, p):
        rows = rows_at(slot * z.share, z.share, 16)
        return remote(
            s.w.at[p, rows], s.w.at[p, rows], s.w_send.at[1, i, p], s.w_recv.at[slot, p], partner
        )

    for p in range(4):
        for i in range(1, z.n_x):
            made = w_copy(((x_at + i) % z.n_x) * 2 + core, i, p)
            made.wait_recv()
            made.start()
            pending.append(made)
    for p in range(4):
        for i in range(z.n_x):
            w_copy(((x_at + i) % z.n_x) * 2 + 1 - core, i, p).wait_recv()
        load_w[p].wait()
    for i in range(1, z.n_ch):
        slot = (ch + i) % z.n_ch
        remote(
            s.gains.at[pl.ds(slot, 1)],
            s.gains.at[pl.ds(slot, 1)],
            s.gain_send.at[i],
            s.gain_recv.at[slot],
            (seq, slot),
        ).wait_recv()
    both = s.gains[0]
    for i in range(1, z.n_ch):
        both = both + s.gains[i]
    gain_two, shift_two = both[0:1], both[1:2]

    def second_grad(j, carry):
        rows = rows_at(j * z.ext_block, z.ext_block, 16)
        s.grad_two[rows] = lax.dot_general(s.u[rows], s.w[0], NT, preferred_element_type=F32)
        return carry

    lax.fori_loop(0, 3, second_grad, 0)

    one = reduce_finish(0)
    gain_one, shift_one = params[8:9], params[9:10]
    mean_one = one[0:1] / count
    inv_one = lax.rsqrt(one[1:2] / count - mean_one * mean_one + EPS)
    scale_one = gain_one * inv_one
    offset_one = shift_one - mean_one * scale_one

    def first_norm(j, carry):
        rows = rows_at(j * z.ext_step, z.ext_step, 16)
        s.normed[rows] = (s.act[rows] * scale_one + offset_one).astype(BF16)
        return carry

    lax.fori_loop(0, z.ext // z.ext_step, first_norm, 0)

    def convolve(j, carry):
        rows = rows_at(j * z.ext_block, z.ext_block, 16)
        s.taps[rows_at(PAD + j * z.ext_block, z.ext_block)] = lax.dot_general(
            s.normed[rows], s.w[1:4].reshape(3 * z.f, z.c), NT, preferred_element_type=F32
        )
        return carry

    lax.fori_loop(0, 3, convolve, 0)

    def before(start, size, columns):
        return s.taps[rows_at(start, size + 8), columns][PAD - DILATION : PAD - DILATION + size]

    def after(start, size, columns):
        low = (PAD + DILATION) // 8 * 8
        skip = PAD + DILATION - low
        return s.taps[rows_at(start + low, size + 8), columns][skip : skip + size]

    def column(k):
        return slice(k * z.f, (k + 1) * z.f)

    def second_act(j, carry):
        start, size = j * z.ext_step, z.ext_step
        rows = rows_at(start, size, 16)
        hidden = (
            s.taps[rows_at(PAD + start, size), column(1)]
            + wide(s.not_first[rows], z.f) * before(start, size, column(0))
            + wide(s.not_last[rows], z.f) * after(start, size, column(2))
        )
        half, square = gelu_half(hidden)
        act = hidden * half
        s.act_two[rows] = act
        s.slope_two[rows] = gelu_slope(hidden, half, square)
        mask = wide(s.live_own[rows], z.f)
        masked, grad = mask * act, mask * s.grad_two[rows]
        terms = (masked, masked * act, grad, grad * act)
        return tuple(total + fold(term) for total, term in zip(carry, terms))

    zero_two = jnp.zeros((8, z.f), F32)
    sums = lax.fori_loop(0, z.ext // z.ext_step, second_act, (zero_two,) * 4)
    sums = [jnp.sum(v, axis=0, keepdims=True) for v in sums]
    own_sum[1][0:1, : z.f] = sums[0]
    own_sum[1][0:1, z.f :] = sums[1]
    own_sum[1][1:2, : z.f] = sums[2]
    own_sum[1][1:2, z.f :] = sums[3]
    reduce_start(1)
    reduce_spread(1)
    two = reduce_finish(1)
    mean_two = two[0:1, : z.f] / count_two
    inv_two = lax.rsqrt(two[0:1, z.f :] / count_two - mean_two * mean_two + EPS)
    shift_two_grad = two[1:2, : z.f]
    gain_two_grad = inv_two * (two[1:2, z.f :] - mean_two * shift_two_grad)
    stats[2:3, : z.f] = gain_two_grad
    stats[2:3, z.f :] = shift_two_grad
    scale_two = gain_two * inv_two
    back_a = shift_two_grad / count_two
    back_b = gain_two_grad / count_two

    def second_norm(j, carry):
        rows = rows_at(j * z.ext_step, z.ext_step, 16)
        centred = (s.act_two[rows] - mean_two) * inv_two
        s.normed_two[rows] = (gain_two * centred + shift_two).astype(BF16)
        grad = scale_two * (s.grad_two[rows] - wide(s.live[rows], z.f) * (back_a + back_b * centred))
        s.taps[rows_at(PAD + j * z.ext_step, z.ext_step), column(2)] = grad * s.slope_two[rows]
        return carry

    lax.fori_loop(0, z.ext // z.ext_step, second_norm, 0)

    own_all = rows_at(own0, z.bins, 16)

    def slot_rows(x_slot, c_slot):
        return rows_at((x_slot * 2 + c_slot) * z.share, z.share, 16)

    def core_copy(p, i):
        return remote(
            s.part.at[p, slot_rows(i, 1 - core)],
            from_core[p].at[i],
            s.core_send.at[p, i],
            s.core_recv.at[p, i],
            partner,
        )

    def core_stage(p):
        for i in range(z.n_x):
            made = core_copy(p, i)
            made.start()
            pending.append(made)

    def x_copy(p, i):
        to = (x_at + i) % z.n_x
        return remote(
            s.to_x.at[p, i - 1],
            s.from_x.at[p, i - 1],
            s.x_send.at[p, i],
            s.x_recv.at[p, i],
            (seq, to * 2 + core),
        )

    def x_stage(p):
        for i in range(z.n_x):
            core_copy(p, i).wait_recv()
        for i in range(1, z.n_x):
            to = (x_at + i) % z.n_x
            rows = slot_rows(to, core)
            s.to_x[p, i - 1] = (s.part[p, rows].astype(F32) + from_core[p][to].astype(F32)).astype(BF16)
            made = x_copy(p, i)
            made.start()
            pending.append(made)

    def y_copy(p):
        return remote(s.to_y.at[p, 1 - y_at], s.from_y.at[p], s.y_send.at[p], s.y_recv.at[p], y_peer)

    def y_stage(p):
        value = s.part[p, slot_rows(x_at, core)].astype(F32) + from_core[p][x_at].astype(F32)
        for i in range(1, z.n_x):
            x_copy(p, i).wait_recv()
            value = value + s.from_x[p, i - 1].astype(F32)
        value = value.astype(BF16)
        s.to_y[p, 0] = value[:, : z.half]
        s.to_y[p, 1] = value[:, z.half :]
        made = y_copy(p)
        made.start()
        pending.append(made)

    def piece_rows(h, i):
        return rows_at(h * 2 * z.share + i * z.piece, z.piece, 16)

    def z_device(i):
        return ((z_hi * z.n_lo + i) * 2 + y_at, ch)

    def z_copy(h, i):
        to = (z_lo + i) % z.n_lo
        return remote(
            s.to_z.at[piece_rows(h, to)],
            s.from_z.at[h, i - 1],
            s.z_send.at[h, i],
            s.z_recv.at[h, i],
            z_device(to),
        )

    def z_stage(h):
        for p in (2 * h, 2 * h + 1):
            y_copy(p).wait_recv()
            value = s.to_y[p, y_at].astype(F32) + s.from_y[p].astype(F32)
            s.to_z[p * z.share : (p + 1) * z.share] = value.astype(BF16)
        for i in range(1, z.n_lo):
            made = z_copy(h, i)
            made.start()
            pending.append(made)

    def back_copy(h, i, at):
        return remote(
            s.mine.at[h, at],
            s.mine.at[h, at],
            s.zback_send.at[h, i],
            s.zback_recv.at[h, at],
            z_device((z_lo + i) % z.n_lo),
        )

    def hi_copy(h, i, at):
        return remote(
            s.hi.at[h, at],
            s.hi.at[h, at],
            s.hi_send.at[h, i],
            s.hi_recv.at[h, at],
            ((((z_hi + i) % z.n_hi) * z.n_lo + z_lo) * 2 + y_at, ch),
        )

    def z_back_stage(h):
        value = s.to_z[piece_rows(h, z_lo)].astype(F32)
        for i in range(1, z.n_lo):
            z_copy(h, i).wait_recv()
            value = value + s.from_z[h, i - 1].astype(F32)
        if z.n_hi > 1:
            s.hi[h, pl.ds(z_hi, 1)] = value.astype(BF16).reshape(1, z.piece, z.half)
            for i in range(1, z.n_hi):
                made = hi_copy(h, i, z_hi)
                made.start()
                pending.append(made)
            for i in range(1, z.n_hi):
                hi_copy(h, i, (z_hi + i) % z.n_hi).wait_recv()
            value = s.hi[h, 0].astype(F32)
            for i in range(1, z.n_hi):
                value = value + s.hi[h, i].astype(F32)
        s.mine[h, pl.ds(z_lo, 1)] = value.astype(BF16).reshape(1, z.piece, z.half)
        for i in range(1, z.n_lo):
            made = back_copy(h, i, z_lo)
            made.start()
            pending.append(made)

    def yback_copy(h):
        return remote(s.mine.at[h], s.other.at[h], s.yback_send.at[h], s.yback_recv.at[h], y_peer)

    def y_back_stage(h):
        for i in range(1, z.n_lo):
            back_copy(h, i, (z_lo + i) % z.n_lo).wait_recv()
        made = yback_copy(h)
        made.start()
        pending.append(made)

    def last_stage(h):
        yback_copy(h).wait_recv()
        for side, held in ((y_at, s.mine), (1 - y_at, s.other)):
            value = held[h].reshape(2, z.share, z.half).astype(F32)
            w_grad[2 * h : 2 * h + 2, :, rows_at(side * z.half, z.half, LANES)] = value

    s.part[0] = lax.dot_general(
        s.normed_two[own_all], s.u[own_all], TN, preferred_element_type=F32
    ).astype(BF16)
    core_stage(0)

    def shift_rows(j, carry):
        start, size = own0 + j * z.own_step, z.own_step
        rows = rows_at(start, size, 16)
        to = rows_at(j * size, size, 16)
        later = wide(s.not_last[rows], z.f) * after(start, size, column(2))
        earlier = wide(s.not_first[rows], z.f) * before(start, size, column(2))
        s.shifted[to, column(0)] = later.astype(BF16)
        s.shifted[to, column(1)] = s.taps[rows_at(PAD + start, size), column(2)].astype(BF16)
        s.shifted[to, column(2)] = earlier.astype(BF16)
        return carry

    lax.fori_loop(0, z.bins // z.own_step, shift_rows, 0)
    for k in range(3):
        s.part[k + 1] = lax.dot_general(
            s.shifted[:, column(k)], s.normed[own_all], TN, preferred_element_type=F32
        ).astype(BF16)
        core_stage(k + 1)
        x_stage(k)

    def first_grad(j, carry):
        rows = rows_at(j * z.own_block, z.own_block, 16)
        s.taps[rows_at(PAD + j * z.own_block, z.own_block), : z.c] = jnp.dot(
            s.shifted[rows], s.w[1:4].reshape(3 * z.f, z.c), preferred_element_type=F32
        )
        return carry

    lax.fori_loop(0, 3, first_grad, 0)
    x_stage(3)
    scale_back, offset_back = inv_one, -mean_one * inv_one

    def held(j):
        return rows_at(PAD + j * z.own_step, z.own_step)

    def first_sums(j, carry):
        grad = s.taps[held(j), : z.c]
        centred = s.act[own(j, z.own_step)] * scale_back + offset_back
        return carry[0] + fold(grad), carry[1] + fold(grad * centred)

    sums = lax.fori_loop(0, z.bins // z.own_step, first_sums, (zero, zero))
    own_sum[2][0:1] = jnp.sum(sums[0], axis=0, keepdims=True)
    own_sum[2][1:2] = jnp.sum(sums[1], axis=0, keepdims=True)
    reduce_start(2)
    reduce_spread(2)

    def block_out(j, carry):
        rows = own(j, z.own_block)
        branch = jnp.dot(s.normed_two[rows], s.w[0], preferred_element_type=F32)
        s.x[rows] = (s.x[rows].astype(F32) + branch).astype(BF16)
        return carry

    lax.fori_loop(0, 3, block_out, 0)
    store_out = pltpu.make_async_copy(s.x.at[own_all], out_hbm, s.local_sem.at[6])
    store_out.start()
    y_stage(0)
    y_stage(1)
    z_stage(0)

    three = reduce_finish(2)
    shift_one_grad, gain_one_grad = three[0:1], three[1:2]
    stats[0:1] = gain_one_grad
    stats[1:2] = shift_one_grad
    first_a = shift_one_grad / count
    first_b = gain_one_grad / count

    def input_grad(j, carry):
        rows = own(j, z.own_step)
        centred = s.act[rows] * scale_back + offset_back
        grad = scale_one * (
            s.taps[held(j), : z.c] - wide(s.live[rows], z.c) * (first_a + first_b * centred)
        )
        slope = s.slope[rows_at(j * z.own_step, z.own_step, 16)].astype(F32)
        s.u[rows] = (s.u[rows].astype(F32) + grad * slope).astype(BF16)
        return carry

    lax.fori_loop(0, z.bins // z.own_step, input_grad, 0)
    store_grad = pltpu.make_async_copy(s.u.at[own_all], grad_hbm, s.local_sem.at[7])
    store_grad.start()

    y_stage(2)
    z_back_stage(0)
    y_stage(3)
    z_stage(1)
    y_back_stage(0)
    z_back_stage(1)
    last_stage(0)
    y_back_stage(1)
    last_stage(1)

    for made in pending:
        made.wait_send()
    store_out.wait()
    store_grad.wait()


def local(z, block_in, cotangent, lengths, gain_one, shift_one, dilated_w, gain_two, shift_two, point_w):
    def row(values):
        return jnp.pad(values.astype(F32), (0, z.c - values.shape[0]))[None]

    params = jnp.concatenate(
        [row(gain_two), row(shift_two), jnp.zeros((6, z.c), F32), row(gain_one), row(shift_one), jnp.zeros((6, z.c), F32)]
    )
    weights = jnp.concatenate([point_w[None], jnp.transpose(dilated_w, (1, 0, 2))], axis=0)
    names = scratch_of(z)
    hbm = pl.BlockSpec(memory_space=pl.ANY)
    vmem = pl.BlockSpec(memory_space=pltpu.VMEM)
    output, input_grad, stats, w_grad = pl.pallas_call(
        functools.partial(kernel, z, tuple(names)),
        out_shape=(
            jax.ShapeDtypeStruct((z.bins, z.c), BF16),
            jax.ShapeDtypeStruct((z.bins, z.c), BF16),
            jax.ShapeDtypeStruct((8, z.c), F32),
            jax.ShapeDtypeStruct((4, z.share, z.c), F32),
        ),
        in_specs=[hbm, hbm, pl.BlockSpec(memory_space=pltpu.SMEM), vmem, hbm],
        out_specs=(hbm, hbm, vmem, vmem),
        scratch_shapes=list(names.values()),
        compiler_params=pltpu.CompilerParams(
            collective_id=0, has_side_effects=True, vmem_limit_bytes=60 * 2**20
        ),
    )(block_in, cotangent, lengths, params, weights)
    mine = lax.dynamic_slice_in_dim(
        stats[2].reshape(2, z.f), lax.axis_index("ch") * z.share, z.share, axis=1
    )
    return (
        output,
        input_grad,
        stats[0],
        stats[1],
        jnp.transpose(w_grad[1:4], (1, 0, 2)),
        mine[0],
        mine[1],
        w_grad[0],
    )


def solution(mesh):
    n_seq, n_ch = mesh.shape["seq"], mesh.shape["ch"]

    def run(block_in, cotangent, lengths, gain_one, shift_one, dilated_w, gain_two, shift_two, point_w):
        z = plan(
            n_seq, n_ch, block_in.shape[0], block_in.shape[1], dilated_w.shape[0] * n_ch, lengths.shape[0]
        )
        return local(
            z, block_in, cotangent, lengths, gain_one, shift_one, dilated_w, gain_two, shift_two, point_w
        )

    return jax.shard_map(
        run,
        mesh=mesh,
        in_specs=(
            P(("seq", "ch"), None),
            P(("seq", "ch"), None),
            P(),
            P(),
            P(),
            P("ch", None, None),
            P("ch"),
            P("ch"),
            P("ch", None),
        ),
        out_specs=(
            P(("seq", "ch"), None),
            P(("seq", "ch"), None),
            P(),
            P(),
            P("ch", None, None),
            P("ch"),
            P("ch"),
            P("ch", None),
        ),
        check_vma=False,
    )
```

```python
import functools
import types

import jax
import jax.numpy as jnp
from jax import lax
from jax.experimental import pallas as pl
from jax.experimental.pallas import tpu as pltpu
from jax.sharding import PartitionSpec as P

DILATION = 17
EPS = 0.001
HALO = 48
PAD = 24
LANES = 128
VMEM_LIMIT = 58 * 2**20
SPLIT = 4
MESH = pl.DeviceIdType.MESH
F32 = jnp.float32
BF16 = jnp.bfloat16
NT = (((1,), (1,)), ((), ()))
TN = (((0,), (0,)), ((), ()))
GELU_A = 0.7978845608028654
GELU_B = GELU_A * 0.044715


def gelu_half(v):
    square = v * v
    half = 0.5 + 0.5 * jnp.tanh(v * (GELU_A + GELU_B * square))
    return half, square


def gelu_slope(v, half, square):
    return half + (2.0 * v) * (half * (1.0 - half)) * (GELU_A + 3.0 * GELU_B * square)


def wide(mask, width):
    return jnp.concatenate([mask] * (width // LANES), axis=1)


def fold(value):
    rows, width = value.shape
    return jnp.sum(value.reshape(rows // 8, 8, width), axis=0)


def rows_at(start, size, step=8):
    return pl.ds(pl.multiple_of(start, step), size)


def plan(n_seq, n_ch, bins, channels, mid, n_windows):
    z = types.SimpleNamespace()
    z.n_seq, z.n_ch = n_seq, n_ch
    z.bins, z.c, z.f, z.n_windows = bins, channels, mid, n_windows
    z.share = mid // n_ch
    z.n_x = n_ch // 2
    z.n_chips = n_seq * z.n_x
    z.window = bins * n_ch * n_seq // n_windows
    z.pair_windows = 2 * bins // z.window
    z.n_lo = SPLIT
    z.n_hi = n_seq // (2 * SPLIT)
    z.ext = bins + HALO
    assert n_ch % 2 == 0 and n_seq % (2 * SPLIT) == 0
    assert 2 * bins % z.window == 0 and HALO >= 2 * DILATION
    z.ext_step = z.ext // 9
    z.ext_block = z.ext // 3
    z.own_step = bins // 8
    z.own_block = bins // 3
    assert z.ext_step % 16 == 0 and z.own_step % 16 == 0
    z.thirds = 3
    z.third = channels // z.thirds
    z.half = z.third // 2
    z.piece = 2 * z.share // SPLIT
    z.near = z.share // 2
    return z


def scratch_of(z):
    dma = pltpu.SemaphoreType.DMA
    vmem = pltpu.VMEM
    return dict(
        x=vmem((z.ext, z.c), BF16),
        u=vmem((z.ext, z.c), BF16),
        x_edge=vmem((HALO, z.c), BF16),
        u_edge=vmem((HALO, z.c), BF16),
        act=vmem((z.ext, z.c), F32),
        slope=vmem((z.bins, z.c), BF16),
        normed=vmem((z.ext, z.c), BF16),
        w=vmem((4, z.f, z.c), BF16),
        taps=vmem((z.ext + 2 * PAD, 3 * z.f), F32),
        grad_two=vmem((z.ext, z.f), F32),
        act_two=vmem((z.ext, z.f), F32),
        slope_two=vmem((z.ext, z.f), F32),
        shifted=vmem((z.bins, 3 * z.f), BF16),
        live=vmem((z.ext, LANES), F32),
        live_own=vmem((z.ext, LANES), F32),
        not_first=vmem((z.ext, LANES), F32),
        not_last=vmem((z.ext, LANES), F32),
        gains=vmem((z.n_ch, 8, z.f), F32),
        **{f"own_sum_{i}": vmem((2, z.c), F32) for i in range(3)},
        **{f"pair_sum_{i}": vmem((2, z.c), F32) for i in range(3)},
        **{f"chip_sum_{i}": vmem((z.n_chips, 2, z.c), F32) for i in range(3)},
        centred=vmem((z.bins, z.f), BF16),
        point=vmem((z.f, z.c), F32),
        part=vmem((4, z.thirds, z.f, z.third), BF16),
        **{f"from_core_{p}": vmem((z.n_x, z.thirds, z.share, z.third), BF16) for p in range(4)},
        to_x=vmem((4, z.n_x - 1, z.thirds, z.share, z.third), BF16),
        from_x=vmem((4, z.n_x - 1, z.thirds, z.share, z.third), BF16),
        held_y=vmem((2, z.thirds, 2, 2 * z.share, z.half), F32),
        to_y=vmem((2, z.thirds, 2, 2 * z.share, z.half), BF16),
        from_y=vmem((2, z.thirds, 2 * z.share, z.half), BF16),
        held_z=vmem((2, z.thirds, 2 * z.share, z.half), F32),
        to_z=vmem((2, z.thirds, 2 * z.share, z.half), BF16),
        from_z=vmem((2, z.thirds, z.n_lo - 1, z.piece, z.half), BF16),
        hi=vmem((2, z.thirds, z.n_hi, z.piece, z.half), BF16),
        mine=vmem((2, z.thirds, z.n_lo, z.piece, z.half), BF16),
        other=vmem((2, z.thirds, z.n_lo, z.piece, z.half), BF16),
        local_sem=dma((6,)),
        halo_send=dma((2,)),
        halo_recv=dma((2,)),
        gain_send=dma((z.n_ch,)),
        gain_recv=dma((z.n_ch,)),
        w_send=dma((4, z.n_x, 4)),
        w_recv=dma((4, z.n_x, 4)),
        pair_send=dma((3,)),
        pair_recv=dma((3,)),
        chip_send=dma((3, z.n_chips)),
        chip_recv=dma((3, z.n_chips)),
        core_send=dma((4, z.n_x)),
        core_recv=dma((4, z.n_x)),
        x_send=dma((4, z.thirds, z.n_x)),
        x_recv=dma((4, z.thirds, z.n_x)),
        y_send=dma((2, z.thirds)),
        y_recv=dma((2, z.thirds)),
        z_send=dma((2, z.thirds, z.n_lo)),
        z_recv=dma((2, z.thirds, z.n_lo)),
        hi_send=dma((2, z.thirds, z.n_hi)),
        hi_recv=dma((2, z.thirds, z.n_hi)),
        zback_send=dma((2, z.thirds, z.n_lo)),
        zback_recv=dma((2, z.thirds, z.n_lo)),
        yback_send=dma((2, z.thirds, z.n_lo)),
        yback_recv=dma((2, z.thirds, z.n_lo)),
    )


def kernel(
    z,
    names,
    x_hbm,
    cot_hbm,
    lengths,
    gain_one,
    shift_one,
    taps_hbm,
    gain_two,
    shift_two,
    point_hbm,
    out,
    out_grad,
    stats,
    w_grad,
    *scratch,
):
    s = types.SimpleNamespace(**dict(zip(names, scratch)))
    seq, ch = lax.axis_index("seq"), lax.axis_index("ch")
    x_at, core = ch // 2, ch % 2
    slow, y_at = seq // 2, seq % 2
    z_hi, z_lo = slow // z.n_lo, slow % z.n_lo
    chip = seq * z.n_x + x_at
    partner = (seq, x_at * 2 + 1 - core)
    y_peer = (slow * 2 + 1 - y_at, ch)
    own0 = core * HALO
    pending = []
    own_sum = (s.own_sum_0, s.own_sum_1, s.own_sum_2)
    pair_sum = (s.pair_sum_0, s.pair_sum_1, s.pair_sum_2)
    chip_sum = (s.chip_sum_0, s.chip_sum_1, s.chip_sum_2)
    from_core = (s.from_core_0, s.from_core_1, s.from_core_2, s.from_core_3)

    def remote(src, dst, send_sem, recv_sem, device):
        return pltpu.make_async_remote_copy(
            src_ref=src,
            dst_ref=dst,
            send_sem=send_sem,
            recv_sem=recv_sem,
            device_id=device,
            device_id_type=MESH,
        )

    def send(*copy):
        made = remote(*copy)
        made.start()
        pending.append(made)

    def chip_device(q):
        return (q // z.n_x, (q % z.n_x) * 2 + core)

    def other_chip(j):
        return (chip + 1 + j) % z.n_chips

    def own(j, size):
        return rows_at(own0 + j * size, size, 16)

    def column(k):
        return slice(k * z.f, (k + 1) * z.f)

    load_x = pltpu.make_async_copy(x_hbm, s.x.at[rows_at(own0, z.bins, 16)], s.local_sem.at[0])
    load_x.start()
    load_u = pltpu.make_async_copy(cot_hbm, s.u.at[rows_at(own0, z.bins, 16)], s.local_sem.at[1])
    load_u.start()
    own_rows = rows_at(ch * z.share, z.share, 16)
    sources = [point_hbm, taps_hbm.at[0], taps_hbm.at[1], taps_hbm.at[2]]
    load_w = [
        pltpu.make_async_copy(src, s.w.at[p, own_rows], s.local_sem.at[2 + p]) for p, src in enumerate(sources)
    ]
    for made in load_w:
        made.start()

    barrier = pltpu.get_barrier_semaphore()

    def greet(j, carry):
        pl.semaphore_signal(barrier, inc=1, device_id=chip_device(other_chip(j)), device_id_type=MESH)
        return carry

    for i in range(z.n_x):
        across = (seq, ((x_at + i) % z.n_x) * 2 + 1 - core)
        pl.semaphore_signal(barrier, inc=1, device_id=across, device_id_type=MESH)
    lax.fori_loop(0, z.n_chips - 1, greet, 0)

    pair = (seq * z.n_ch + ch) // 2
    window_lengths = [lengths[pair * z.pair_windows + i] for i in range(z.pair_windows)]

    def make_masks(j, total):
        rows = rows_at(j * z.ext_step, z.ext_step, 16)
        at = lax.broadcasted_iota(jnp.int32, (z.ext_step, LANES), 0) + j * z.ext_step
        place = at + core * (z.bins - HALO)
        inside, limit = place, jnp.full(place.shape, window_lengths[0], jnp.int32)
        for i in range(1, z.pair_windows):
            past = place >= i * z.window
            inside = jnp.where(past, place - i * z.window, inside)
            limit = jnp.where(past, window_lengths[i], limit)
        live = (inside < limit).astype(F32)
        mine = ((at >= own0) & (at < own0 + z.bins)).astype(F32)
        s.live[rows] = live
        s.live_own[rows] = live * mine
        s.not_first[rows] = (inside >= DILATION).astype(F32)
        s.not_last[rows] = (inside < z.window - DILATION).astype(F32)
        return total + fold(live * mine)

    live_rows = lax.fori_loop(0, z.ext // z.ext_step, make_masks, jnp.zeros((8, LANES), F32))
    own_count = jnp.maximum(wide(jnp.sum(live_rows, axis=0, keepdims=True), z.f), 1.0)
    bin_total = lax.fori_loop(0, z.n_windows, lambda i, t: t + lengths[i], jnp.int32(0))
    count = jnp.full((1, z.c), bin_total, jnp.int32).astype(F32)
    count_two = count[:, : z.f]
    s.taps[0:PAD] = jnp.zeros((PAD, 3 * z.f), F32)
    s.taps[PAD + z.ext : 2 * PAD + z.ext] = jnp.zeros((PAD, 3 * z.f), F32)

    chosen = lax.broadcasted_iota(jnp.int32, (z.share, z.f), 1) == (
        lax.broadcasted_iota(jnp.int32, (z.share, z.f), 0) + ch * z.share
    )
    both = [v[...].astype(F32).reshape(1, z.share) for v in (gain_two, shift_two)]
    both = jnp.concatenate(both + [jnp.zeros((6, z.share), F32)], axis=0)
    placed = jnp.dot(both.astype(BF16), chosen.astype(BF16), preferred_element_type=F32)
    s.gains[pl.ds(ch, 1)] = placed.reshape(1, 8, z.f)

    load_x.wait()

    def first_act(j, carry):
        rows = own(j, z.own_step)
        v = s.x[rows].astype(F32)
        half, _ = gelu_half(v)
        act = v * half
        s.act[rows] = act
        masked = wide(s.live[rows], z.c) * act
        return carry[0] + fold(masked), carry[1] + fold(masked * act)

    zero = jnp.zeros((8, z.c), F32)
    steps = z.bins // z.own_step
    sums = lax.fori_loop(0, steps // 2, first_act, (zero, zero))

    pl.semaphore_wait(barrier, z.n_chips - 1 + z.n_x)

    order = (1, 2, 3, 0)
    near0 = y_at * z.near

    def slot_at(i, c_slot):
        return ((x_at + i) % z.n_x) * 2 + c_slot

    def half_rows(slot, y_half):
        return rows_at(slot * z.share + y_half * z.near, z.near, 16)

    def w_copy(kind, i, p, src, rows, to):
        return remote(src, s.w.at[p, rows], s.w_send.at[kind, i, p], s.w_recv.at[kind, i, p], to)

    for p in order:
        for i in range(1, z.n_x):
            send_w = w_copy(
                0,
                i,
                p,
                sources[p].at[rows_at(near0, z.near, 16)],
                half_rows(ch, y_at),
                (seq, slot_at(i, core)),
            )
            send_w.start()
            pending.append(send_w)
        send_w = w_copy(0, 0, p, sources[p], own_rows, partner)
        send_w.start()
        pending.append(send_w)

    def w_pass(kind, p):
        for i in range(1, z.n_x):
            rows = half_rows(slot_at(z.n_x - i, core), y_at if kind == 0 else 1 - y_at)
            here = s.w.at[p, rows]
            w_copy(kind, i, p, here, rows, partner).wait_recv()
            onward = [w_copy(2 + kind, i, p, here, rows, partner)]
            if kind == 0:
                onward.append(w_copy(1, i, p, here, rows, y_peer))
            for made in onward:
                made.start()
                pending.append(made)

    def w_here(p):
        load_w[p].wait()
        whole = rows_at(slot_at(0, 1 - core) * z.share, z.share, 16)
        w_copy(0, 0, p, sources[p], whole, partner).wait_recv()
        for i in range(1, z.n_x):
            for kind in range(2):
                rows = half_rows(slot_at(z.n_x - i, 1 - core), y_at if kind == 0 else 1 - y_at)
                w_copy(2 + kind, i, p, s.w.at[p, rows], rows, partner).wait_recv()

    away = (1 - core) * (z.bins - HALO)
    halo_copies = [
        remote(src.at[rows_at(away, HALO, 16)], dst, s.halo_send.at[i], s.halo_recv.at[i], partner)
        for i, (src, dst) in enumerate(((x_hbm, s.x_edge), (cot_hbm, s.u_edge)))
    ]
    for made in halo_copies:
        made.start()
        pending.append(made)
    for i in range(1, z.n_ch):
        send(
            s.gains.at[pl.ds(ch, 1)],
            s.gains.at[pl.ds(ch, 1)],
            s.gain_send.at[i],
            s.gain_recv.at[ch],
            (seq, (ch + i) % z.n_ch),
        )

    def reduce_start(i):
        send(own_sum[i], pair_sum[i], s.pair_send.at[i], s.pair_recv.at[i], partner)

    def chip_copy(i, slot, j):
        return remote(
            chip_sum[i].at[slot],
            chip_sum[i].at[slot],
            s.chip_send.at[i, j],
            s.chip_recv.at[i, slot],
            chip_device(other_chip(j)),
        )

    def reduce_spread(i):
        remote(own_sum[i], pair_sum[i], s.pair_send.at[i], s.pair_recv.at[i], partner).wait_recv()
        chip_sum[i][pl.ds(chip, 1)] = (own_sum[i][...] + pair_sum[i][...]).reshape(1, 2, z.c)

        for j in range(z.n_chips - 1):
            made = chip_copy(i, chip, j)
            made.start()
            pending.append(made)

    def reduce_finish(i):
        for j in range(z.n_chips - 1):
            chip_copy(i, other_chip(j), j).wait_recv()
        return jnp.sum(chip_sum[i][...], axis=0)

    sums = lax.fori_loop(steps // 2, steps, first_act, sums)
    own_sum[0][0:1] = jnp.sum(sums[0], axis=0, keepdims=True)
    own_sum[0][1:2] = jnp.sum(sums[1], axis=0, keepdims=True)
    reduce_start(0)

    load_u.wait()

    def first_slope(j, total):
        rows = own(j, z.own_step)
        v = s.x[rows].astype(F32)
        half, square = gelu_half(v)
        s.slope[rows_at(j * z.own_step, z.own_step, 16)] = gelu_slope(v, half, square).astype(BF16)
        masked = s.u[rows].astype(F32) * wide(s.live[rows], z.c)
        s.u[rows] = masked.astype(BF16)
        return total + fold(masked)

    def halo_rows():
        return rows_at((1 - core) * z.bins, HALO, 16)

    u_sum = lax.fori_loop(0, steps // 2, first_slope, zero)
    reduce_spread(0)
    w_pass(0, 1)
    u_sum = lax.fori_loop(steps // 2, steps, first_slope, u_sum)
    w_pass(0, 2)
    for made in halo_copies:
        made.wait_recv()
    edge = s.x_edge[...].astype(F32)
    s.act[halo_rows()] = edge * gelu_half(edge)[0]
    s.u[halo_rows()] = (s.u_edge[...].astype(F32) * wide(s.live[halo_rows()], z.c)).astype(BF16)
    w_pass(0, 3)
    w_pass(1, 1)
    u_sum = jnp.sum(u_sum, axis=0, keepdims=True)

    for i in range(1, z.n_ch):
        slot = (ch + i) % z.n_ch
        remote(
            s.gains.at[pl.ds(slot, 1)],
            s.gains.at[pl.ds(slot, 1)],
            s.gain_send.at[i],
            s.gain_recv.at[slot],
            (seq, slot),
        ).wait_recv()
    both = s.gains[0]
    for i in range(1, z.n_ch):
        both = both + s.gains[i]
    whole_gain, whole_shift = both[0:1], both[1:2]

    one = reduce_finish(0)
    mean_one = one[0:1] / count
    inv_one = lax.rsqrt(one[1:2] / count - mean_one * mean_one + EPS)
    scale_one = gain_one[...].astype(F32).reshape(1, z.c) * inv_one
    offset_one = shift_one[...].astype(F32).reshape(1, z.c) - mean_one * scale_one

    def first_norm(j, carry):
        rows = rows_at(j * z.ext_step, z.ext_step, 16)
        s.normed[rows] = (s.act[rows] * scale_one + offset_one).astype(BF16)
        return carry

    lax.fori_loop(0, z.ext // z.ext_step, first_norm, 0)

    w_pass(1, 2)
    w_pass(0, 0)
    for k in range(3):

        def convolve(j, carry):
            s.taps[rows_at(PAD + j * z.ext_block, z.ext_block), column(k)] = lax.dot_general(
                s.normed[rows_at(j * z.ext_block, z.ext_block, 16)],
                s.w[k + 1],
                NT,
                preferred_element_type=F32,
            )
            return carry

        w_here(k + 1)
        lax.fori_loop(0, 3, convolve, 0)
        if k == 0:
            w_pass(1, 3)
        if k == 1:
            w_pass(1, 0)

    w_here(0)

    def second_grad(j, carry):
        rows = rows_at(j * z.ext_block, z.ext_block, 16)
        s.grad_two[rows] = lax.dot_general(s.u[rows], s.w[0], NT, preferred_element_type=F32)
        return carry

    lax.fori_loop(0, 3, second_grad, 0)

    def before(start, size, columns):
        return s.taps[rows_at(start, size + 8), columns][PAD - DILATION : PAD - DILATION + size]

    def after(start, size, columns):
        low = (PAD + DILATION) // 8 * 8
        skip = PAD + DILATION - low
        return s.taps[rows_at(start + low, size + 8), columns][skip : skip + size]

    def second_act(j, carry):
        start, size = j * z.ext_step, z.ext_step
        rows = rows_at(start, size, 16)
        hidden = (
            s.taps[rows_at(PAD + start, size), column(1)]
            + wide(s.not_first[rows], z.f) * before(start, size, column(0))
            + wide(s.not_last[rows], z.f) * after(start, size, column(2))
        )
        half, square = gelu_half(hidden)
        act = hidden * half
        s.act_two[rows] = act
        s.slope_two[rows] = gelu_slope(hidden, half, square)
        mask = wide(s.live_own[rows], z.f)
        masked, grad = mask * act, mask * s.grad_two[rows]
        terms = (masked, masked * act, grad, grad * act)
        return tuple(total + fold(term) for total, term in zip(carry, terms))

    zero_two = jnp.zeros((8, z.f), F32)
    sums = lax.fori_loop(0, z.ext // z.ext_step, second_act, (zero_two,) * 4)
    sums = [jnp.sum(v, axis=0, keepdims=True) for v in sums]
    own_sum[1][0:1, : z.f] = sums[0]
    own_sum[1][0:1, z.f :] = sums[1]
    own_sum[1][1:2, : z.f] = sums[2]
    own_sum[1][1:2, z.f :] = sums[3]
    reduce_start(1)
    own_mean = sums[0] / own_count

    def centre(j, carry):
        s.centred[rows_at(j * z.own_step, z.own_step, 16)] = (s.act_two[own(j, z.own_step)] - own_mean).astype(BF16)
        return carry

    lax.fori_loop(0, steps, centre, 0)
    reduce_spread(1)
    own_all = rows_at(own0, z.bins, 16)
    s.point[...] = lax.dot_general(s.centred[...], s.u[own_all], TN, preferred_element_type=F32)
    two = reduce_finish(1)
    mean_two = two[0:1, : z.f] / count_two
    inv_two = lax.rsqrt(two[0:1, z.f :] / count_two - mean_two * mean_two + EPS)
    shift_two_grad = two[1:2, : z.f]
    gain_two_grad = inv_two * (two[1:2, z.f :] - mean_two * shift_two_grad)
    scale_two = whole_gain * inv_two
    offset_two = whole_shift - mean_two * scale_two
    back_b = scale_two * inv_two * gain_two_grad / count_two
    back_a = scale_two * shift_two_grad / count_two - mean_two * back_b

    def second_back(j, carry):
        rows = rows_at(j * z.ext_step, z.ext_step, 16)
        grad = scale_two * s.grad_two[rows] - wide(s.live[rows], z.f) * (back_a + back_b * s.act_two[rows])
        s.taps[rows_at(PAD + j * z.ext_step, z.ext_step), column(2)] = grad * s.slope_two[rows]
        return carry

    def slot_rows(x_slot, c_slot):
        return rows_at((x_slot * 2 + c_slot) * z.share, z.share, 16)

    def launch(made):
        made.start()
        pending.append(made)

    def hold(p, value):
        for part in range(z.thirds):
            s.part[p, part] = value[:, part * z.third : (part + 1) * z.third].astype(BF16)
        for i in range(z.n_x):
            launch(core_copy(p, i))

    def core_copy(p, i):
        return remote(
            s.part.at[p, :, slot_rows(i, 1 - core)],
            from_core[p].at[i],
            s.core_send.at[p, i],
            s.core_recv.at[p, i],
            partner,
        )

    def x_copy(p, part, i):
        return remote(
            s.to_x.at[p, i - 1, part],
            s.from_x.at[p, i - 1, part],
            s.x_send.at[p, part, i],
            s.x_recv.at[p, part, i],
            (seq, slot_at(i, core)),
        )

    def x_stage(p):
        for i in range(z.n_x):
            core_copy(p, i).wait_recv()
        for part in range(z.thirds):
            for i in range(1, z.n_x):
                to = (x_at + i) % z.n_x
                value = s.part[p, part, slot_rows(to, core)].astype(F32) + from_core[p][to, part].astype(F32)
                s.to_x[p, i - 1, part] = value.astype(BF16)
                launch(x_copy(p, part, i))

    def y_copy(h, part):
        return remote(
            s.to_y.at[h, part, 1 - y_at],
            s.from_y.at[h, part],
            s.y_send.at[h, part],
            s.y_recv.at[h, part],
            y_peer,
        )

    def y_stage(h, part):
        for at, p in enumerate((2 * h, 2 * h + 1)):
            value = s.part[p, part, slot_rows(x_at, core)].astype(F32) + from_core[p][x_at, part].astype(F32)
            for i in range(1, z.n_x):
                x_copy(p, part, i).wait_recv()
                value = value + s.from_x[p, i - 1, part].astype(F32)
            rows = slice(at * z.share, (at + 1) * z.share)
            for side in range(2):
                piece = value[:, side * z.half : (side + 1) * z.half]
                s.held_y[h, part, side, rows] = piece
                s.to_y[h, part, side, rows] = piece.astype(BF16)
        launch(y_copy(h, part))

    def piece_rows(i):
        return rows_at(i * z.piece, z.piece, 16)

    def z_device(i):
        return ((z_hi * z.n_lo + i) * 2 + y_at, ch)

    def z_copy(h, part, i):
        to = (z_lo + i) % z.n_lo
        return remote(
            s.to_z.at[h, part, piece_rows(to)],
            s.from_z.at[h, part, i - 1],
            s.z_send.at[h, part, i],
            s.z_recv.at[h, part, i],
            z_device(to),
        )

    def z_stage(h, part):
        y_copy(h, part).wait_recv()
        value = s.held_y[h, part, y_at] + s.from_y[h, part].astype(F32)
        s.held_z[h, part] = value
        s.to_z[h, part] = value.astype(BF16)
        for i in range(1, z.n_lo):
            launch(z_copy(h, part, i))

    def hi_copy(h, part, i, at):
        return remote(
            s.hi.at[h, part, at],
            s.hi.at[h, part, at],
            s.hi_send.at[h, part, i],
            s.hi_recv.at[h, part, at],
            ((((z_hi + i) % z.n_hi) * z.n_lo + z_lo) * 2 + y_at, ch),
        )

    def back_copy(h, part, i, at):
        return remote(
            s.mine.at[h, part, at],
            s.mine.at[h, part, at],
            s.zback_send.at[h, part, i],
            s.zback_recv.at[h, part, at],
            z_device((z_lo + i) % z.n_lo),
        )

    def yback_copy(h, part, at):
        return remote(
            s.mine.at[h, part, at],
            s.other.at[h, part, at],
            s.yback_send.at[h, part, at],
            s.yback_recv.at[h, part, at],
            y_peer,
        )

    def z_back_stage(h, part):
        value = s.held_z[h, part, piece_rows(z_lo)]
        for i in range(1, z.n_lo):
            z_copy(h, part, i).wait_recv()
            value = value + s.from_z[h, part, i - 1].astype(F32)
        if z.n_hi > 1:
            s.hi[h, part, pl.ds(z_hi, 1)] = value.astype(BF16).reshape(1, z.piece, z.half)
            for i in range(1, z.n_hi):
                launch(hi_copy(h, part, i, z_hi))
            for i in range(1, z.n_hi):
                hi_copy(h, part, i, (z_hi + i) % z.n_hi).wait_recv()
            value = s.hi[h, part, 0].astype(F32)
            for i in range(1, z.n_hi):
                value = value + s.hi[h, part, i].astype(F32)
        s.mine[h, part, pl.ds(z_lo, 1)] = value.astype(BF16).reshape(1, z.piece, z.half)
        for i in range(1, z.n_lo):
            launch(back_copy(h, part, i, z_lo))
        launch(yback_copy(h, part, z_lo))

    def y_back_stage(h, part):
        for i in range(1, z.n_lo):
            at = (z_lo + i) % z.n_lo
            back_copy(h, part, i, at).wait_recv()
            launch(yback_copy(h, part, at))

    def last_stage(h, part):
        for i in range(z.n_lo):
            yback_copy(h, part, i).wait_recv()
        for side, held in ((y_at, s.mine), (1 - y_at, s.other)):
            value = held[h, part].reshape(2, z.share, z.half).astype(F32)
            lanes = rows_at(part * z.third + side * z.half, z.half, LANES)
            w_grad[2 * h : 2 * h + 2, :, lanes] = value

    def each(stage, h):
        for part in range(z.thirds):
            stage(h, part)

    def down(row):
        return wide(jnp.transpose(jnp.broadcast_to(row, (LANES, z.f))), z.c)

    hold(0, down(scale_two) * s.point[...] + down(scale_two * (own_mean - mean_two) + whole_shift) * u_sum)
    blocks = z.ext // z.ext_step
    lax.fori_loop(0, blocks // 2, second_back, 0)
    x_stage(0)
    lax.fori_loop(blocks // 2, blocks, second_back, 0)

    def shift_rows(j, carry):
        start, size = own0 + j * z.own_step, z.own_step
        rows = rows_at(start, size, 16)
        to = rows_at(j * size, size, 16)
        later = wide(s.not_last[rows], z.f) * after(start, size, column(2))
        earlier = wide(s.not_first[rows], z.f) * before(start, size, column(2))
        s.shifted[to, column(0)] = later.astype(BF16)
        s.shifted[to, column(1)] = s.taps[rows_at(PAD + start, size), column(2)].astype(BF16)
        s.shifted[to, column(2)] = earlier.astype(BF16)
        return carry

    lax.fori_loop(0, z.bins // z.own_step, shift_rows, 0)
    for k in range(3):
        hold(
            k + 1,
            lax.dot_general(s.shifted[:, column(k)], s.normed[own_all], TN, preferred_element_type=F32),
        )
        if k > 0:
            x_stage(k)

    def first_grad(j, carry):
        rows = rows_at(j * z.own_block, z.own_block, 16)
        s.taps[rows_at(PAD + j * z.own_block, z.own_block), : z.c] = jnp.dot(
            s.shifted[rows], s.w[1:4].reshape(3 * z.f, z.c), preferred_element_type=F32
        )
        return carry

    lax.fori_loop(0, 1, first_grad, 0)
    x_stage(3)
    lax.fori_loop(1, 3, first_grad, 0)
    offset_back = -mean_one * inv_one

    def held(j):
        return rows_at(PAD + j * z.own_step, z.own_step)

    def first_sums(j, carry):
        grad = s.taps[held(j), : z.c]
        centred = s.act[own(j, z.own_step)] * inv_one + offset_back
        return carry[0] + fold(grad), carry[1] + fold(grad * centred)

    sums = lax.fori_loop(0, z.bins // z.own_step, first_sums, (zero, zero))
    own_sum[2][0:1] = jnp.sum(sums[0], axis=0, keepdims=True)
    own_sum[2][1:2] = jnp.sum(sums[1], axis=0, keepdims=True)
    reduce_start(2)
    each(y_stage, 0)
    reduce_spread(2)

    def block_out(j, carry):
        rows = own(j, z.own_block)
        normed = (s.act_two[rows] * scale_two + offset_two).astype(BF16)
        branch = jnp.dot(normed, s.w[0], preferred_element_type=F32)
        out[rows_at(j * z.own_block, z.own_block, 16)] = (s.x[rows].astype(F32) + branch).astype(BF16)
        return carry

    lax.fori_loop(0, 3, block_out, 0)
    each(z_stage, 0)
    each(y_stage, 1)
    each(z_back_stage, 0)

    three = reduce_finish(2)
    shift_one_grad, gain_one_grad = three[0:1], three[1:2]
    stats[0:1] = gain_one_grad
    stats[1:2] = shift_one_grad
    picked = jnp.concatenate([gain_two_grad, shift_two_grad, jnp.zeros((6, z.f), F32)], axis=0)
    stats[2:4, : z.share] = lax.dot_general(
        picked, chosen.astype(F32), NT, precision=lax.Precision.HIGHEST, preferred_element_type=F32
    )[0:2]
    first_b = scale_one * inv_one * gain_one_grad / count
    first_a = scale_one * shift_one_grad / count - mean_one * first_b

    def input_grad(j, carry):
        rows, at = own(j, z.own_step), rows_at(j * z.own_step, z.own_step, 16)
        grad = scale_one * s.taps[held(j), : z.c] - wide(s.live[rows], z.c) * (first_a + first_b * s.act[rows])
        out_grad[at] = (s.u[rows].astype(F32) + grad * s.slope[at].astype(F32)).astype(BF16)
        return carry

    lax.fori_loop(0, steps, input_grad, 0)
    each(z_stage, 1)
    each(y_back_stage, 0)
    each(z_back_stage, 1)
    each(last_stage, 0)
    each(y_back_stage, 1)
    each(last_stage, 1)

    for made in pending:
        made.wait_send()


def write_out(out, out_grad, stats, w_grad, *refs):
    outs, sem = refs[:8], refs[8]
    copies = [
        pltpu.make_async_copy(src, dst, sem.at[i])
        for i, (src, dst) in enumerate(
            ((out, outs[0]), (out_grad, outs[1]), (w_grad.at[1:4], outs[4]), (w_grad.at[0], outs[7]))
        )
    ]
    for made in copies:
        made.start()
    channels, share = outs[2].shape[0], outs[5].shape[0]
    outs[2][...] = stats[0:1].reshape(channels)
    outs[3][...] = stats[1:2].reshape(channels)
    outs[5][...] = stats[2:3, :share].reshape(share)
    outs[6][...] = stats[3:4, :share].reshape(share)
    for made in copies:
        made.wait()


def local(z, block_in, cotangent, lengths, gain_one, shift_one, dilated_w, gain_two, shift_two, point_w):
    names = scratch_of(z)
    hbm = pl.BlockSpec(memory_space=pl.ANY)
    vmem = pl.BlockSpec(memory_space=pltpu.VMEM)
    smem = pl.BlockSpec(memory_space=pltpu.SMEM)
    shape = jax.ShapeDtypeStruct
    big = shape((z.bins, z.c), BF16)
    results = pl.pallas_call(
        functools.partial(kernel, z, tuple(names)),
        out_shape=(big, big, shape((8, z.c), F32), shape((4, z.share, z.c), F32)),
        in_specs=[hbm, hbm, smem, vmem, vmem, hbm, vmem, vmem, hbm],
        out_specs=(vmem,) * 4,
        scratch_shapes=list(names.values()),
        compiler_params=pltpu.CompilerParams(
            collective_id=0, has_side_effects=True, vmem_limit_bytes=VMEM_LIMIT
        ),
    )(
        block_in,
        cotangent,
        lengths,
        gain_one,
        shift_one,
        jnp.transpose(dilated_w, (1, 0, 2)),
        gain_two,
        shift_two,
        point_w,
    )
    row, piece = shape((z.c,), F32), shape((z.share,), F32)
    outs = pl.pallas_call(
        write_out,
        out_shape=(big, big, row, row, shape((3, z.share, z.c), F32), piece, piece, shape((z.share, z.c), F32)),
        in_specs=[vmem] * 4,
        out_specs=(hbm, hbm, vmem, vmem, hbm, vmem, vmem, hbm),
        scratch_shapes=[pltpu.SemaphoreType.DMA((4,))],
        compiler_params=pltpu.CompilerParams(vmem_limit_bytes=2 * 2**20),
    )(*results)
    return (*outs[:4], jnp.transpose(outs[4], (1, 0, 2)), *outs[5:])


def solution(mesh):
    n_seq, n_ch = mesh.shape["seq"], mesh.shape["ch"]

    def run(block_in, cotangent, lengths, gain_one, shift_one, dilated_w, gain_two, shift_two, point_w):
        z = plan(
            n_seq, n_ch, block_in.shape[0], block_in.shape[1], dilated_w.shape[0] * n_ch, lengths.shape[0]
        )
        return local(
            z, block_in, cotangent, lengths, gain_one, shift_one, dilated_w, gain_two, shift_two, point_w
        )

    return jax.shard_map(
        run,
        mesh=mesh,
        in_specs=(
            P(("seq", "ch"), None),
            P(("seq", "ch"), None),
            P(),
            P(),
            P(),
            P("ch", None, None),
            P("ch"),
            P("ch"),
            P("ch", None),
        ),
        out_specs=(
            P(("seq", "ch"), None),
            P(("seq", "ch"), None),
            P(),
            P(),
            P("ch", None, None),
            P("ch"),
            P("ch"),
            P("ch", None),
        ),
        check_vma=False,
    )
```

```python
import functools
import types

import jax
import jax.numpy as jnp
from jax import lax
from jax.experimental import pallas as pl
from jax.experimental.pallas import tpu as pltpu
from jax.sharding import PartitionSpec as P

DILATION = 17
EPS = 0.001
HALO = 48
PAD = 24
LANES = 128
VMEM_LIMIT = 54 * 2**20
SPLIT = 4
MESH = pl.DeviceIdType.MESH
F32 = jnp.float32
BF16 = jnp.bfloat16
NT = (((1,), (1,)), ((), ()))
TN = (((0,), (0,)), ((), ()))
GELU_A = 0.7978845608028654
GELU_B = GELU_A * 0.044715


def gelu_half(v):
    square = v * v
    half = 0.5 + 0.5 * jnp.tanh(v * (GELU_A + GELU_B * square))
    return half, square


def gelu_slope(v, half, square):
    return half + (2.0 * v) * (half * (1.0 - half)) * (GELU_A + 3.0 * GELU_B * square)


def wide(mask, width):
    return jnp.concatenate([mask] * (width // LANES), axis=1)


def fold(value):
    rows, width = value.shape
    return jnp.sum(value.reshape(rows // 8, 8, width), axis=0)


def rows_at(start, size, step=8):
    return pl.ds(pl.multiple_of(start, step), size)


def plan(n_seq, n_ch, bins, channels, mid, n_windows):
    z = types.SimpleNamespace()
    z.n_seq, z.n_ch = n_seq, n_ch
    z.bins, z.c, z.f, z.n_windows = bins, channels, mid, n_windows
    z.share = mid // n_ch
    z.n_x = n_ch // 2
    z.n_chips = n_seq * z.n_x
    z.window = bins * n_ch * n_seq // n_windows
    z.pair_windows = 2 * bins // z.window
    z.n_lo = SPLIT
    z.n_hi = n_seq // (2 * SPLIT)
    z.ext = bins + HALO
    assert n_ch % 2 == 0 and n_seq % (2 * SPLIT) == 0
    assert 2 * bins % z.window == 0 and HALO >= 2 * DILATION
    z.ext_step = z.ext // 9
    z.ext_block = z.ext // 3
    z.own_step = bins // 8
    z.own_block = bins // 3
    assert z.ext_step % 16 == 0 and z.own_step % 16 == 0
    z.thirds = 3
    z.third = channels // z.thirds
    z.half = z.third // 2
    z.piece = 2 * z.share // SPLIT
    z.near = z.share // 2
    return z


def scratch_of(z):
    dma = pltpu.SemaphoreType.DMA
    vmem = pltpu.VMEM
    return dict(
        x=vmem((z.ext, z.c), BF16),
        u=vmem((z.ext, z.c), BF16),
        x_edge=vmem((HALO, z.c), BF16),
        u_edge=vmem((HALO, z.c), BF16),
        act=vmem((z.ext, z.c), F32),
        slope=vmem((z.bins, z.c), BF16),
        normed=vmem((z.ext, z.c), BF16),
        w=vmem((4, z.f, z.c), BF16),
        taps=vmem((z.ext + 2 * PAD, 3 * z.f), F32),
        grad_two=vmem((z.ext, z.f), F32),
        act_two=vmem((z.ext, z.f), F32),
        slope_two=vmem((z.ext, z.f), F32),
        shifted=vmem((z.bins, 3 * z.f), BF16),
        live=vmem((z.ext, LANES), F32),
        live_own=vmem((z.ext, LANES), F32),
        not_first=vmem((z.ext, LANES), F32),
        not_last=vmem((z.ext, LANES), F32),
        gains=vmem((z.n_ch, 8, z.f), F32),
        **{f"own_sum_{i}": vmem((2, z.c), F32) for i in range(3)},
        **{f"pair_sum_{i}": vmem((2, z.c), F32) for i in range(3)},
        **{f"chip_sum_{i}": vmem((z.n_chips, 2, z.c), F32) for i in range(3)},
        centred=vmem((z.bins, z.f), BF16),
        point=vmem((z.f, z.c), F32),
        part=vmem((4, z.thirds, z.f, z.third), BF16),
        **{f"from_core_{p}": vmem((z.n_x, z.thirds, z.share, z.third), BF16) for p in range(4)},
        to_x=vmem((4, z.n_x - 1, z.thirds, z.share, z.third), BF16),
        from_x=vmem((4, z.n_x - 1, z.thirds, z.share, z.third), BF16),
        held_y=vmem((2, z.thirds, 2, 2 * z.share, z.half), F32),
        to_y=vmem((2, z.thirds, 2, 2 * z.share, z.half), BF16),
        from_y=vmem((2, z.thirds, 2 * z.share, z.half), BF16),
        held_z=vmem((2, z.thirds, 2 * z.share, z.half), F32),
        to_z=vmem((2, z.thirds, 2 * z.share, z.half), BF16),
        from_z=vmem((2, z.thirds, z.n_lo - 1, z.piece, z.half), BF16),
        hi=vmem((2, z.thirds, z.n_hi, z.piece, z.half), BF16),
        mine=vmem((2, z.thirds, z.n_lo, z.piece, z.half), BF16),
        other=vmem((2, z.thirds, z.n_lo, z.piece, z.half), BF16),
        local_sem=dma((6,)),
        halo_send=dma((2,)),
        halo_recv=dma((2,)),
        gain_send=dma((z.n_ch,)),
        gain_recv=dma((z.n_ch,)),
        w_send=dma((4, z.n_x, 4)),
        w_recv=dma((4, z.n_x, 4)),
        pair_send=dma((3,)),
        pair_recv=dma((3,)),
        chip_send=dma((3, z.n_chips)),
        chip_recv=dma((3, z.n_chips)),
        core_send=dma((4, z.n_x)),
        core_recv=dma((4, z.n_x)),
        x_send=dma((4, z.thirds, z.n_x)),
        x_recv=dma((4, z.thirds, z.n_x)),
        y_send=dma((2, z.thirds)),
        y_recv=dma((2, z.thirds)),
        z_send=dma((2, z.thirds, z.n_lo)),
        z_recv=dma((2, z.thirds, z.n_lo)),
        hi_send=dma((2, z.thirds, z.n_hi)),
        hi_recv=dma((2, z.thirds, z.n_hi)),
        zback_send=dma((2, z.thirds, z.n_lo)),
        zback_recv=dma((2, z.thirds, z.n_lo)),
        yback_send=dma((2, z.thirds, z.n_lo)),
        yback_recv=dma((2, z.thirds, z.n_lo)),
    )


def kernel(
    z,
    names,
    x_hbm,
    cot_hbm,
    lengths,
    gain_one,
    shift_one,
    taps_hbm,
    gain_two,
    shift_two,
    point_hbm,
    out,
    out_grad,
    stats,
    w_grad,
    *scratch,
):
    s = types.SimpleNamespace(**dict(zip(names, scratch)))
    seq, ch = lax.axis_index("seq"), lax.axis_index("ch")
    x_at, core = ch // 2, ch % 2
    slow, y_at = seq // 2, seq % 2
    z_hi, z_lo = slow // z.n_lo, slow % z.n_lo
    chip = seq * z.n_x + x_at
    partner = (seq, x_at * 2 + 1 - core)
    y_peer = (slow * 2 + 1 - y_at, ch)
    own0 = core * HALO
    pending = []
    own_sum = (s.own_sum_0, s.own_sum_1, s.own_sum_2)
    pair_sum = (s.pair_sum_0, s.pair_sum_1, s.pair_sum_2)
    chip_sum = (s.chip_sum_0, s.chip_sum_1, s.chip_sum_2)
    from_core = (s.from_core_0, s.from_core_1, s.from_core_2, s.from_core_3)

    def remote(src, dst, send_sem, recv_sem, device):
        return pltpu.make_async_remote_copy(
            src_ref=src,
            dst_ref=dst,
            send_sem=send_sem,
            recv_sem=recv_sem,
            device_id=device,
            device_id_type=MESH,
        )

    def send(*copy):
        made = remote(*copy)
        made.start()
        pending.append(made)

    def chip_device(q):
        return (q // z.n_x, (q % z.n_x) * 2 + core)

    def other_chip(j):
        return (chip + 1 + j) % z.n_chips

    def own(j, size):
        return rows_at(own0 + j * size, size, 16)

    def column(k):
        return slice(k * z.f, (k + 1) * z.f)

    load_x = pltpu.make_async_copy(x_hbm, s.x.at[rows_at(own0, z.bins, 16)], s.local_sem.at[0])
    load_x.start()
    load_u = pltpu.make_async_copy(cot_hbm, s.u.at[rows_at(own0, z.bins, 16)], s.local_sem.at[1])
    load_u.start()
    own_rows = rows_at(ch * z.share, z.share, 16)
    sources = [point_hbm, taps_hbm.at[0], taps_hbm.at[1], taps_hbm.at[2]]
    load_w = [
        pltpu.make_async_copy(src, s.w.at[p, own_rows], s.local_sem.at[2 + p]) for p, src in enumerate(sources)
    ]
    for made in load_w:
        made.start()

    barrier = pltpu.get_barrier_semaphore()

    def greet(j, carry):
        pl.semaphore_signal(barrier, inc=1, device_id=chip_device(other_chip(j)), device_id_type=MESH)
        return carry

    for i in range(z.n_x):
        across = (seq, ((x_at + i) % z.n_x) * 2 + 1 - core)
        pl.semaphore_signal(barrier, inc=1, device_id=across, device_id_type=MESH)
    lax.fori_loop(0, z.n_chips - 1, greet, 0)

    pair = (seq * z.n_ch + ch) // 2
    window_lengths = [lengths[pair * z.pair_windows + i] for i in range(z.pair_windows)]

    def make_masks(j, total):
        rows = rows_at(j * z.ext_step, z.ext_step, 16)
        at = lax.broadcasted_iota(jnp.int32, (z.ext_step, LANES), 0) + j * z.ext_step
        place = at + core * (z.bins - HALO)
        inside, limit = place, jnp.full(place.shape, window_lengths[0], jnp.int32)
        for i in range(1, z.pair_windows):
            past = place >= i * z.window
            inside = jnp.where(past, place - i * z.window, inside)
            limit = jnp.where(past, window_lengths[i], limit)
        live = (inside < limit).astype(F32)
        mine = ((at >= own0) & (at < own0 + z.bins)).astype(F32)
        s.live[rows] = live
        s.live_own[rows] = live * mine
        s.not_first[rows] = (inside >= DILATION).astype(F32)
        s.not_last[rows] = (inside < z.window - DILATION).astype(F32)
        return total + fold(live * mine)

    live_rows = lax.fori_loop(0, z.ext // z.ext_step, make_masks, jnp.zeros((8, LANES), F32))
    own_count = jnp.maximum(wide(jnp.sum(live_rows, axis=0, keepdims=True), z.f), 1.0)
    bin_total = lax.fori_loop(0, z.n_windows, lambda i, t: t + lengths[i], jnp.int32(0))
    count = jnp.full((1, z.c), bin_total, jnp.int32).astype(F32)
    count_two = count[:, : z.f]
    s.taps[0:PAD] = jnp.zeros((PAD, 3 * z.f), F32)
    s.taps[PAD + z.ext : 2 * PAD + z.ext] = jnp.zeros((PAD, 3 * z.f), F32)

    chosen = lax.broadcasted_iota(jnp.int32, (z.share, z.f), 1) == (
        lax.broadcasted_iota(jnp.int32, (z.share, z.f), 0) + ch * z.share
    )
    both = [v[...].astype(F32).reshape(1, z.share) for v in (gain_two, shift_two)]
    both = jnp.concatenate(both + [jnp.zeros((6, z.share), F32)], axis=0)
    placed = jnp.dot(both.astype(BF16), chosen.astype(BF16), preferred_element_type=F32)
    s.gains[pl.ds(ch, 1)] = placed.reshape(1, 8, z.f)

    load_x.wait()

    def first_act(j, carry):
        rows = own(j, z.own_step)
        v = s.x[rows].astype(F32)
        half, _ = gelu_half(v)
        act = v * half
        s.act[rows] = act
        masked = wide(s.live[rows], z.c) * act
        return carry[0] + fold(masked), carry[1] + fold(masked * act)

    zero = jnp.zeros((8, z.c), F32)
    steps = z.bins // z.own_step
    sums = lax.fori_loop(0, steps // 2, first_act, (zero, zero))

    pl.semaphore_wait(barrier, z.n_chips - 1 + z.n_x)

    order = (1, 2, 3, 0)
    near0 = y_at * z.near

    def slot_at(i, c_slot):
        return ((x_at + i) % z.n_x) * 2 + c_slot

    def half_rows(slot, y_half):
        return rows_at(slot * z.share + y_half * z.near, z.near, 16)

    def w_copy(kind, i, p, src, rows, to):
        return remote(src, s.w.at[p, rows], s.w_send.at[kind, i, p], s.w_recv.at[kind, i, p], to)

    for p in order:
        for i in range(1, z.n_x):
            send_w = w_copy(
                0,
                i,
                p,
                sources[p].at[rows_at(near0, z.near, 16)],
                half_rows(ch, y_at),
                (seq, slot_at(i, core)),
            )
            send_w.start()
            pending.append(send_w)
        send_w = w_copy(0, 0, p, sources[p], own_rows, partner)
        send_w.start()
        pending.append(send_w)

    def w_pass(kind, p):
        for i in range(1, z.n_x):
            rows = half_rows(slot_at(z.n_x - i, core), y_at if kind == 0 else 1 - y_at)
            here = s.w.at[p, rows]
            w_copy(kind, i, p, here, rows, partner).wait_recv()
            onward = [w_copy(2 + kind, i, p, here, rows, partner)]
            if kind == 0:
                onward.append(w_copy(1, i, p, here, rows, y_peer))
            for made in onward:
                made.start()
                pending.append(made)

    def w_here(p):
        load_w[p].wait()
        whole = rows_at(slot_at(0, 1 - core) * z.share, z.share, 16)
        w_copy(0, 0, p, sources[p], whole, partner).wait_recv()
        for i in range(1, z.n_x):
            for kind in range(2):
                rows = half_rows(slot_at(z.n_x - i, 1 - core), y_at if kind == 0 else 1 - y_at)
                w_copy(2 + kind, i, p, s.w.at[p, rows], rows, partner).wait_recv()

    away = (1 - core) * (z.bins - HALO)
    halo_copies = [
        remote(src.at[rows_at(away, HALO, 16)], dst, s.halo_send.at[i], s.halo_recv.at[i], partner)
        for i, (src, dst) in enumerate(((x_hbm, s.x_edge), (cot_hbm, s.u_edge)))
    ]
    for made in halo_copies:
        made.start()
        pending.append(made)
    for i in range(1, z.n_ch):
        send(
            s.gains.at[pl.ds(ch, 1)],
            s.gains.at[pl.ds(ch, 1)],
            s.gain_send.at[i],
            s.gain_recv.at[ch],
            (seq, (ch + i) % z.n_ch),
        )

    def reduce_start(i):
        send(own_sum[i], pair_sum[i], s.pair_send.at[i], s.pair_recv.at[i], partner)

    def chip_copy(i, slot, j):
        return remote(
            chip_sum[i].at[slot],
            chip_sum[i].at[slot],
            s.chip_send.at[i, j],
            s.chip_recv.at[i, slot],
            chip_device(other_chip(j)),
        )

    def reduce_spread(i):
        remote(own_sum[i], pair_sum[i], s.pair_send.at[i], s.pair_recv.at[i], partner).wait_recv()
        chip_sum[i][pl.ds(chip, 1)] = (own_sum[i][...] + pair_sum[i][...]).reshape(1, 2, z.c)

        for j in range(z.n_chips - 1):
            made = chip_copy(i, chip, j)
            made.start()
            pending.append(made)

    def reduce_finish(i):
        for j in range(z.n_chips - 1):
            chip_copy(i, other_chip(j), j).wait_recv()
        return jnp.sum(chip_sum[i][...], axis=0)

    sums = lax.fori_loop(steps // 2, steps, first_act, sums)
    own_sum[0][0:1] = jnp.sum(sums[0], axis=0, keepdims=True)
    own_sum[0][1:2] = jnp.sum(sums[1], axis=0, keepdims=True)
    reduce_start(0)

    load_u.wait()

    def first_slope(j, total):
        rows = own(j, z.own_step)
        v = s.x[rows].astype(F32)
        half, square = gelu_half(v)
        s.slope[rows_at(j * z.own_step, z.own_step, 16)] = gelu_slope(v, half, square).astype(BF16)
        masked = s.u[rows].astype(F32) * wide(s.live[rows], z.c)
        s.u[rows] = masked.astype(BF16)
        return total + fold(masked)

    def halo_rows():
        return rows_at((1 - core) * z.bins, HALO, 16)

    u_sum = lax.fori_loop(0, steps // 2, first_slope, zero)
    reduce_spread(0)
    w_pass(0, 1)
    u_sum = lax.fori_loop(steps // 2, steps, first_slope, u_sum)
    w_pass(0, 2)
    for made in halo_copies:
        made.wait_recv()
    edge = s.x_edge[...].astype(F32)
    s.act[halo_rows()] = edge * gelu_half(edge)[0]
    s.u[halo_rows()] = (s.u_edge[...].astype(F32) * wide(s.live[halo_rows()], z.c)).astype(BF16)
    w_pass(0, 3)
    w_pass(1, 1)
    u_sum = jnp.sum(u_sum, axis=0, keepdims=True)

    for i in range(1, z.n_ch):
        slot = (ch + i) % z.n_ch
        remote(
            s.gains.at[pl.ds(slot, 1)],
            s.gains.at[pl.ds(slot, 1)],
            s.gain_send.at[i],
            s.gain_recv.at[slot],
            (seq, slot),
        ).wait_recv()
    both = s.gains[0]
    for i in range(1, z.n_ch):
        both = both + s.gains[i]
    whole_gain, whole_shift = both[0:1], both[1:2]

    one = reduce_finish(0)
    mean_one = one[0:1] / count
    inv_one = lax.rsqrt(one[1:2] / count - mean_one * mean_one + EPS)
    scale_one = gain_one[...].astype(F32).reshape(1, z.c) * inv_one
    offset_one = shift_one[...].astype(F32).reshape(1, z.c) - mean_one * scale_one

    def first_norm(j, carry):
        rows = rows_at(j * z.ext_step, z.ext_step, 16)
        s.normed[rows] = (s.act[rows] * scale_one + offset_one).astype(BF16)
        return carry

    lax.fori_loop(0, z.ext // z.ext_step, first_norm, 0)

    w_pass(1, 2)
    w_pass(0, 0)
    for k in range(3):

        def convolve(j, carry):
            s.taps[rows_at(PAD + j * z.ext_block, z.ext_block), column(k)] = lax.dot_general(
                s.normed[rows_at(j * z.ext_block, z.ext_block, 16)],
                s.w[k + 1],
                NT,
                preferred_element_type=F32,
            )
            return carry

        w_here(k + 1)
        lax.fori_loop(0, 3, convolve, 0)
        if k == 0:
            w_pass(1, 3)
        if k == 1:
            w_pass(1, 0)

    w_here(0)

    def second_grad(j, carry):
        rows = rows_at(j * z.ext_block, z.ext_block, 16)
        s.grad_two[rows] = lax.dot_general(s.u[rows], s.w[0], NT, preferred_element_type=F32)
        return carry

    lax.fori_loop(0, 3, second_grad, 0)

    def before(start, size, columns):
        return s.taps[rows_at(start, size + 8), columns][PAD - DILATION : PAD - DILATION + size]

    def after(start, size, columns):
        low = (PAD + DILATION) // 8 * 8
        skip = PAD + DILATION - low
        return s.taps[rows_at(start + low, size + 8), columns][skip : skip + size]

    def second_act(j, carry):
        start, size = j * z.ext_step, z.ext_step
        rows = rows_at(start, size, 16)
        hidden = (
            s.taps[rows_at(PAD + start, size), column(1)]
            + wide(s.not_first[rows], z.f) * before(start, size, column(0))
            + wide(s.not_last[rows], z.f) * after(start, size, column(2))
        )
        half, square = gelu_half(hidden)
        act = hidden * half
        s.act_two[rows] = act
        s.slope_two[rows] = gelu_slope(hidden, half, square)
        mask = wide(s.live_own[rows], z.f)
        masked, grad = mask * act, mask * s.grad_two[rows]
        terms = (masked, masked * act, grad, grad * act)
        return tuple(total + fold(term) for total, term in zip(carry, terms))

    zero_two = jnp.zeros((8, z.f), F32)
    sums = lax.fori_loop(0, z.ext // z.ext_step, second_act, (zero_two,) * 4)
    sums = [jnp.sum(v, axis=0, keepdims=True) for v in sums]
    own_sum[1][0:1, : z.f] = sums[0]
    own_sum[1][0:1, z.f :] = sums[1]
    own_sum[1][1:2, : z.f] = sums[2]
    own_sum[1][1:2, z.f :] = sums[3]
    reduce_start(1)
    own_mean = sums[0] / own_count

    def centre(j, carry):
        s.centred[rows_at(j * z.own_step, z.own_step, 16)] = (s.act_two[own(j, z.own_step)] - own_mean).astype(BF16)
        return carry

    lax.fori_loop(0, steps, centre, 0)
    reduce_spread(1)
    own_all = rows_at(own0, z.bins, 16)
    s.point[...] = lax.dot_general(s.centred[...], s.u[own_all], TN, preferred_element_type=F32)
    two = reduce_finish(1)
    mean_two = two[0:1, : z.f] / count_two
    inv_two = lax.rsqrt(two[0:1, z.f :] / count_two - mean_two * mean_two + EPS)
    shift_two_grad = two[1:2, : z.f]
    gain_two_grad = inv_two * (two[1:2, z.f :] - mean_two * shift_two_grad)
    scale_two = whole_gain * inv_two
    offset_two = whole_shift - mean_two * scale_two
    back_b = scale_two * inv_two * gain_two_grad / count_two
    back_a = scale_two * shift_two_grad / count_two - mean_two * back_b

    def second_back(j, carry):
        rows = rows_at(j * z.ext_step, z.ext_step, 16)
        grad = scale_two * s.grad_two[rows] - wide(s.live[rows], z.f) * (back_a + back_b * s.act_two[rows])
        s.taps[rows_at(PAD + j * z.ext_step, z.ext_step), column(2)] = grad * s.slope_two[rows]
        return carry

    def slot_rows(x_slot, c_slot):
        return rows_at((x_slot * 2 + c_slot) * z.share, z.share, 16)

    def launch(made):
        made.start()
        pending.append(made)

    def hold(p, value):
        for part in range(z.thirds):
            s.part[p, part] = value[:, part * z.third : (part + 1) * z.third].astype(BF16)
        for i in range(z.n_x):
            launch(core_copy(p, i))

    def core_copy(p, i):
        return remote(
            s.part.at[p, :, slot_rows(i, 1 - core)],
            from_core[p].at[i],
            s.core_send.at[p, i],
            s.core_recv.at[p, i],
            partner,
        )

    def x_copy(p, part, i):
        return remote(
            s.to_x.at[p, i - 1, part],
            s.from_x.at[p, i - 1, part],
            s.x_send.at[p, part, i],
            s.x_recv.at[p, part, i],
            (seq, slot_at(i, core)),
        )

    def x_stage(p):
        for i in range(z.n_x):
            core_copy(p, i).wait_recv()
        for part in range(z.thirds):
            for i in range(1, z.n_x):
                to = (x_at + i) % z.n_x
                value = s.part[p, part, slot_rows(to, core)].astype(F32) + from_core[p][to, part].astype(F32)
                s.to_x[p, i - 1, part] = value.astype(BF16)
                launch(x_copy(p, part, i))

    def y_copy(h, part):
        return remote(
            s.to_y.at[h, part, 1 - y_at],
            s.from_y.at[h, part],
            s.y_send.at[h, part],
            s.y_recv.at[h, part],
            y_peer,
        )

    def y_stage(h, part):
        for at, p in enumerate((2 * h, 2 * h + 1)):
            value = s.part[p, part, slot_rows(x_at, core)].astype(F32) + from_core[p][x_at, part].astype(F32)
            for i in range(1, z.n_x):
                x_copy(p, part, i).wait_recv()
                value = value + s.from_x[p, i - 1, part].astype(F32)
            rows = slice(at * z.share, (at + 1) * z.share)
            for side in range(2):
                piece = value[:, side * z.half : (side + 1) * z.half]
                s.held_y[h, part, side, rows] = piece
                s.to_y[h, part, side, rows] = piece.astype(BF16)
        launch(y_copy(h, part))

    def piece_rows(i):
        return rows_at(i * z.piece, z.piece, 16)

    def z_device(i):
        return ((z_hi * z.n_lo + i) * 2 + y_at, ch)

    def z_copy(h, part, i):
        to = (z_lo + i) % z.n_lo
        return remote(
            s.to_z.at[h, part, piece_rows(to)],
            s.from_z.at[h, part, i - 1],
            s.z_send.at[h, part, i],
            s.z_recv.at[h, part, i],
            z_device(to),
        )

    def z_stage(h, part):
        y_copy(h, part).wait_recv()
        value = s.held_y[h, part, y_at] + s.from_y[h, part].astype(F32)
        s.held_z[h, part] = value
        s.to_z[h, part] = value.astype(BF16)
        for i in range(1, z.n_lo):
            launch(z_copy(h, part, i))

    def hi_copy(h, part, i, at):
        return remote(
            s.hi.at[h, part, at],
            s.hi.at[h, part, at],
            s.hi_send.at[h, part, i],
            s.hi_recv.at[h, part, at],
            ((((z_hi + i) % z.n_hi) * z.n_lo + z_lo) * 2 + y_at, ch),
        )

    def back_copy(h, part, i, at):
        return remote(
            s.mine.at[h, part, at],
            s.mine.at[h, part, at],
            s.zback_send.at[h, part, i],
            s.zback_recv.at[h, part, at],
            z_device((z_lo + i) % z.n_lo),
        )

    def yback_copy(h, part, at):
        return remote(
            s.mine.at[h, part, at],
            s.other.at[h, part, at],
            s.yback_send.at[h, part, at],
            s.yback_recv.at[h, part, at],
            y_peer,
        )

    def z_back_stage(h, part):
        value = s.held_z[h, part, piece_rows(z_lo)]
        for i in range(1, z.n_lo):
            z_copy(h, part, i).wait_recv()
            value = value + s.from_z[h, part, i - 1].astype(F32)
        if z.n_hi > 1:
            s.hi[h, part, pl.ds(z_hi, 1)] = value.astype(BF16).reshape(1, z.piece, z.half)
            for i in range(1, z.n_hi):
                launch(hi_copy(h, part, i, z_hi))
            for i in range(1, z.n_hi):
                hi_copy(h, part, i, (z_hi + i) % z.n_hi).wait_recv()
            value = s.hi[h, part, 0].astype(F32)
            for i in range(1, z.n_hi):
                value = value + s.hi[h, part, i].astype(F32)
        s.mine[h, part, pl.ds(z_lo, 1)] = value.astype(BF16).reshape(1, z.piece, z.half)
        for i in range(1, z.n_lo):
            launch(back_copy(h, part, i, z_lo))
        launch(yback_copy(h, part, z_lo))

    def y_back_stage(h, part):
        for i in range(1, z.n_lo):
            at = (z_lo + i) % z.n_lo
            back_copy(h, part, i, at).wait_recv()
            launch(yback_copy(h, part, at))

    def last_stage(h, part):
        for i in range(z.n_lo):
            yback_copy(h, part, i).wait_recv()
        for side, held in ((y_at, s.mine), (1 - y_at, s.other)):
            value = held[h, part].reshape(2, z.share, z.half).astype(F32)
            lanes = rows_at(part * z.third + side * z.half, z.half, LANES)
            w_grad[2 * h : 2 * h + 2, :, lanes] = value

    def each(stage, h):
        for part in range(z.thirds):
            stage(h, part)

    def down(row):
        return wide(jnp.transpose(jnp.broadcast_to(row, (LANES, z.f))), z.c)

    hold(0, down(scale_two) * s.point[...] + down(scale_two * (own_mean - mean_two) + whole_shift) * u_sum)
    blocks = z.ext // z.ext_step
    lax.fori_loop(0, blocks // 2, second_back, 0)
    x_stage(0)
    lax.fori_loop(blocks // 2, blocks, second_back, 0)

    def shift_rows(j, carry):
        start, size = own0 + j * z.own_step, z.own_step
        rows = rows_at(start, size, 16)
        to = rows_at(j * size, size, 16)
        later = wide(s.not_last[rows], z.f) * after(start, size, column(2))
        earlier = wide(s.not_first[rows], z.f) * before(start, size, column(2))
        s.shifted[to, column(0)] = later.astype(BF16)
        s.shifted[to, column(1)] = s.taps[rows_at(PAD + start, size), column(2)].astype(BF16)
        s.shifted[to, column(2)] = earlier.astype(BF16)
        return carry

    lax.fori_loop(0, z.bins // z.own_step, shift_rows, 0)
    for k in range(3):
        hold(
            k + 1,
            lax.dot_general(s.shifted[:, column(k)], s.normed[own_all], TN, preferred_element_type=F32),
        )
        if k > 0:
            x_stage(k)

    def first_grad(j, carry):
        rows = rows_at(j * z.own_block, z.own_block, 16)
        s.taps[rows_at(PAD + j * z.own_block, z.own_block), : z.c] = jnp.dot(
            s.shifted[rows], s.w[1:4].reshape(3 * z.f, z.c), preferred_element_type=F32
        )
        return carry

    lax.fori_loop(0, 1, first_grad, 0)
    x_stage(3)
    lax.fori_loop(1, 3, first_grad, 0)
    offset_back = -mean_one * inv_one

    def held(j):
        return rows_at(PAD + j * z.own_step, z.own_step)

    def first_sums(j, carry):
        grad = s.taps[held(j), : z.c]
        centred = s.act[own(j, z.own_step)] * inv_one + offset_back
        return carry[0] + fold(grad), carry[1] + fold(grad * centred)

    sums = lax.fori_loop(0, z.bins // z.own_step, first_sums, (zero, zero))
    own_sum[2][0:1] = jnp.sum(sums[0], axis=0, keepdims=True)
    own_sum[2][1:2] = jnp.sum(sums[1], axis=0, keepdims=True)
    reduce_start(2)
    each(y_stage, 0)
    reduce_spread(2)

    def block_out(j, carry):
        rows = own(j, z.own_block)
        normed = (s.act_two[rows] * scale_two + offset_two).astype(BF16)
        branch = jnp.dot(normed, s.w[0], preferred_element_type=F32)
        out[rows_at(j * z.own_block, z.own_block, 16)] = (s.x[rows].astype(F32) + branch).astype(BF16)
        return carry

    lax.fori_loop(0, 3, block_out, 0)
    each(z_stage, 0)
    each(y_stage, 1)
    each(z_back_stage, 0)

    three = reduce_finish(2)
    shift_one_grad, gain_one_grad = three[0:1], three[1:2]
    stats[0:1] = gain_one_grad
    stats[1:2] = shift_one_grad
    picked = jnp.concatenate([gain_two_grad, shift_two_grad, jnp.zeros((6, z.f), F32)], axis=0)
    stats[2:4, : z.share] = lax.dot_general(
        picked, chosen.astype(F32), NT, precision=lax.Precision.HIGHEST, preferred_element_type=F32
    )[0:2]
    first_b = scale_one * inv_one * gain_one_grad / count
    first_a = scale_one * shift_one_grad / count - mean_one * first_b

    def input_grad(j, carry):
        rows, at = own(j, z.own_step), rows_at(j * z.own_step, z.own_step, 16)
        grad = scale_one * s.taps[held(j), : z.c] - wide(s.live[rows], z.c) * (first_a + first_b * s.act[rows])
        out_grad[at] = (s.u[rows].astype(F32) + grad * s.slope[at].astype(F32)).astype(BF16)
        return carry

    lax.fori_loop(0, steps, input_grad, 0)
    each(z_stage, 1)
    each(y_back_stage, 0)
    each(z_back_stage, 1)
    each(last_stage, 0)
    each(y_back_stage, 1)
    each(last_stage, 1)

    for made in pending:
        made.wait_send()


def write_out(out, out_grad, stats, w_grad, *refs):
    outs, sem = refs[:8], refs[8]
    copies = [
        pltpu.make_async_copy(src, dst, sem.at[i])
        for i, (src, dst) in enumerate(
            ((out, outs[0]), (out_grad, outs[1]), (w_grad.at[1:4], outs[4]), (w_grad.at[0], outs[7]))
        )
    ]
    for made in copies:
        made.start()
    channels, share = outs[2].shape[0], outs[5].shape[0]
    outs[2][...] = stats[0:1].reshape(channels)
    outs[3][...] = stats[1:2].reshape(channels)
    outs[5][...] = stats[2:3, :share].reshape(share)
    outs[6][...] = stats[3:4, :share].reshape(share)
    for made in copies:
        made.wait()


def local(z, block_in, cotangent, lengths, gain_one, shift_one, dilated_w, gain_two, shift_two, point_w):
    names = scratch_of(z)
    hbm = pl.BlockSpec(memory_space=pl.ANY)
    vmem = pl.BlockSpec(memory_space=pltpu.VMEM)
    smem = pl.BlockSpec(memory_space=pltpu.SMEM)
    shape = jax.ShapeDtypeStruct
    big = shape((z.bins, z.c), BF16)
    held = pltpu.VMEM((z.bins, z.c), BF16)
    results = pl.pallas_call(
        functools.partial(kernel, z, tuple(names)),
        out_shape=(held, held, pltpu.VMEM((8, z.c), F32), pltpu.VMEM((4, z.share, z.c), F32)),
        in_specs=[hbm, hbm, smem, vmem, vmem, hbm, vmem, vmem, hbm],
        out_specs=(vmem,) * 4,
        scratch_shapes=list(names.values()),
        compiler_params=pltpu.CompilerParams(
            collective_id=0, has_side_effects=True, vmem_limit_bytes=VMEM_LIMIT
        ),
    )(
        block_in,
        cotangent,
        lengths,
        gain_one,
        shift_one,
        jnp.transpose(dilated_w, (1, 0, 2)),
        gain_two,
        shift_two,
        point_w,
    )
    row, piece = shape((z.c,), F32), shape((z.share,), F32)
    outs = pl.pallas_call(
        write_out,
        out_shape=(big, big, row, row, shape((3, z.share, z.c), F32), piece, piece, shape((z.share, z.c), F32)),
        in_specs=[vmem] * 4,
        out_specs=(hbm, hbm, vmem, vmem, hbm, vmem, vmem, hbm),
        scratch_shapes=[pltpu.SemaphoreType.DMA((4,))],
        compiler_params=pltpu.CompilerParams(vmem_limit_bytes=2 * 2**20),
    )(*results)
    return (*outs[:4], jnp.transpose(outs[4], (1, 0, 2)), *outs[5:])


def solution(mesh):
    n_seq, n_ch = mesh.shape["seq"], mesh.shape["ch"]

    def run(block_in, cotangent, lengths, gain_one, shift_one, dilated_w, gain_two, shift_two, point_w):
        z = plan(
            n_seq, n_ch, block_in.shape[0], block_in.shape[1], dilated_w.shape[0] * n_ch, lengths.shape[0]
        )
        return local(
            z, block_in, cotangent, lengths, gain_one, shift_one, dilated_w, gain_two, shift_two, point_w
        )

    return jax.shard_map(
        run,
        mesh=mesh,
        in_specs=(
            P(("seq", "ch"), None),
            P(("seq", "ch"), None),
            P(),
            P(),
            P(),
            P("ch", None, None),
            P("ch"),
            P("ch"),
            P("ch", None),
        ),
        out_specs=(
            P(("seq", "ch"), None),
            P(("seq", "ch"), None),
            P(),
            P(),
            P("ch", None, None),
            P("ch"),
            P("ch"),
            P("ch", None),
        ),
        check_vma=False,
    )
```

```python
import functools
import types

import jax
import jax.numpy as jnp
from jax import lax
from jax.experimental import pallas as pl
from jax.experimental.pallas import tpu as pltpu
from jax.sharding import PartitionSpec as P

DILATION = 17
EPS = 0.001
HALO = 48
PAD = 24
LANES = 128
LINE = 4
VMEM_LIMIT = 57 * 2**20
MESH = pl.DeviceIdType.MESH
F32 = jnp.float32
BF16 = jnp.bfloat16
NT = (((1,), (1,)), ((), ()))
TN = (((0,), (0,)), ((), ()))
GELU_A = 0.7978845608028654
GELU_B = GELU_A * 0.044715


def gelu_half(v):
    square = v * v
    half = 0.5 + 0.5 * jnp.tanh(v * (GELU_A + GELU_B * square))
    return half, square


def gelu_slope(v, half, square):
    return half + (2.0 * v) * (half * (1.0 - half)) * (GELU_A + 3.0 * GELU_B * square)


def wide(mask, width):
    return jnp.concatenate([mask] * (width // LANES), axis=1)


def fold(value):
    rows, width = value.shape
    return jnp.sum(value.reshape(rows // 8, 8, width), axis=0)


def rows_at(start, size, step=8):
    return pl.ds(pl.multiple_of(start, step), size)


def plan(n_seq, n_ch, bins, channels, mid, n_windows):
    z = types.SimpleNamespace()
    z.n_seq, z.n_ch = n_seq, n_ch
    z.bins, z.c, z.f, z.n_windows = bins, channels, mid, n_windows
    z.share = mid // n_ch
    z.n_x = n_ch // 2
    z.n_chips = n_seq * z.n_x
    z.window = bins * n_ch * n_seq // n_windows
    z.pair_windows = 2 * bins // z.window
    z.lines = n_seq // (2 * LINE)
    z.swaps = 1 + z.lines.bit_length()
    z.doublings = z.swaps
    z.ext = bins + HALO
    assert n_ch % 2 == 0 and n_seq == 2 * LINE << (z.swaps - 2)
    assert 2 * bins % z.window == 0 and HALO >= 2 * DILATION
    z.ext_step = z.ext // 9
    z.ext_block = z.ext // 3
    z.own_step = bins // 8
    z.own_block = bins // 3
    assert z.ext_step % 16 == 0 and z.own_step % 16 == 0
    z.thirds = 3
    z.third = channels // z.thirds
    z.half = z.third // 2
    z.near = z.share // 2
    return z


def scratch_of(z):
    dma = pltpu.SemaphoreType.DMA
    vmem = pltpu.VMEM
    return dict(
        x=vmem((z.ext, z.c), BF16),
        u=vmem((z.ext, z.c), BF16),
        x_edge=vmem((HALO, z.c), BF16),
        u_edge=vmem((HALO, z.c), BF16),
        act=vmem((z.ext, z.c), F32),
        slope=vmem((z.bins, z.c), BF16),
        normed=vmem((z.ext, z.c), BF16),
        w=vmem((4, z.f, z.c), BF16),
        taps=vmem((z.ext + 2 * PAD, 3 * z.f), F32),
        grad_two=vmem((z.ext, z.f), F32),
        act_two=vmem((z.ext, z.f), F32),
        slope_two=vmem((z.ext, z.f), F32),
        shifted=vmem((z.bins, 3 * z.f), BF16),
        live=vmem((z.ext, LANES), F32),
        live_own=vmem((z.ext, LANES), F32),
        not_first=vmem((z.ext, LANES), F32),
        not_last=vmem((z.ext, LANES), F32),
        gains=vmem((z.n_ch, 8, z.f), F32),
        **{f"own_sum_{i}": vmem((2, z.c), F32) for i in range(3)},
        **{f"pair_sum_{i}": vmem((2, z.c), F32) for i in range(3)},
        **{f"chip_sum_{i}": vmem((z.n_chips, 2, z.c), F32) for i in range(3)},
        centred=vmem((z.bins, z.f), BF16),
        point=vmem((z.f, z.c), F32),
        part=vmem((4, z.thirds, z.f, z.third), BF16),
        **{f"from_core_{p}": vmem((z.n_x, z.thirds, z.share, z.third), BF16) for p in range(4)},
        to_x=vmem((3, z.n_x - 1, z.thirds, z.share, z.third), BF16),
        from_x=vmem((3, z.n_x - 1, z.thirds, z.share, z.third), BF16),
        held=vmem((3, z.thirds, z.share, z.third), F32),
        to_inner=vmem((3, z.thirds, z.share, z.third), BF16),
        from_end=vmem((3, z.thirds, z.share, z.third), BF16),
        to_swap=vmem((z.swaps, 3, z.thirds, z.share, z.third), BF16),
        from_swap=vmem((z.swaps, 3, z.thirds, z.share, z.third), BF16),
        final=vmem((3, z.thirds, z.share, z.third), BF16),
        held_side=vmem((z.thirds, z.n_x, z.share, z.half), F32),
        to_side=vmem((z.thirds, z.n_x, z.share, z.half), BF16),
        from_side=vmem((z.thirds, z.n_x, z.share, z.half), BF16),
        held_far=vmem((z.thirds, z.share, z.half), F32),
        to_far=vmem((z.thirds, z.n_x, z.share, z.half), BF16),
        from_far=vmem((z.thirds, z.n_x, z.share, z.half), BF16),
        to_z=vmem((z.doublings, z.thirds, z.share, z.half), BF16),
        from_z=vmem((z.doublings, z.thirds, z.share, z.half), BF16),
        mine=vmem((z.thirds, z.share, z.half), BF16),
        other=vmem((z.thirds, z.share, z.half), BF16),
        local_sem=dma((6,)),
        halo_send=dma((2,)),
        halo_recv=dma((2,)),
        gain_send=dma((z.n_ch,)),
        gain_recv=dma((z.n_ch,)),
        w_send=dma((4, z.n_x, 4)),
        w_recv=dma((4, z.n_x, 4)),
        pair_send=dma((3,)),
        pair_recv=dma((3,)),
        chip_send=dma((3, z.n_chips)),
        chip_recv=dma((3, z.n_chips)),
        core_send=dma((4, z.n_x)),
        core_recv=dma((4, z.n_x)),
        x_send=dma((4, z.thirds, z.n_x)),
        x_recv=dma((4, z.thirds, z.n_x)),
        inner_send=dma((4, z.thirds)),
        inner_recv=dma((4, z.thirds)),
        swap_send=dma((z.swaps, 4, z.thirds)),
        swap_recv=dma((z.swaps, 4, z.thirds)),
        final_send=dma((4, z.thirds)),
        final_recv=dma((4, z.thirds)),
        side_send=dma((z.thirds,)),
        side_recv=dma((z.thirds,)),
        far_send=dma((z.thirds, z.n_x)),
        far_recv=dma((z.thirds, z.n_x)),
        z_send=dma((z.doublings, z.thirds)),
        z_recv=dma((z.doublings, z.thirds)),
        back_send=dma((z.thirds,)),
        back_recv=dma((z.thirds,)),
    )


def kernel(
    z,
    names,
    x_hbm,
    cot_hbm,
    lengths,
    gain_one,
    shift_one,
    taps_hbm,
    gain_two,
    shift_two,
    point_hbm,
    out,
    out_grad,
    stats,
    w_grad,
    *scratch,
):
    s = types.SimpleNamespace(**dict(zip(names, scratch)))
    seq, ch = lax.axis_index("seq"), lax.axis_index("ch")
    x_at, core = ch // 2, ch % 2
    slow, y_at = seq // 2, seq % 2
    chip = seq * z.n_x + x_at
    partner = (seq, x_at * 2 + 1 - core)
    y_peer = (slow * 2 + 1 - y_at, ch)
    own0 = core * HALO
    pending = []
    own_sum = (s.own_sum_0, s.own_sum_1, s.own_sum_2)
    pair_sum = (s.pair_sum_0, s.pair_sum_1, s.pair_sum_2)
    chip_sum = (s.chip_sum_0, s.chip_sum_1, s.chip_sum_2)
    from_core = (s.from_core_0, s.from_core_1, s.from_core_2, s.from_core_3)

    def remote(src, dst, send_sem, recv_sem, device):
        return pltpu.make_async_remote_copy(
            src_ref=src,
            dst_ref=dst,
            send_sem=send_sem,
            recv_sem=recv_sem,
            device_id=device,
            device_id_type=MESH,
        )

    def send(*copy):
        made = remote(*copy)
        made.start()
        pending.append(made)

    def chip_device(q):
        return (q // z.n_x, (q % z.n_x) * 2 + core)

    def other_chip(j):
        return (chip + 1 + j) % z.n_chips

    def own(j, size):
        return rows_at(own0 + j * size, size, 16)

    def column(k):
        return slice(k * z.f, (k + 1) * z.f)

    load_x = pltpu.make_async_copy(x_hbm, s.x.at[rows_at(own0, z.bins, 16)], s.local_sem.at[0])
    load_x.start()
    load_u = pltpu.make_async_copy(cot_hbm, s.u.at[rows_at(own0, z.bins, 16)], s.local_sem.at[1])
    load_u.start()
    own_rows = rows_at(ch * z.share, z.share, 16)
    sources = [point_hbm, taps_hbm.at[0], taps_hbm.at[1], taps_hbm.at[2]]
    load_w = [
        pltpu.make_async_copy(src, s.w.at[p, own_rows], s.local_sem.at[2 + p]) for p, src in enumerate(sources)
    ]
    for made in load_w:
        made.start()

    barrier = pltpu.get_barrier_semaphore()

    def greet(j, carry):
        pl.semaphore_signal(barrier, inc=1, device_id=chip_device(other_chip(j)), device_id_type=MESH)
        return carry

    for i in range(z.n_x):
        across = (seq, ((x_at + i) % z.n_x) * 2 + 1 - core)
        pl.semaphore_signal(barrier, inc=1, device_id=across, device_id_type=MESH)
    lax.fori_loop(0, z.n_chips - 1, greet, 0)

    pair = (seq * z.n_ch + ch) // 2
    window_lengths = [lengths[pair * z.pair_windows + i] for i in range(z.pair_windows)]

    def make_masks(j, total):
        rows = rows_at(j * z.ext_step, z.ext_step, 16)
        at = lax.broadcasted_iota(jnp.int32, (z.ext_step, LANES), 0) + j * z.ext_step
        place = at + core * (z.bins - HALO)
        inside, limit = place, jnp.full(place.shape, window_lengths[0], jnp.int32)
        for i in range(1, z.pair_windows):
            past = place >= i * z.window
            inside = jnp.where(past, place - i * z.window, inside)
            limit = jnp.where(past, window_lengths[i], limit)
        live = (inside < limit).astype(F32)
        mine = ((at >= own0) & (at < own0 + z.bins)).astype(F32)
        s.live[rows] = live
        s.live_own[rows] = live * mine
        s.not_first[rows] = (inside >= DILATION).astype(F32)
        s.not_last[rows] = (inside < z.window - DILATION).astype(F32)
        return total + fold(live * mine)

    live_rows = lax.fori_loop(0, z.ext // z.ext_step, make_masks, jnp.zeros((8, LANES), F32))
    own_count = jnp.maximum(wide(jnp.sum(live_rows, axis=0, keepdims=True), z.f), 1.0)
    bin_total = lax.fori_loop(0, z.n_windows, lambda i, t: t + lengths[i], jnp.int32(0))
    count = jnp.full((1, z.c), bin_total, jnp.int32).astype(F32)
    count_two = count[:, : z.f]
    s.taps[0:PAD] = jnp.zeros((PAD, 3 * z.f), F32)
    s.taps[PAD + z.ext : 2 * PAD + z.ext] = jnp.zeros((PAD, 3 * z.f), F32)

    chosen = lax.broadcasted_iota(jnp.int32, (z.share, z.f), 1) == (
        lax.broadcasted_iota(jnp.int32, (z.share, z.f), 0) + ch * z.share
    )
    both = [v[...].astype(F32).reshape(1, z.share) for v in (gain_two, shift_two)]
    both = jnp.concatenate(both + [jnp.zeros((6, z.share), F32)], axis=0)
    placed = jnp.dot(both.astype(BF16), chosen.astype(BF16), preferred_element_type=F32)
    s.gains[pl.ds(ch, 1)] = placed.reshape(1, 8, z.f)

    load_x.wait()

    def first_act(j, carry):
        rows = own(j, z.own_step)
        v = s.x[rows].astype(F32)
        half, _ = gelu_half(v)
        act = v * half
        s.act[rows] = act
        masked = wide(s.live[rows], z.c) * act
        return carry[0] + fold(masked), carry[1] + fold(masked * act)

    zero = jnp.zeros((8, z.c), F32)
    steps = z.bins // z.own_step
    sums = lax.fori_loop(0, steps // 2, first_act, (zero, zero))

    pl.semaphore_wait(barrier, z.n_chips - 1 + z.n_x)

    near0 = y_at * z.near

    def slot_at(i, c_slot):
        return ((x_at + i) % z.n_x) * 2 + c_slot

    def half_rows(slot, y_half):
        return rows_at(slot * z.share + y_half * z.near, z.near, 16)

    def x_rows(slot, p):
        return half_rows(slot, y_at) if p else rows_at(slot * z.share, z.share, 16)

    def w_copy(kind, i, p, src, rows, to):
        return remote(src, s.w.at[p, rows], s.w_send.at[kind, i, p], s.w_recv.at[kind, i, p], to)

    def w_along(p):
        for i in range(1, z.n_x):
            made = w_copy(
                0,
                i,
                p,
                sources[p].at[rows_at(near0, z.near, 16)] if p else sources[p],
                x_rows(ch, p),
                (seq, slot_at(i, core)),
            )
            made.start()
            pending.append(made)

    def w_across(p):
        made = w_copy(0, 0, p, sources[p], own_rows, partner)
        made.start()
        pending.append(made)

    w_along(1)
    w_along(2)

    def w_pass(kind, p):
        for i in range(1, z.n_x):
            slot = slot_at(z.n_x - i, core)
            rows = x_rows(slot, p) if kind == 0 else half_rows(slot, 1 - y_at)
            here = s.w.at[p, rows]
            w_copy(kind, i, p, here, rows, partner).wait_recv()
            onward = [w_copy(2 + kind, i, p, here, rows, partner)]
            if kind == 0 and p:
                onward.append(w_copy(1, i, p, here, rows, y_peer))
            for made in onward:
                made.start()
                pending.append(made)

    def w_here(p):
        load_w[p].wait()
        whole = rows_at(slot_at(0, 1 - core) * z.share, z.share, 16)
        w_copy(0, 0, p, sources[p], whole, partner).wait_recv()
        for i in range(1, z.n_x):
            slot = slot_at(z.n_x - i, 1 - core)
            for kind in range(2 if p else 1):
                rows = x_rows(slot, p) if kind == 0 else half_rows(slot, 1 - y_at)
                w_copy(2 + kind, i, p, s.w.at[p, rows], rows, partner).wait_recv()

    def reduce_start(i):
        send(own_sum[i], pair_sum[i], s.pair_send.at[i], s.pair_recv.at[i], partner)

    def chip_copy(i, slot, j):
        return remote(
            chip_sum[i].at[slot],
            chip_sum[i].at[slot],
            s.chip_send.at[i, j],
            s.chip_recv.at[i, slot],
            chip_device(other_chip(j)),
        )

    def reduce_spread(i):
        remote(own_sum[i], pair_sum[i], s.pair_send.at[i], s.pair_recv.at[i], partner).wait_recv()
        chip_sum[i][pl.ds(chip, 1)] = (own_sum[i][...] + pair_sum[i][...]).reshape(1, 2, z.c)

        for j in range(z.n_chips - 1):
            made = chip_copy(i, chip, j)
            made.start()
            pending.append(made)

    def reduce_finish(i):
        for j in range(z.n_chips - 1):
            chip_copy(i, other_chip(j), j).wait_recv()
        return jnp.sum(chip_sum[i][...], axis=0)

    sums = lax.fori_loop(steps // 2, steps, first_act, sums)
    own_sum[0][0:1] = jnp.sum(sums[0], axis=0, keepdims=True)
    own_sum[0][1:2] = jnp.sum(sums[1], axis=0, keepdims=True)
    reduce_start(0)

    load_u.wait()

    def first_slope(j, total):
        rows = own(j, z.own_step)
        v = s.x[rows].astype(F32)
        half, square = gelu_half(v)
        s.slope[rows_at(j * z.own_step, z.own_step, 16)] = gelu_slope(v, half, square).astype(BF16)
        masked = s.u[rows].astype(F32) * wide(s.live[rows], z.c)
        s.u[rows] = masked.astype(BF16)
        return total + fold(masked)

    def halo_rows():
        return rows_at((1 - core) * z.bins, HALO, 16)

    reduce_spread(0)
    w_along(3)
    w_along(0)
    w_across(1)
    w_across(2)

    away = (1 - core) * (z.bins - HALO)
    halo_copies = [
        remote(src.at[rows_at(away, HALO, 16)], dst, s.halo_send.at[i], s.halo_recv.at[i], partner)
        for i, (src, dst) in enumerate(((x_hbm, s.x_edge), (cot_hbm, s.u_edge)))
    ]
    for made in halo_copies:
        made.start()
        pending.append(made)
    w_across(3)
    w_across(0)
    for i in range(1, z.n_ch):
        send(
            s.gains.at[pl.ds(ch, 1)],
            s.gains.at[pl.ds(ch, 1)],
            s.gain_send.at[i],
            s.gain_recv.at[ch],
            (seq, (ch + i) % z.n_ch),
        )
    u_sum = lax.fori_loop(0, steps // 2, first_slope, zero)
    w_pass(0, 1)
    w_pass(0, 2)
    u_sum = lax.fori_loop(steps // 2, steps, first_slope, u_sum)
    for made in halo_copies:
        made.wait_recv()
    edge = s.x_edge[...].astype(F32)
    s.act[halo_rows()] = edge * gelu_half(edge)[0]
    s.u[halo_rows()] = (s.u_edge[...].astype(F32) * wide(s.live[halo_rows()], z.c)).astype(BF16)
    w_pass(0, 3)
    w_pass(1, 1)
    u_sum = jnp.sum(u_sum, axis=0, keepdims=True)

    for i in range(1, z.n_ch):
        slot = (ch + i) % z.n_ch
        remote(
            s.gains.at[pl.ds(slot, 1)],
            s.gains.at[pl.ds(slot, 1)],
            s.gain_send.at[i],
            s.gain_recv.at[slot],
            (seq, slot),
        ).wait_recv()
    both = s.gains[0]
    for i in range(1, z.n_ch):
        both = both + s.gains[i]
    whole_gain, whole_shift = both[0:1], both[1:2]

    one = reduce_finish(0)
    mean_one = one[0:1] / count
    inv_one = lax.rsqrt(one[1:2] / count - mean_one * mean_one + EPS)
    scale_one = gain_one[...].astype(F32).reshape(1, z.c) * inv_one
    offset_one = shift_one[...].astype(F32).reshape(1, z.c) - mean_one * scale_one

    def convolve(first, last):
        def step(j, carry):
            s.taps[rows_at(PAD + j * z.ext_block, z.ext_block), first * z.f : last * z.f] = lax.dot_general(
                s.normed[rows_at(j * z.ext_block, z.ext_block, 16)],
                s.w[first + 1 : last + 1].reshape((last - first) * z.f, z.c),
                NT,
                preferred_element_type=F32,
            )
            return carry

        lax.fori_loop(0, 3, step, 0)

    w_pass(1, 2)
    w_here(1)

    def first_norm(j, carry):
        rows = rows_at(j * z.ext_block, z.ext_block, 16)
        normed = (s.act[rows] * scale_one + offset_one).astype(BF16)
        s.normed[rows] = normed
        s.taps[rows_at(PAD + j * z.ext_block, z.ext_block), : z.f] = lax.dot_general(
            normed, s.w[1], NT, preferred_element_type=F32
        )
        return carry

    lax.fori_loop(0, 3, first_norm, 0)
    w_pass(0, 0)
    w_pass(1, 3)
    w_here(2)
    w_here(3)
    convolve(1, 3)
    w_here(0)

    def before(start, size, columns):
        return s.taps[rows_at(start, size + 8), columns][PAD - DILATION : PAD - DILATION + size]

    def after(start, size, columns):
        low = (PAD + DILATION) // 8 * 8
        skip = PAD + DILATION - low
        return s.taps[rows_at(start + low, size + 8), columns][skip : skip + size]

    def second_act(j, carry):
        start, size = j * z.ext_block, z.ext_block
        rows = rows_at(start, size, 16)
        grad = lax.dot_general(s.u[rows], s.w[0], NT, preferred_element_type=F32)
        s.grad_two[rows] = grad
        hidden = (
            s.taps[rows_at(PAD + start, size), column(1)]
            + wide(s.not_first[rows], z.f) * before(start, size, column(0))
            + wide(s.not_last[rows], z.f) * after(start, size, column(2))
        )
        half, square = gelu_half(hidden)
        act = hidden * half
        s.act_two[rows] = act
        s.slope_two[rows] = gelu_slope(hidden, half, square)
        mask = wide(s.live_own[rows], z.f)
        masked, grad = mask * act, mask * grad
        terms = (masked, masked * act, grad, grad * act)
        return tuple(total + fold(term) for total, term in zip(carry, terms))

    zero_two = jnp.zeros((8, z.f), F32)
    sums = lax.fori_loop(0, 3, second_act, (zero_two,) * 4)
    sums = [jnp.sum(v, axis=0, keepdims=True) for v in sums]
    own_sum[1][0:1, : z.f] = sums[0]
    own_sum[1][0:1, z.f :] = sums[1]
    own_sum[1][1:2, : z.f] = sums[2]
    own_sum[1][1:2, z.f :] = sums[3]
    reduce_start(1)
    own_mean = sums[0] / own_count

    def centre(j, carry):
        s.centred[rows_at(j * z.own_step, z.own_step, 16)] = (s.act_two[own(j, z.own_step)] - own_mean).astype(BF16)
        return carry

    lax.fori_loop(0, steps, centre, 0)
    reduce_spread(1)
    own_all = rows_at(own0, z.bins, 16)
    s.point[...] = lax.dot_general(s.centred[...], s.u[own_all], TN, preferred_element_type=F32)
    two = reduce_finish(1)
    mean_two = two[0:1, : z.f] / count_two
    inv_two = lax.rsqrt(two[0:1, z.f :] / count_two - mean_two * mean_two + EPS)
    shift_two_grad = two[1:2, : z.f]
    gain_two_grad = inv_two * (two[1:2, z.f :] - mean_two * shift_two_grad)
    scale_two = whole_gain * inv_two
    offset_two = whole_shift - mean_two * scale_two
    back_b = scale_two * inv_two * gain_two_grad / count_two
    back_a = scale_two * shift_two_grad / count_two - mean_two * back_b

    def second_back(j, carry):
        rows = rows_at(j * z.ext_step, z.ext_step, 16)
        grad = scale_two * s.grad_two[rows] - wide(s.live[rows], z.f) * (back_a + back_b * s.act_two[rows])
        s.taps[rows_at(PAD + j * z.ext_step, z.ext_step), column(2)] = grad * s.slope_two[rows]
        return carry

    def slot_rows(x_slot, c_slot):
        return rows_at((x_slot * 2 + c_slot) * z.share, z.share, 16)

    def launch(made):
        made.start()
        pending.append(made)

    def settle(until=None):
        done = pending[:until]
        del pending[:until]
        for made in done:
            if not isinstance(made, tuple):
                made.wait_send()
        for which in (inner, at_end):
            mine = [made[1] for made in done if isinstance(made, tuple) and made[0] is which]

            @pl.when(which)
            def _():
                for copy in mine:
                    copy().wait_send()

    def hold(p, value):
        for part in range(z.thirds):
            s.part[p, part] = value[:, part * z.third : (part + 1) * z.third].astype(BF16)
        for i in range(z.n_x):
            launch(core_copy(p, i))

    def core_copy(p, i):
        return remote(
            s.part.at[p, :, slot_rows(i, 1 - core)],
            from_core[p].at[i],
            s.core_send.at[p, i],
            s.core_recv.at[p, i],
            partner,
        )

    def chip_part(p, part, to):
        return s.part[p, part, slot_rows(to, core)].astype(F32) + from_core[p][to, part].astype(F32)

    def x_copy(p, part, i):
        return remote(
            s.to_x.at[p, i - 1, part],
            s.from_x.at[p, i - 1, part],
            s.x_send.at[p, part, i],
            s.x_recv.at[p, part, i],
            (seq, slot_at(i, core)),
        )

    def x_stage(p):
        for i in range(z.n_x):
            core_copy(p, i).wait_recv()
        for part in range(z.thirds):
            for i in range(1, z.n_x):
                s.to_x[p, i - 1, part] = chip_part(p, part, (x_at + i) % z.n_x).astype(BF16)
                launch(x_copy(p, part, i))

    def x_sum(p, part):
        value = chip_part(p, part, x_at)
        for i in range(1, z.n_x):
            x_copy(p, part, i).wait_recv()
            value = value + s.from_x[p, i - 1, part].astype(F32)
        return value

    place = slow % LINE
    inner = place * (LINE - 1 - place) > 0
    at_end = place * (LINE - 1 - place) == 0
    beside = (slow + 1 - 2 * (slow % 2)) * 2 + y_at
    swap_with = [(slow + 3 - 2 * place) * 2 + y_at]
    for step in range(z.swaps - 2):
        far = LINE << step
        swap_with.append((slow + far - 2 * far * (slow // far % 2)) * 2 + y_at)
    swap_with.append(slow * 2 + 1 - y_at)

    def inner_copy(p, part):
        return remote(
            s.to_inner.at[p, part],
            s.from_end.at[p, part],
            s.inner_send.at[p, part],
            s.inner_recv.at[p, part],
            (beside, ch),
        )

    def swap_copy(step, p, part):
        return remote(
            s.to_swap.at[step, p, part],
            s.from_swap.at[step, p, part],
            s.swap_send.at[step, p, part],
            s.swap_recv.at[step, p, part],
            (swap_with[step], ch),
        )

    def final_copy(p, part):
        return remote(
            s.final.at[p, part],
            s.final.at[p, part],
            s.final_send.at[p, part],
            s.final_recv.at[p, part],
            (beside, ch),
        )

    def launch_if(which, copy, *at):
        copy(*at).start()
        pending.append((which, functools.partial(copy, *at)))

    def gather_stage(p, part):
        value = x_sum(p, part)

        @pl.when(inner)
        def _():
            s.held[p, part] = value

        @pl.when(at_end)
        def _():
            s.to_inner[p, part] = value.astype(BF16)
            launch_if(at_end, inner_copy, p, part)

    def swapped(step, p, part):
        swap_copy(step, p, part).wait_recv()
        return s.to_swap[step, p, part].astype(F32) + s.from_swap[step, p, part].astype(F32)

    def swap_stage(step, p, part):
        @pl.when(inner)
        def _():
            if step == 0:
                inner_copy(p, part).wait_recv()
                value = s.held[p, part] + s.from_end[p, part].astype(F32)
            else:
                value = swapped(step - 1, p, part)
            s.to_swap[step, p, part] = value.astype(BF16)
            launch_if(inner, swap_copy, step, p, part)

    def keep(p, part):
        w_grad[p, :, part * z.third : (part + 1) * z.third] = s.final[p, part].astype(F32)

    def final_stage(p, part):
        @pl.when(inner)
        def _():
            s.final[p, part] = swapped(z.swaps - 1, p, part).astype(BF16)
            launch_if(inner, final_copy, p, part)
            keep(p, part)

    def last_stage(p, part):
        @pl.when(at_end)
        def _():
            final_copy(p, part).wait_recv()
            keep(p, part)

    def split(value):
        left, right = value[:, : z.half], value[:, z.half :]
        return jnp.where(y_at == 0, left, right), jnp.where(y_at == 0, right, left)

    def side_copy(part):
        return remote(
            s.to_side.at[part], s.from_side.at[part], s.side_send.at[part], s.side_recv.at[part], y_peer
        )

    def side_stage():
        for i in range(z.n_x):
            core_copy(3, i).wait_recv()
        for part in range(z.thirds):
            for i in range(z.n_x):
                own_half, give = split(chip_part(3, part, (x_at + i) % z.n_x))
                s.held_side[part, i] = own_half
                s.to_side[part, i] = give.astype(BF16)
            launch(side_copy(part))

    def far_copy(part, i):
        return remote(
            s.to_far.at[part, i],
            s.from_far.at[part, i],
            s.far_send.at[part, i],
            s.far_recv.at[part, i],
            (seq, slot_at(i, core)),
        )

    def far_stage(part):
        side_copy(part).wait_recv()
        s.held_far[part] = s.held_side[part, 0] + s.from_side[part, 0].astype(F32)
        for i in range(1, z.n_x):
            s.to_far[part, i] = (s.held_side[part, i] + s.from_side[part, i].astype(F32)).astype(BF16)
            launch(far_copy(part, i))

    def z_copy(step, part):
        far = 1 << step
        to = slow + far - 2 * far * (slow // far % 2)
        return remote(
            s.to_z.at[step, part],
            s.from_z.at[step, part],
            s.z_send.at[step, part],
            s.z_recv.at[step, part],
            (to * 2 + y_at, ch),
        )

    def z_sum(step, part):
        z_copy(step, part).wait_recv()
        return s.to_z[step, part].astype(F32) + s.from_z[step, part].astype(F32)

    def z_stage(step, part):
        if step == 0:
            value = s.held_far[part]
            for i in range(1, z.n_x):
                far_copy(part, i).wait_recv()
                value = value + s.from_far[part, i].astype(F32)
        else:
            value = z_sum(step - 1, part)
        s.to_z[step, part] = value.astype(BF16)
        launch(z_copy(step, part))

    def back_copy(part):
        return remote(s.mine.at[part], s.other.at[part], s.back_send.at[part], s.back_recv.at[part], y_peer)

    def back_stage(part):
        s.mine[part] = z_sum(z.doublings - 1, part).astype(BF16)
        launch(back_copy(part))

    def join_stage(part):
        back_copy(part).wait_recv()
        for side, half in ((y_at, s.mine), (1 - y_at, s.other)):
            lanes = rows_at(part * z.third + side * z.half, z.half, LANES)
            w_grad[3, :, lanes] = half[part].astype(F32)

    todo = []
    for n in range(3 * z.thirds):
        p, part = n // z.thirds, n % z.thirds
        at = 5.2 + 1.07 * n
        todo.append((at, functools.partial(gather_stage, p, part)))
        for step in range(z.swaps):
            todo.append((at + 3.6 * (step + 1), functools.partial(swap_stage, step, p, part)))
        todo.append((at + 3.6 * (z.swaps + 1), functools.partial(final_stage, p, part)))
        todo.append((at + 3.6 * (z.swaps + 2), functools.partial(last_stage, p, part)))
    for part in range(z.thirds):
        at = 11.4 + 1.07 * part
        todo.append((at, functools.partial(far_stage, part)))
        for step in range(z.doublings):
            todo.append((at + 3.0 + 3.2 * step, functools.partial(z_stage, step, part)))
        todo.append((at + 4.0 + 3.2 * z.doublings, functools.partial(back_stage, part)))
        todo.append((at + 7.0 + 3.2 * z.doublings, functools.partial(join_stage, part)))
    todo.sort(key=lambda item: item[0])

    def serve(until):
        while todo and todo[0][0] <= until:
            todo.pop(0)[1]()

    def down(row):
        return wide(jnp.transpose(jnp.broadcast_to(row, (LANES, z.f))), z.c)

    hold(0, down(scale_two) * s.point[...] + down(scale_two * (own_mean - mean_two) + whole_shift) * u_sum)
    blocks = z.ext // z.ext_step
    lax.fori_loop(0, blocks // 2, second_back, 0)
    x_stage(0)
    lax.fori_loop(blocks // 2, blocks, second_back, 0)

    def shift_rows(j, carry):
        start, size = own0 + j * z.own_step, z.own_step
        rows = rows_at(start, size, 16)
        to = rows_at(j * size, size, 16)
        later = wide(s.not_last[rows], z.f) * after(start, size, column(2))
        earlier = wide(s.not_first[rows], z.f) * before(start, size, column(2))
        s.shifted[to, column(0)] = later.astype(BF16)
        s.shifted[to, column(1)] = s.taps[rows_at(PAD + start, size), column(2)].astype(BF16)
        s.shifted[to, column(2)] = earlier.astype(BF16)
        return carry

    lax.fori_loop(0, z.bins // z.own_step, shift_rows, 0)
    for k in range(3):
        hold(
            k + 1,
            lax.dot_general(s.shifted[:, column(k)], s.normed[own_all], TN, preferred_element_type=F32),
        )
        if k > 0:
            x_stage(k)

    offset_back = -mean_one * inv_one

    def first_grad(j, carry):
        rows = rows_at(j * z.own_block, z.own_block, 16)
        grad = jnp.dot(s.shifted[rows], s.w[1:4].reshape(3 * z.f, z.c), preferred_element_type=F32)
        s.taps[rows_at(PAD + j * z.own_block, z.own_block), : z.c] = grad
        centred = s.act[own(j, z.own_block)] * inv_one + offset_back
        return carry[0] + fold(grad), carry[1] + fold(grad * centred)

    sums = (zero, zero)
    sums = lax.fori_loop(0, 1, first_grad, sums)
    side_stage()
    serve(7.5)
    sums = lax.fori_loop(1, 2, first_grad, sums)
    serve(8.7)
    sums = lax.fori_loop(2, 3, first_grad, sums)
    serve(9.8)

    def held(j):
        return rows_at(PAD + j * z.own_step, z.own_step)

    own_sum[2][0:1] = jnp.sum(sums[0], axis=0, keepdims=True)
    own_sum[2][1:2] = jnp.sum(sums[1], axis=0, keepdims=True)
    reduce_start(2)
    serve(10.5)
    reduce_spread(2)
    early = len(pending)

    def block_out(j, carry):
        rows = own(j, z.own_block)
        normed = (s.act_two[rows] * scale_two + offset_two).astype(BF16)
        branch = jnp.dot(normed, s.w[0], preferred_element_type=F32)
        out[rows_at(j * z.own_block, z.own_block, 16)] = (s.x[rows].astype(F32) + branch).astype(BF16)
        return carry

    for j in range(3):
        block_out(j, 0)
        serve(12.0 + j)
    settle(early)
    early = len(pending)
    serve(19.0)

    three = reduce_finish(2)
    shift_one_grad, gain_one_grad = three[0:1], three[1:2]
    stats[0:1] = gain_one_grad
    stats[1:2] = shift_one_grad
    picked = jnp.concatenate([gain_two_grad, shift_two_grad, jnp.zeros((6, z.f), F32)], axis=0)
    stats[2:4, : z.share] = lax.dot_general(
        picked, chosen.astype(F32), NT, precision=lax.Precision.HIGHEST, preferred_element_type=F32
    )[0:2]
    first_b = scale_one * inv_one * gain_one_grad / count
    first_a = scale_one * shift_one_grad / count - mean_one * first_b

    def input_grad(j, carry):
        rows, at = own(j, z.own_step), rows_at(j * z.own_step, z.own_step, 16)
        grad = scale_one * s.taps[held(j), : z.c] - wide(s.live[rows], z.c) * (first_a + first_b * s.act[rows])
        out_grad[at] = (s.u[rows].astype(F32) + grad * s.slope[at].astype(F32)).astype(BF16)
        return carry

    lax.fori_loop(0, steps // 2, input_grad, 0)
    serve(20.5)
    lax.fori_loop(steps // 2, steps, input_grad, 0)
    serve(21.5)
    settle(early)
    early = len(pending)
    serve(28.0)
    settle(early)
    serve(99.0)

    settle()


def write_out(out, out_grad, stats, w_grad, *refs):
    outs, (rows, pieces, sem) = refs[:8], refs[8:]

    def copy(i, src, dst):
        made = pltpu.make_async_copy(src, dst, sem.at[i])
        made.start()
        return made

    pairs = ((out, outs[0]), (out_grad, outs[1]), (w_grad.at[1:4], outs[4]), (w_grad.at[0], outs[7]))
    copies = [copy(i, *pair) for i, pair in enumerate(pairs)]
    channels, share = rows.shape[1], pieces.shape[1]
    for i in range(2):
        rows[i] = stats[i : i + 1].reshape(channels)
        pieces[i] = stats[i + 2 : i + 3, :share].reshape(share)
    small = ((rows.at[0], outs[2]), (rows.at[1], outs[3]), (pieces.at[0], outs[5]), (pieces.at[1], outs[6]))
    copies += [copy(4 + i, *pair) for i, pair in enumerate(small)]
    for made in copies:
        made.wait()


def local(z, block_in, cotangent, lengths, gain_one, shift_one, dilated_w, gain_two, shift_two, point_w):
    names = scratch_of(z)
    hbm = pl.BlockSpec(memory_space=pl.ANY)
    vmem = pl.BlockSpec(memory_space=pltpu.VMEM)
    smem = pl.BlockSpec(memory_space=pltpu.SMEM)
    shape = jax.ShapeDtypeStruct
    big = shape((z.bins, z.c), BF16)
    held = pltpu.VMEM((z.bins, z.c), BF16)
    results = pl.pallas_call(
        functools.partial(kernel, z, tuple(names)),
        out_shape=(held, held, pltpu.VMEM((8, z.c), F32), pltpu.VMEM((4, z.share, z.c), F32)),
        in_specs=[hbm, hbm, smem, vmem, vmem, hbm, vmem, vmem, hbm],
        out_specs=(vmem,) * 4,
        scratch_shapes=list(names.values()),
        compiler_params=pltpu.CompilerParams(
            collective_id=0, has_side_effects=True, vmem_limit_bytes=VMEM_LIMIT
        ),
    )(
        block_in,
        cotangent,
        lengths,
        gain_one,
        shift_one,
        jnp.transpose(dilated_w, (1, 0, 2)),
        gain_two,
        shift_two,
        point_w,
    )
    row, piece = shape((z.c,), F32), shape((z.share,), F32)
    outs = pl.pallas_call(
        write_out,
        out_shape=(big, big, row, row, shape((3, z.share, z.c), F32), piece, piece, shape((z.share, z.c), F32)),
        in_specs=[vmem] * 4,
        out_specs=(hbm,) * 8,
        scratch_shapes=[
            pltpu.VMEM((2, z.c), F32),
            pltpu.VMEM((2, z.share), F32),
            pltpu.SemaphoreType.DMA((8,)),
        ],
        compiler_params=pltpu.CompilerParams(vmem_limit_bytes=2 * 2**20),
    )(*results)
    return (*outs[:4], jnp.transpose(outs[4], (1, 0, 2)), *outs[5:])


def solution(mesh):
    n_seq, n_ch = mesh.shape["seq"], mesh.shape["ch"]

    def run(block_in, cotangent, lengths, gain_one, shift_one, dilated_w, gain_two, shift_two, point_w):
        z = plan(
            n_seq, n_ch, block_in.shape[0], block_in.shape[1], dilated_w.shape[0] * n_ch, lengths.shape[0]
        )
        return local(
            z, block_in, cotangent, lengths, gain_one, shift_one, dilated_w, gain_two, shift_two, point_w
        )

    return jax.shard_map(
        run,
        mesh=mesh,
        in_specs=(
            P(("seq", "ch"), None),
            P(("seq", "ch"), None),
            P(),
            P(),
            P(),
            P("ch", None, None),
            P("ch"),
            P("ch"),
            P("ch", None),
        ),
        out_specs=(
            P(("seq", "ch"), None),
            P(("seq", "ch"), None),
            P(),
            P(),
            P("ch", None, None),
            P("ch"),
            P("ch"),
            P("ch", None),
        ),
        check_vma=False,
    )
```

```python
import functools
import types

import jax
import jax.numpy as jnp
from jax import lax
from jax.experimental import pallas as pl
from jax.experimental.pallas import tpu as pltpu
from jax.sharding import PartitionSpec as P

DILATION = 17
EPS = 0.001
HALO = 48
PAD = 24
LANES = 128
LINE = 4
VMEM_LIMIT = 57 * 2**20
MESH = pl.DeviceIdType.MESH
F32 = jnp.float32
BF16 = jnp.bfloat16
NT = (((1,), (1,)), ((), ()))
TN = (((0,), (0,)), ((), ()))
GELU_A = 0.7978845608028654
GELU_B = GELU_A * 0.044715


def gelu_half(v):
    square = v * v
    half = 0.5 + 0.5 * jnp.tanh(v * (GELU_A + GELU_B * square))
    return half, square


def gelu_slope(v, half, square):
    return half + (2.0 * v) * (half * (1.0 - half)) * (GELU_A + 3.0 * GELU_B * square)


def wide(mask, width):
    return jnp.concatenate([mask] * (width // LANES), axis=1)


def fold(value):
    rows, width = value.shape
    return jnp.sum(value.reshape(rows // 8, 8, width), axis=0)


def rows_at(start, size, step=8):
    return pl.ds(pl.multiple_of(start, step), size)


def plan(n_seq, n_ch, bins, channels, mid, n_windows):
    z = types.SimpleNamespace()
    z.n_seq, z.n_ch = n_seq, n_ch
    z.bins, z.c, z.f, z.n_windows = bins, channels, mid, n_windows
    z.share = mid // n_ch
    z.n_x = n_ch // 2
    z.n_chips = n_seq * z.n_x
    z.window = bins * n_ch * n_seq // n_windows
    z.pair_windows = 2 * bins // z.window
    z.lines = n_seq // (2 * LINE)
    z.swaps = 1 + z.lines.bit_length()
    z.doublings = z.swaps
    z.ext = bins + HALO
    assert n_ch % 2 == 0 and n_seq == 2 * LINE << (z.swaps - 2)
    assert 2 * bins % z.window == 0 and HALO >= 2 * DILATION
    z.ext_step = z.ext // 9
    z.ext_block = z.ext // 3
    z.own_step = bins // 8
    z.own_block = bins // 3
    assert z.ext_step % 16 == 0 and z.own_step % 16 == 0
    z.thirds = 3
    z.third = channels // z.thirds
    z.half = z.third // 2
    z.near = z.share // 2
    return z


def scratch_of(z):
    dma = pltpu.SemaphoreType.DMA
    vmem = pltpu.VMEM
    return dict(
        x=vmem((z.ext, z.c), BF16),
        u=vmem((z.ext, z.c), BF16),
        x_edge=vmem((HALO, z.c), BF16),
        u_edge=vmem((HALO, z.c), BF16),
        act=vmem((z.ext, z.c), F32),
        slope=vmem((z.bins, z.c), BF16),
        normed=vmem((z.ext, z.c), BF16),
        w=vmem((4, z.f, z.c), BF16),
        taps=vmem((z.ext + 2 * PAD, 3 * z.f), F32),
        grad_two=vmem((z.ext, z.f), F32),
        act_two=vmem((z.ext, z.f), F32),
        slope_two=vmem((z.ext, z.f), F32),
        shifted=vmem((z.bins, 3 * z.f), BF16),
        live=vmem((z.ext, LANES), F32),
        live_own=vmem((z.ext, LANES), F32),
        not_first=vmem((z.ext, LANES), F32),
        not_last=vmem((z.ext, LANES), F32),
        gains=vmem((z.n_ch, 8, z.f), F32),
        **{f"own_sum_{i}": vmem((2, z.c), F32) for i in range(3)},
        **{f"pair_sum_{i}": vmem((2, z.c), F32) for i in range(3)},
        **{f"chip_sum_{i}": vmem((z.n_chips, 2, z.c), F32) for i in range(3)},
        centred=vmem((z.bins, z.f), BF16),
        point=vmem((z.f, z.c), F32),
        part=vmem((4, z.thirds, z.f, z.third), BF16),
        **{f"from_core_{p}": vmem((z.n_x, z.thirds, z.share, z.third), BF16) for p in range(4)},
        to_x=vmem((3, z.n_x - 1, z.thirds, z.share, z.third), BF16),
        from_x=vmem((3, z.n_x - 1, z.thirds, z.share, z.third), BF16),
        held=vmem((3, z.thirds, z.share, z.third), F32),
        to_inner=vmem((3, z.thirds, z.share, z.third), BF16),
        from_end=vmem((3, z.thirds, z.share, z.third), BF16),
        to_swap=vmem((z.swaps, 3, z.thirds, z.share, z.third), BF16),
        from_swap=vmem((z.swaps, 3, z.thirds, z.share, z.third), BF16),
        final=vmem((3, z.thirds, z.share, z.third), BF16),
        held_side=vmem((z.thirds, z.n_x, z.share, z.half), F32),
        to_side=vmem((z.thirds, z.n_x, z.share, z.half), BF16),
        from_side=vmem((z.thirds, z.n_x, z.share, z.half), BF16),
        held_far=vmem((z.thirds, z.share, z.half), F32),
        to_far=vmem((z.thirds, z.n_x, z.share, z.half), BF16),
        from_far=vmem((z.thirds, z.n_x, z.share, z.half), BF16),
        to_z=vmem((z.doublings, z.thirds, z.share, z.half), BF16),
        from_z=vmem((z.doublings, z.thirds, z.share, z.half), BF16),
        mine=vmem((z.thirds, z.share, z.half), BF16),
        other=vmem((z.thirds, z.share, z.half), BF16),
        local_sem=dma((6,)),
        halo_send=dma((2,)),
        halo_recv=dma((2,)),
        gain_send=dma((z.n_ch,)),
        gain_recv=dma((z.n_ch,)),
        w_send=dma((4, z.n_x, 4)),
        w_recv=dma((4, z.n_x, 4)),
        pair_send=dma((3,)),
        pair_recv=dma((3,)),
        chip_send=dma((3, z.n_chips)),
        chip_recv=dma((3, z.n_chips)),
        core_send=dma((4, z.n_x)),
        core_recv=dma((4, z.n_x)),
        x_send=dma((4, z.thirds, z.n_x)),
        x_recv=dma((4, z.thirds, z.n_x)),
        inner_send=dma((4, z.thirds)),
        inner_recv=dma((4, z.thirds)),
        swap_send=dma((z.swaps, 4, z.thirds)),
        swap_recv=dma((z.swaps, 4, z.thirds)),
        final_send=dma((4, z.thirds)),
        final_recv=dma((4, z.thirds)),
        side_send=dma((z.thirds,)),
        side_recv=dma((z.thirds,)),
        far_send=dma((z.thirds, z.n_x)),
        far_recv=dma((z.thirds, z.n_x)),
        z_send=dma((z.doublings, z.thirds)),
        z_recv=dma((z.doublings, z.thirds)),
        back_send=dma((z.thirds,)),
        back_recv=dma((z.thirds,)),
    )


def kernel(
    z,
    names,
    x_hbm,
    cot_hbm,
    lengths,
    gain_one,
    shift_one,
    taps_hbm,
    gain_two,
    shift_two,
    point_hbm,
    out,
    out_grad,
    stats,
    w_grad,
    *scratch,
):
    s = types.SimpleNamespace(**dict(zip(names, scratch)))
    seq, ch = lax.axis_index("seq"), lax.axis_index("ch")
    x_at, core = ch // 2, ch % 2
    slow, y_at = seq // 2, seq % 2
    chip = seq * z.n_x + x_at
    partner = (seq, x_at * 2 + 1 - core)
    y_peer = (slow * 2 + 1 - y_at, ch)
    own0 = core * HALO
    pending = []
    own_sum = (s.own_sum_0, s.own_sum_1, s.own_sum_2)
    pair_sum = (s.pair_sum_0, s.pair_sum_1, s.pair_sum_2)
    chip_sum = (s.chip_sum_0, s.chip_sum_1, s.chip_sum_2)
    from_core = (s.from_core_0, s.from_core_1, s.from_core_2, s.from_core_3)

    def remote(src, dst, send_sem, recv_sem, device):
        return pltpu.make_async_remote_copy(
            src_ref=src,
            dst_ref=dst,
            send_sem=send_sem,
            recv_sem=recv_sem,
            device_id=device,
            device_id_type=MESH,
        )

    def send(*copy):
        made = remote(*copy)
        made.start()
        pending.append(made)

    def chip_device(q):
        return (q // z.n_x, (q % z.n_x) * 2 + core)

    def other_chip(j):
        return (chip + 1 + j) % z.n_chips

    def own(j, size):
        return rows_at(own0 + j * size, size, 16)

    def column(k):
        return slice(k * z.f, (k + 1) * z.f)

    load_x = pltpu.make_async_copy(x_hbm, s.x.at[rows_at(own0, z.bins, 16)], s.local_sem.at[0])
    load_x.start()
    load_u = pltpu.make_async_copy(cot_hbm, s.u.at[rows_at(own0, z.bins, 16)], s.local_sem.at[1])
    load_u.start()
    own_rows = rows_at(ch * z.share, z.share, 16)
    sources = [point_hbm, taps_hbm.at[0], taps_hbm.at[1], taps_hbm.at[2]]
    load_w = [
        pltpu.make_async_copy(src, s.w.at[p, own_rows], s.local_sem.at[2 + p]) for p, src in enumerate(sources)
    ]
    for made in load_w:
        made.start()

    barrier = pltpu.get_barrier_semaphore()

    def greet(j, carry):
        pl.semaphore_signal(barrier, inc=1, device_id=chip_device(other_chip(j)), device_id_type=MESH)
        return carry

    for i in range(z.n_x):
        across = (seq, ((x_at + i) % z.n_x) * 2 + 1 - core)
        pl.semaphore_signal(barrier, inc=1, device_id=across, device_id_type=MESH)
    lax.fori_loop(0, z.n_chips - 1, greet, 0)

    pair = (seq * z.n_ch + ch) // 2
    window_lengths = [lengths[pair * z.pair_windows + i] for i in range(z.pair_windows)]

    def make_masks(j, total):
        rows = rows_at(j * z.ext_step, z.ext_step, 16)
        at = lax.broadcasted_iota(jnp.int32, (z.ext_step, LANES), 0) + j * z.ext_step
        place = at + core * (z.bins - HALO)
        inside, limit = place, jnp.full(place.shape, window_lengths[0], jnp.int32)
        for i in range(1, z.pair_windows):
            past = place >= i * z.window
            inside = jnp.where(past, place - i * z.window, inside)
            limit = jnp.where(past, window_lengths[i], limit)
        live = (inside < limit).astype(F32)
        mine = ((at >= own0) & (at < own0 + z.bins)).astype(F32)
        s.live[rows] = live
        s.live_own[rows] = live * mine
        s.not_first[rows] = (inside >= DILATION).astype(F32)
        s.not_last[rows] = (inside < z.window - DILATION).astype(F32)
        return total + fold(live * mine)

    live_rows = lax.fori_loop(0, z.ext // z.ext_step, make_masks, jnp.zeros((8, LANES), F32))
    own_count = jnp.maximum(wide(jnp.sum(live_rows, axis=0, keepdims=True), z.f), 1.0)
    bin_total = lax.fori_loop(0, z.n_windows, lambda i, t: t + lengths[i], jnp.int32(0))
    count = jnp.full((1, z.c), bin_total, jnp.int32).astype(F32)
    count_two = count[:, : z.f]
    s.taps[0:PAD] = jnp.zeros((PAD, 3 * z.f), F32)
    s.taps[PAD + z.ext : 2 * PAD + z.ext] = jnp.zeros((PAD, 3 * z.f), F32)

    chosen = lax.broadcasted_iota(jnp.int32, (z.share, z.f), 1) == (
        lax.broadcasted_iota(jnp.int32, (z.share, z.f), 0) + ch * z.share
    )
    both = [v[...].astype(F32).reshape(1, z.share) for v in (gain_two, shift_two)]
    both = jnp.concatenate(both + [jnp.zeros((6, z.share), F32)], axis=0)
    placed = jnp.dot(both.astype(BF16), chosen.astype(BF16), preferred_element_type=F32)
    s.gains[pl.ds(ch, 1)] = placed.reshape(1, 8, z.f)

    load_x.wait()

    def first_act(j, carry):
        rows = own(j, z.own_step)
        v = s.x[rows].astype(F32)
        half, _ = gelu_half(v)
        act = v * half
        s.act[rows] = act
        masked = wide(s.live[rows], z.c) * act
        return carry[0] + fold(masked), carry[1] + fold(masked * act)

    zero = jnp.zeros((8, z.c), F32)
    steps = z.bins // z.own_step
    sums = lax.fori_loop(0, steps // 2, first_act, (zero, zero))

    pl.semaphore_wait(barrier, z.n_chips - 1 + z.n_x)

    near0 = y_at * z.near

    def slot_at(i, c_slot):
        return ((x_at + i) % z.n_x) * 2 + c_slot

    def half_rows(slot, y_half):
        return rows_at(slot * z.share + y_half * z.near, z.near, 16)

    def x_rows(slot, p):
        return half_rows(slot, y_at) if p else rows_at(slot * z.share, z.share, 16)

    def w_copy(kind, i, p, src, rows, to):
        return remote(src, s.w.at[p, rows], s.w_send.at[kind, i, p], s.w_recv.at[kind, i, p], to)

    def w_along(p):
        for i in range(1, z.n_x):
            made = w_copy(
                0,
                i,
                p,
                sources[p].at[rows_at(near0, z.near, 16)] if p else sources[p],
                x_rows(ch, p),
                (seq, slot_at(i, core)),
            )
            made.start()
            pending.append(made)

    def w_across(p):
        made = w_copy(0, 0, p, sources[p], own_rows, partner)
        made.start()
        pending.append(made)

    w_along(1)
    w_along(2)

    def w_pass(kind, p):
        for i in range(1, z.n_x):
            slot = slot_at(z.n_x - i, core)
            rows = x_rows(slot, p) if kind == 0 else half_rows(slot, 1 - y_at)
            here = s.w.at[p, rows]
            w_copy(kind, i, p, here, rows, partner).wait_recv()
            onward = [w_copy(2 + kind, i, p, here, rows, partner)]
            if kind == 0 and p:
                onward.append(w_copy(1, i, p, here, rows, y_peer))
            for made in onward:
                made.start()
                pending.append(made)

    def w_here(p):
        load_w[p].wait()
        whole = rows_at(slot_at(0, 1 - core) * z.share, z.share, 16)
        w_copy(0, 0, p, sources[p], whole, partner).wait_recv()
        for i in range(1, z.n_x):
            slot = slot_at(z.n_x - i, 1 - core)
            for kind in range(2 if p else 1):
                rows = x_rows(slot, p) if kind == 0 else half_rows(slot, 1 - y_at)
                w_copy(2 + kind, i, p, s.w.at[p, rows], rows, partner).wait_recv()

    def reduce_start(i):
        send(own_sum[i], pair_sum[i], s.pair_send.at[i], s.pair_recv.at[i], partner)

    def chip_copy(i, slot, j):
        return remote(
            chip_sum[i].at[slot],
            chip_sum[i].at[slot],
            s.chip_send.at[i, j],
            s.chip_recv.at[i, slot],
            chip_device(other_chip(j)),
        )

    def reduce_spread(i):
        remote(own_sum[i], pair_sum[i], s.pair_send.at[i], s.pair_recv.at[i], partner).wait_recv()
        chip_sum[i][pl.ds(chip, 1)] = (own_sum[i][...] + pair_sum[i][...]).reshape(1, 2, z.c)

        for j in range(z.n_chips - 1):
            made = chip_copy(i, chip, j)
            made.start()
            pending.append(made)

    def reduce_finish(i):
        for j in range(z.n_chips - 1):
            chip_copy(i, other_chip(j), j).wait_recv()
        return jnp.sum(chip_sum[i][...], axis=0)

    sums = lax.fori_loop(steps // 2, steps, first_act, sums)
    own_sum[0][0:1] = jnp.sum(sums[0], axis=0, keepdims=True)
    own_sum[0][1:2] = jnp.sum(sums[1], axis=0, keepdims=True)
    reduce_start(0)

    load_u.wait()

    def first_slope(j, total):
        rows = own(j, z.own_step)
        v = s.x[rows].astype(F32)
        half, square = gelu_half(v)
        s.slope[rows_at(j * z.own_step, z.own_step, 16)] = gelu_slope(v, half, square).astype(BF16)
        masked = s.u[rows].astype(F32) * wide(s.live[rows], z.c)
        s.u[rows] = masked.astype(BF16)
        return total + fold(masked)

    def halo_rows():
        return rows_at((1 - core) * z.bins, HALO, 16)

    reduce_spread(0)
    w_along(3)
    w_along(0)
    w_across(1)
    w_across(2)

    away = (1 - core) * (z.bins - HALO)
    halo_copies = [
        remote(src.at[rows_at(away, HALO, 16)], dst, s.halo_send.at[i], s.halo_recv.at[i], partner)
        for i, (src, dst) in enumerate(((x_hbm, s.x_edge), (cot_hbm, s.u_edge)))
    ]
    for made in halo_copies:
        made.start()
        pending.append(made)
    w_across(3)
    w_across(0)
    for i in range(1, z.n_ch):
        send(
            s.gains.at[pl.ds(ch, 1)],
            s.gains.at[pl.ds(ch, 1)],
            s.gain_send.at[i],
            s.gain_recv.at[ch],
            (seq, (ch + i) % z.n_ch),
        )
    u_sum = lax.fori_loop(0, steps // 2, first_slope, zero)
    w_pass(0, 1)
    w_pass(0, 2)
    u_sum = lax.fori_loop(steps // 2, steps, first_slope, u_sum)
    for made in halo_copies:
        made.wait_recv()
    edge = s.x_edge[...].astype(F32)
    s.act[halo_rows()] = edge * gelu_half(edge)[0]
    s.u[halo_rows()] = (s.u_edge[...].astype(F32) * wide(s.live[halo_rows()], z.c)).astype(BF16)
    w_pass(0, 3)
    w_pass(1, 1)
    u_sum = jnp.sum(u_sum, axis=0, keepdims=True)

    for i in range(1, z.n_ch):
        slot = (ch + i) % z.n_ch
        remote(
            s.gains.at[pl.ds(slot, 1)],
            s.gains.at[pl.ds(slot, 1)],
            s.gain_send.at[i],
            s.gain_recv.at[slot],
            (seq, slot),
        ).wait_recv()
    both = s.gains[0]
    for i in range(1, z.n_ch):
        both = both + s.gains[i]
    whole_gain, whole_shift = both[0:1], both[1:2]

    one = reduce_finish(0)
    mean_one = one[0:1] / count
    inv_one = lax.rsqrt(one[1:2] / count - mean_one * mean_one + EPS)
    scale_one = gain_one[...].astype(F32).reshape(1, z.c) * inv_one
    offset_one = shift_one[...].astype(F32).reshape(1, z.c) - mean_one * scale_one

    def convolve(first, last):
        def step(j, carry):
            s.taps[rows_at(PAD + j * z.ext_block, z.ext_block), first * z.f : last * z.f] = lax.dot_general(
                s.normed[rows_at(j * z.ext_block, z.ext_block, 16)],
                s.w[first + 1 : last + 1].reshape((last - first) * z.f, z.c),
                NT,
                preferred_element_type=F32,
            )
            return carry

        lax.fori_loop(0, 3, step, 0)

    w_pass(1, 2)
    w_here(1)

    def first_norm(j, carry):
        rows = rows_at(j * z.ext_block, z.ext_block, 16)
        normed = (s.act[rows] * scale_one + offset_one).astype(BF16)
        s.normed[rows] = normed
        s.taps[rows_at(PAD + j * z.ext_block, z.ext_block), : z.f] = lax.dot_general(
            normed, s.w[1], NT, preferred_element_type=F32
        )
        return carry

    lax.fori_loop(0, 3, first_norm, 0)
    w_pass(0, 0)
    w_pass(1, 3)
    w_here(2)
    w_here(3)
    convolve(1, 3)
    w_here(0)

    def before(start, size, columns):
        return s.taps[rows_at(start, size + 8), columns][PAD - DILATION : PAD - DILATION + size]

    def after(start, size, columns):
        low = (PAD + DILATION) // 8 * 8
        skip = PAD + DILATION - low
        return s.taps[rows_at(start + low, size + 8), columns][skip : skip + size]

    def second_act(j, carry):
        start, size = j * z.ext_block, z.ext_block
        rows = rows_at(start, size, 16)
        grad = lax.dot_general(s.u[rows], s.w[0], NT, preferred_element_type=F32)
        s.grad_two[rows] = grad
        hidden = (
            s.taps[rows_at(PAD + start, size), column(1)]
            + wide(s.not_first[rows], z.f) * before(start, size, column(0))
            + wide(s.not_last[rows], z.f) * after(start, size, column(2))
        )
        half, square = gelu_half(hidden)
        act = hidden * half
        s.act_two[rows] = act
        s.slope_two[rows] = gelu_slope(hidden, half, square)
        mask = wide(s.live_own[rows], z.f)
        masked, grad = mask * act, mask * grad
        terms = (masked, masked * act, grad, grad * act)
        return tuple(total + fold(term) for total, term in zip(carry, terms))

    zero_two = jnp.zeros((8, z.f), F32)
    sums = lax.fori_loop(0, 3, second_act, (zero_two,) * 4)
    sums = [jnp.sum(v, axis=0, keepdims=True) for v in sums]
    own_sum[1][0:1, : z.f] = sums[0]
    own_sum[1][0:1, z.f :] = sums[1]
    own_sum[1][1:2, : z.f] = sums[2]
    own_sum[1][1:2, z.f :] = sums[3]
    reduce_start(1)
    own_mean = sums[0] / own_count

    def centre(j, carry):
        s.centred[rows_at(j * z.own_step, z.own_step, 16)] = (s.act_two[own(j, z.own_step)] - own_mean).astype(BF16)
        return carry

    lax.fori_loop(0, steps, centre, 0)
    reduce_spread(1)
    own_all = rows_at(own0, z.bins, 16)
    s.point[...] = lax.dot_general(s.centred[...], s.u[own_all], TN, preferred_element_type=F32)
    two = reduce_finish(1)
    mean_two = two[0:1, : z.f] / count_two
    inv_two = lax.rsqrt(two[0:1, z.f :] / count_two - mean_two * mean_two + EPS)
    shift_two_grad = two[1:2, : z.f]
    gain_two_grad = inv_two * (two[1:2, z.f :] - mean_two * shift_two_grad)
    scale_two = whole_gain * inv_two
    offset_two = whole_shift - mean_two * scale_two
    back_b = scale_two * inv_two * gain_two_grad / count_two
    back_a = scale_two * shift_two_grad / count_two - mean_two * back_b

    def second_back(j, carry):
        rows = rows_at(j * z.ext_step, z.ext_step, 16)
        grad = scale_two * s.grad_two[rows] - wide(s.live[rows], z.f) * (back_a + back_b * s.act_two[rows])
        s.taps[rows_at(PAD + j * z.ext_step, z.ext_step), column(2)] = grad * s.slope_two[rows]
        return carry

    def slot_rows(x_slot, c_slot):
        return rows_at((x_slot * 2 + c_slot) * z.share, z.share, 16)

    def launch(made):
        made.start()
        pending.append(made)

    def settle(until=None):
        done = pending[:until]
        del pending[:until]
        for made in done:
            if not isinstance(made, tuple):
                made.wait_send()
        for which in (inner, at_end):
            mine = [made[1] for made in done if isinstance(made, tuple) and made[0] is which]

            @pl.when(which)
            def _():
                for copy in mine:
                    copy().wait_send()

    def hold(p, value):
        for part in range(z.thirds):
            s.part[p, part] = value[:, part * z.third : (part + 1) * z.third].astype(BF16)
        for i in range(z.n_x):
            launch(core_copy(p, i))

    def core_copy(p, i):
        return remote(
            s.part.at[p, :, slot_rows(i, 1 - core)],
            from_core[p].at[i],
            s.core_send.at[p, i],
            s.core_recv.at[p, i],
            partner,
        )

    def chip_part(p, part, to):
        return s.part[p, part, slot_rows(to, core)].astype(F32) + from_core[p][to, part].astype(F32)

    def x_copy(p, part, i):
        return remote(
            s.to_x.at[p, i - 1, part],
            s.from_x.at[p, i - 1, part],
            s.x_send.at[p, part, i],
            s.x_recv.at[p, part, i],
            (seq, slot_at(i, core)),
        )

    def x_stage(p):
        for i in range(z.n_x):
            core_copy(p, i).wait_recv()
        for part in range(z.thirds):
            for i in range(1, z.n_x):
                s.to_x[p, i - 1, part] = chip_part(p, part, (x_at + i) % z.n_x).astype(BF16)
                launch(x_copy(p, part, i))

    def x_sum(p, part):
        value = chip_part(p, part, x_at)
        for i in range(1, z.n_x):
            x_copy(p, part, i).wait_recv()
            value = value + s.from_x[p, i - 1, part].astype(F32)
        return value

    place = slow % LINE
    inner = place * (LINE - 1 - place) > 0
    at_end = place * (LINE - 1 - place) == 0
    beside = (slow + 1 - 2 * (slow % 2)) * 2 + y_at
    swap_with = [(slow + 3 - 2 * place) * 2 + y_at]
    for step in range(z.swaps - 2):
        far = LINE << step
        swap_with.append((slow + far - 2 * far * (slow // far % 2)) * 2 + y_at)
    swap_with.append(slow * 2 + 1 - y_at)

    def inner_copy(p, part):
        return remote(
            s.to_inner.at[p, part],
            s.from_end.at[p, part],
            s.inner_send.at[p, part],
            s.inner_recv.at[p, part],
            (beside, ch),
        )

    def swap_copy(step, p, part):
        return remote(
            s.to_swap.at[step, p, part],
            s.from_swap.at[step, p, part],
            s.swap_send.at[step, p, part],
            s.swap_recv.at[step, p, part],
            (swap_with[step], ch),
        )

    def final_copy(p, part):
        return remote(
            s.final.at[p, part],
            s.final.at[p, part],
            s.final_send.at[p, part],
            s.final_recv.at[p, part],
            (beside, ch),
        )

    def launch_if(which, copy, *at):
        copy(*at).start()
        pending.append((which, functools.partial(copy, *at)))

    def gather_stage(p, part):
        value = x_sum(p, part)

        @pl.when(inner)
        def _():
            s.held[p, part] = value

        @pl.when(at_end)
        def _():
            s.to_inner[p, part] = value.astype(BF16)
            launch_if(at_end, inner_copy, p, part)

    def swapped(step, p, part):
        swap_copy(step, p, part).wait_recv()
        return s.to_swap[step, p, part].astype(F32) + s.from_swap[step, p, part].astype(F32)

    def swap_stage(step, p, part):
        @pl.when(inner)
        def _():
            if step == 0:
                inner_copy(p, part).wait_recv()
                value = s.held[p, part] + s.from_end[p, part].astype(F32)
            else:
                value = swapped(step - 1, p, part)
            s.to_swap[step, p, part] = value.astype(BF16)
            launch_if(inner, swap_copy, step, p, part)

    def keep(p, part):
        w_grad[p, :, part * z.third : (part + 1) * z.third] = s.final[p, part].astype(F32)

    def final_stage(p, part):
        @pl.when(inner)
        def _():
            s.final[p, part] = swapped(z.swaps - 1, p, part).astype(BF16)
            launch_if(inner, final_copy, p, part)
            keep(p, part)

    def last_stage(p, part):
        @pl.when(at_end)
        def _():
            final_copy(p, part).wait_recv()
            keep(p, part)

    def split(value):
        left, right = value[:, : z.half], value[:, z.half :]
        return jnp.where(y_at == 0, left, right), jnp.where(y_at == 0, right, left)

    def side_copy(part):
        return remote(
            s.to_side.at[part], s.from_side.at[part], s.side_send.at[part], s.side_recv.at[part], y_peer
        )

    def side_stage():
        for i in range(z.n_x):
            core_copy(3, i).wait_recv()
        for part in range(z.thirds):
            for i in range(z.n_x):
                own_half, give = split(chip_part(3, part, (x_at + i) % z.n_x))
                s.held_side[part, i] = own_half
                s.to_side[part, i] = give.astype(BF16)
            launch(side_copy(part))

    def far_copy(part, i):
        return remote(
            s.to_far.at[part, i],
            s.from_far.at[part, i],
            s.far_send.at[part, i],
            s.far_recv.at[part, i],
            (seq, slot_at(i, core)),
        )

    def far_stage(part):
        side_copy(part).wait_recv()
        s.held_far[part] = s.held_side[part, 0] + s.from_side[part, 0].astype(F32)
        for i in range(1, z.n_x):
            s.to_far[part, i] = (s.held_side[part, i] + s.from_side[part, i].astype(F32)).astype(BF16)
            launch(far_copy(part, i))

    def z_copy(step, part):
        far = 1 << step
        to = slow + far - 2 * far * (slow // far % 2)
        return remote(
            s.to_z.at[step, part],
            s.from_z.at[step, part],
            s.z_send.at[step, part],
            s.z_recv.at[step, part],
            (to * 2 + y_at, ch),
        )

    def z_sum(step, part):
        z_copy(step, part).wait_recv()
        return s.to_z[step, part].astype(F32) + s.from_z[step, part].astype(F32)

    def z_stage(step, part):
        if step == 0:
            value = s.held_far[part]
            for i in range(1, z.n_x):
                far_copy(part, i).wait_recv()
                value = value + s.from_far[part, i].astype(F32)
        else:
            value = z_sum(step - 1, part)
        s.to_z[step, part] = value.astype(BF16)
        launch(z_copy(step, part))

    def back_copy(part):
        return remote(s.mine.at[part], s.other.at[part], s.back_send.at[part], s.back_recv.at[part], y_peer)

    def back_stage(part):
        s.mine[part] = z_sum(z.doublings - 1, part).astype(BF16)
        launch(back_copy(part))

    def join_stage(part):
        back_copy(part).wait_recv()
        for side, half in ((y_at, s.mine), (1 - y_at, s.other)):
            lanes = rows_at(part * z.third + side * z.half, z.half, LANES)
            w_grad[3, :, lanes] = half[part].astype(F32)

    todo = []
    for n in range(3 * z.thirds):
        p, part = n // z.thirds, n % z.thirds
        at = 5.2 + 1.07 * n
        todo.append((at, functools.partial(gather_stage, p, part)))
        for step in range(z.swaps):
            todo.append((at + 3.6 * (step + 1), functools.partial(swap_stage, step, p, part)))
        todo.append((at + 3.6 * (z.swaps + 1), functools.partial(final_stage, p, part)))
        todo.append((at + 3.6 * (z.swaps + 2), functools.partial(last_stage, p, part)))
    for part in range(z.thirds):
        at = 11.4 + 1.07 * part
        todo.append((at, functools.partial(far_stage, part)))
        for step in range(z.doublings):
            todo.append((at + 3.0 + 3.2 * step, functools.partial(z_stage, step, part)))
        todo.append((at + 4.0 + 3.2 * z.doublings, functools.partial(back_stage, part)))
        todo.append((at + 7.0 + 3.2 * z.doublings, functools.partial(join_stage, part)))
    todo.sort(key=lambda item: item[0])

    def serve(until):
        while todo and todo[0][0] <= until:
            todo.pop(0)[1]()

    def down(row):
        return wide(jnp.transpose(jnp.broadcast_to(row, (LANES, z.f))), z.c)

    hold(0, down(scale_two) * s.point[...] + down(scale_two * (own_mean - mean_two) + whole_shift) * u_sum)
    blocks = z.ext // z.ext_step
    lax.fori_loop(0, blocks // 2, second_back, 0)
    x_stage(0)
    lax.fori_loop(blocks // 2, blocks, second_back, 0)

    def shift_rows(j, carry):
        start, size = own0 + j * z.own_step, z.own_step
        rows = rows_at(start, size, 16)
        to = rows_at(j * size, size, 16)
        later = wide(s.not_last[rows], z.f) * after(start, size, column(2))
        earlier = wide(s.not_first[rows], z.f) * before(start, size, column(2))
        s.shifted[to, column(0)] = later.astype(BF16)
        s.shifted[to, column(1)] = s.taps[rows_at(PAD + start, size), column(2)].astype(BF16)
        s.shifted[to, column(2)] = earlier.astype(BF16)
        return carry

    lax.fori_loop(0, z.bins // z.own_step, shift_rows, 0)
    for k in range(3):
        hold(
            k + 1,
            lax.dot_general(s.shifted[:, column(k)], s.normed[own_all], TN, preferred_element_type=F32),
        )
        if k > 0:
            x_stage(k)
            serve((0.0, 5.3, 6.4)[k])

    offset_back = -mean_one * inv_one

    def first_grad(j, carry):
        rows = rows_at(j * z.own_block, z.own_block, 16)
        grad = jnp.dot(s.shifted[rows], s.w[1:4].reshape(3 * z.f, z.c), preferred_element_type=F32)
        s.taps[rows_at(PAD + j * z.own_block, z.own_block), : z.c] = grad
        centred = s.act[own(j, z.own_block)] * inv_one + offset_back
        return carry[0] + fold(grad), carry[1] + fold(grad * centred)

    sums = (zero, zero)
    sums = lax.fori_loop(0, 1, first_grad, sums)
    side_stage()
    serve(8.0)
    sums = lax.fori_loop(1, 2, first_grad, sums)
    serve(9.2)
    sums = lax.fori_loop(2, 3, first_grad, sums)
    serve(10.3)

    def held(j):
        return rows_at(PAD + j * z.own_step, z.own_step)

    own_sum[2][0:1] = jnp.sum(sums[0], axis=0, keepdims=True)
    own_sum[2][1:2] = jnp.sum(sums[1], axis=0, keepdims=True)
    reduce_start(2)
    serve(10.5)
    reduce_spread(2)
    early = len(pending)

    def block_out(j, carry):
        rows = own(j, z.own_block)
        normed = (s.act_two[rows] * scale_two + offset_two).astype(BF16)
        branch = jnp.dot(normed, s.w[0], preferred_element_type=F32)
        out[rows_at(j * z.own_block, z.own_block, 16)] = (s.x[rows].astype(F32) + branch).astype(BF16)
        return carry

    for j in range(3):
        block_out(j, 0)
        serve(12.0 + j)
    settle(early)
    early = len(pending)
    serve(19.0)

    three = reduce_finish(2)
    shift_one_grad, gain_one_grad = three[0:1], three[1:2]
    stats[0:1] = gain_one_grad
    stats[1:2] = shift_one_grad
    picked = jnp.concatenate([gain_two_grad, shift_two_grad, jnp.zeros((6, z.f), F32)], axis=0)
    stats[2:4, : z.share] = lax.dot_general(
        picked, chosen.astype(F32), NT, precision=lax.Precision.HIGHEST, preferred_element_type=F32
    )[0:2]
    first_b = scale_one * inv_one * gain_one_grad / count
    first_a = scale_one * shift_one_grad / count - mean_one * first_b

    def input_grad(j, carry):
        rows, at = own(j, z.own_step), rows_at(j * z.own_step, z.own_step, 16)
        grad = scale_one * s.taps[held(j), : z.c] - wide(s.live[rows], z.c) * (first_a + first_b * s.act[rows])
        out_grad[at] = (s.u[rows].astype(F32) + grad * s.slope[at].astype(F32)).astype(BF16)
        return carry

    lax.fori_loop(0, steps // 2, input_grad, 0)
    serve(20.5)
    lax.fori_loop(steps // 2, steps, input_grad, 0)
    serve(21.5)
    settle(early)
    early = len(pending)
    serve(28.0)
    settle(early)
    serve(99.0)

    settle()


def write_out(out, out_grad, stats, w_grad, *refs):
    outs, (rows, pieces, sem) = refs[:8], refs[8:]

    def copy(i, src, dst):
        made = pltpu.make_async_copy(src, dst, sem.at[i])
        made.start()
        return made

    pairs = ((out, outs[0]), (out_grad, outs[1]), (w_grad.at[1:4], outs[4]), (w_grad.at[0], outs[7]))
    copies = [copy(i, *pair) for i, pair in enumerate(pairs)]
    channels, share = rows.shape[1], pieces.shape[1]
    for i in range(2):
        rows[i] = stats[i : i + 1].reshape(channels)
        pieces[i] = stats[i + 2 : i + 3, :share].reshape(share)
    small = ((rows.at[0], outs[2]), (rows.at[1], outs[3]), (pieces.at[0], outs[5]), (pieces.at[1], outs[6]))
    copies += [copy(4 + i, *pair) for i, pair in enumerate(small)]
    for made in copies:
        made.wait()


def local(z, block_in, cotangent, lengths, gain_one, shift_one, dilated_w, gain_two, shift_two, point_w):
    names = scratch_of(z)
    hbm = pl.BlockSpec(memory_space=pl.ANY)
    vmem = pl.BlockSpec(memory_space=pltpu.VMEM)
    smem = pl.BlockSpec(memory_space=pltpu.SMEM)
    shape = jax.ShapeDtypeStruct
    big = shape((z.bins, z.c), BF16)
    held = pltpu.VMEM((z.bins, z.c), BF16)
    results = pl.pallas_call(
        functools.partial(kernel, z, tuple(names)),
        out_shape=(held, held, pltpu.VMEM((8, z.c), F32), pltpu.VMEM((4, z.share, z.c), F32)),
        in_specs=[hbm, hbm, smem, vmem, vmem, hbm, vmem, vmem, hbm],
        out_specs=(vmem,) * 4,
        scratch_shapes=list(names.values()),
        compiler_params=pltpu.CompilerParams(
            collective_id=0, has_side_effects=True, vmem_limit_bytes=VMEM_LIMIT
        ),
    )(
        block_in,
        cotangent,
        lengths,
        gain_one,
        shift_one,
        jnp.transpose(dilated_w, (1, 0, 2)),
        gain_two,
        shift_two,
        point_w,
    )
    row, piece = shape((z.c,), F32), shape((z.share,), F32)
    outs = pl.pallas_call(
        write_out,
        out_shape=(big, big, row, row, shape((3, z.share, z.c), F32), piece, piece, shape((z.share, z.c), F32)),
        in_specs=[vmem] * 4,
        out_specs=(hbm,) * 8,
        scratch_shapes=[
            pltpu.VMEM((2, z.c), F32),
            pltpu.VMEM((2, z.share), F32),
            pltpu.SemaphoreType.DMA((8,)),
        ],
        compiler_params=pltpu.CompilerParams(vmem_limit_bytes=2 * 2**20),
    )(*results)
    return (*outs[:4], jnp.transpose(outs[4], (1, 0, 2)), *outs[5:])


def solution(mesh):
    n_seq, n_ch = mesh.shape["seq"], mesh.shape["ch"]

    def run(block_in, cotangent, lengths, gain_one, shift_one, dilated_w, gain_two, shift_two, point_w):
        z = plan(
            n_seq, n_ch, block_in.shape[0], block_in.shape[1], dilated_w.shape[0] * n_ch, lengths.shape[0]
        )
        return local(
            z, block_in, cotangent, lengths, gain_one, shift_one, dilated_w, gain_two, shift_two, point_w
        )

    return jax.shard_map(
        run,
        mesh=mesh,
        in_specs=(
            P(("seq", "ch"), None),
            P(("seq", "ch"), None),
            P(),
            P(),
            P(),
            P("ch", None, None),
            P("ch"),
            P("ch"),
            P("ch", None),
        ),
        out_specs=(
            P(("seq", "ch"), None),
            P(("seq", "ch"), None),
            P(),
            P(),
            P("ch", None, None),
            P("ch"),
            P("ch"),
            P("ch", None),
        ),
        check_vma=False,
    )
```

```python
import functools
import types

import jax
import jax.numpy as jnp
from jax import lax
from jax.experimental import pallas as pl
from jax.experimental.pallas import tpu as pltpu
from jax.sharding import PartitionSpec as P

DILATION = 17
EPS = 0.001
HALO = 48
PAD = 24
LANES = 128
LINE = 4
VMEM_LIMIT = 57 * 2**20
MESH = pl.DeviceIdType.MESH
F32 = jnp.float32
BF16 = jnp.bfloat16
NT = (((1,), (1,)), ((), ()))
TN = (((0,), (0,)), ((), ()))
GELU_A = 0.7978845608028654
GELU_B = GELU_A * 0.044715


def gelu_half(v):
    square = v * v
    half = 0.5 + 0.5 * jnp.tanh(v * (GELU_A + GELU_B * square))
    return half, square


def gelu_slope(v, half, square):
    return half + (2.0 * v) * (half * (1.0 - half)) * (GELU_A + 3.0 * GELU_B * square)


def wide(mask, width):
    return jnp.concatenate([mask] * (width // LANES), axis=1)


def fold(value):
    rows, width = value.shape
    return jnp.sum(value.reshape(rows // 8, 8, width), axis=0)


def rows_at(start, size, step=8):
    return pl.ds(pl.multiple_of(start, step), size)


def plan(n_seq, n_ch, bins, channels, mid, n_windows):
    z = types.SimpleNamespace()
    z.n_seq, z.n_ch = n_seq, n_ch
    z.bins, z.c, z.f, z.n_windows = bins, channels, mid, n_windows
    z.share = mid // n_ch
    z.n_x = n_ch // 2
    z.n_chips = n_seq * z.n_x
    z.window = bins * n_ch * n_seq // n_windows
    z.pair_windows = 2 * bins // z.window
    z.lines = n_seq // (2 * LINE)
    z.swaps = 1 + z.lines.bit_length()
    z.doublings = z.swaps
    z.ext = bins + HALO
    assert n_ch % 2 == 0 and n_seq == 2 * LINE << (z.swaps - 2)
    assert 2 * bins % z.window == 0 and HALO >= 2 * DILATION
    z.ext_step = z.ext // 9
    z.ext_block = z.ext // 3
    z.own_step = bins // 8
    z.own_block = bins // 3
    assert z.ext_step % 16 == 0 and z.own_step % 16 == 0
    z.thirds = 3
    z.third = channels // z.thirds
    z.half = z.third // 2
    z.near = z.share // 2
    return z


def scratch_of(z):
    dma = pltpu.SemaphoreType.DMA
    vmem = pltpu.VMEM
    return dict(
        x=vmem((z.ext, z.c), BF16),
        u=vmem((z.ext, z.c), BF16),
        x_edge=vmem((HALO, z.c), BF16),
        u_edge=vmem((HALO, z.c), BF16),
        act=vmem((z.ext, z.c), F32),
        slope=vmem((z.bins, z.c), BF16),
        normed=vmem((z.ext, z.c), BF16),
        w=vmem((4, z.f, z.c), BF16),
        taps=vmem((z.ext + 2 * PAD, 3 * z.f), F32),
        grad_two=vmem((z.ext, z.f), F32),
        act_two=vmem((z.ext, z.f), F32),
        slope_two=vmem((z.ext, z.f), F32),
        shifted=vmem((z.bins, 3 * z.f), BF16),
        live=vmem((z.ext, LANES), F32),
        live_own=vmem((z.ext, LANES), F32),
        not_first=vmem((z.ext, LANES), F32),
        not_last=vmem((z.ext, LANES), F32),
        gains=vmem((z.n_ch, 8, z.f), F32),
        **{f"own_sum_{i}": vmem((2, z.c), F32) for i in range(3)},
        **{f"pair_sum_{i}": vmem((2, z.c), F32) for i in range(3)},
        **{f"chip_sum_{i}": vmem((z.n_chips, 2, z.c), F32) for i in range(3)},
        centred=vmem((z.bins, z.f), BF16),
        point=vmem((z.f, z.c), F32),
        part=vmem((4, z.thirds, z.f, z.third), BF16),
        **{f"from_core_{p}": vmem((z.n_x, z.thirds, z.share, z.third), BF16) for p in range(4)},
        to_x=vmem((3, z.n_x - 1, z.thirds, z.share, z.third), BF16),
        from_x=vmem((3, z.n_x - 1, z.thirds, z.share, z.third), BF16),
        held=vmem((3, z.thirds, z.share, z.third), F32),
        to_inner=vmem((3, z.thirds, z.share, z.third), BF16),
        from_end=vmem((3, z.thirds, z.share, z.third), BF16),
        to_swap=vmem((z.swaps, 3, z.thirds, z.share, z.third), BF16),
        from_swap=vmem((z.swaps, 3, z.thirds, z.share, z.third), BF16),
        final=vmem((3, z.thirds, z.share, z.third), BF16),
        held_side=vmem((z.thirds, z.n_x, z.share, z.half), F32),
        to_side=vmem((z.thirds, z.n_x, z.share, z.half), BF16),
        from_side=vmem((z.thirds, z.n_x, z.share, z.half), BF16),
        held_far=vmem((z.thirds, z.share, z.half), F32),
        to_far=vmem((z.thirds, z.n_x, z.share, z.half), BF16),
        from_far=vmem((z.thirds, z.n_x, z.share, z.half), BF16),
        to_z=vmem((z.doublings, z.thirds, z.share, z.half), BF16),
        from_z=vmem((z.doublings, z.thirds, z.share, z.half), BF16),
        mine=vmem((z.thirds, z.share, z.half), BF16),
        other=vmem((z.thirds, z.share, z.half), BF16),
        local_sem=dma((6,)),
        halo_send=dma((2,)),
        halo_recv=dma((2,)),
        gain_send=dma((z.n_ch,)),
        gain_recv=dma((z.n_ch,)),
        w_send=dma((4, z.n_x, 4)),
        w_recv=dma((4, z.n_x, 4)),
        pair_send=dma((3,)),
        pair_recv=dma((3,)),
        chip_send=dma((3, z.n_chips)),
        chip_recv=dma((3, z.n_chips)),
        core_send=dma((4, z.n_x)),
        core_recv=dma((4, z.n_x)),
        x_send=dma((4, z.thirds, z.n_x)),
        x_recv=dma((4, z.thirds, z.n_x)),
        inner_send=dma((4, z.thirds)),
        inner_recv=dma((4, z.thirds)),
        swap_send=dma((z.swaps, 4, z.thirds)),
        swap_recv=dma((z.swaps, 4, z.thirds)),
        final_send=dma((4, z.thirds)),
        final_recv=dma((4, z.thirds)),
        side_send=dma((z.thirds,)),
        side_recv=dma((z.thirds,)),
        far_send=dma((z.thirds, z.n_x)),
        far_recv=dma((z.thirds, z.n_x)),
        z_send=dma((z.doublings, z.thirds)),
        z_recv=dma((z.doublings, z.thirds)),
        back_send=dma((z.thirds,)),
        back_recv=dma((z.thirds,)),
    )


def kernel(
    z,
    names,
    x_hbm,
    cot_hbm,
    lengths,
    gain_one,
    shift_one,
    taps_hbm,
    gain_two,
    shift_two,
    point_hbm,
    out,
    out_grad,
    stats,
    w_grad,
    *scratch,
):
    s = types.SimpleNamespace(**dict(zip(names, scratch)))
    seq, ch = lax.axis_index("seq"), lax.axis_index("ch")
    x_at, core = ch // 2, ch % 2
    slow, y_at = seq // 2, seq % 2
    chip = seq * z.n_x + x_at
    partner = (seq, x_at * 2 + 1 - core)
    y_peer = (slow * 2 + 1 - y_at, ch)
    own0 = core * HALO
    pending = []
    own_sum = (s.own_sum_0, s.own_sum_1, s.own_sum_2)
    pair_sum = (s.pair_sum_0, s.pair_sum_1, s.pair_sum_2)
    chip_sum = (s.chip_sum_0, s.chip_sum_1, s.chip_sum_2)
    from_core = (s.from_core_0, s.from_core_1, s.from_core_2, s.from_core_3)

    def remote(src, dst, send_sem, recv_sem, device):
        return pltpu.make_async_remote_copy(
            src_ref=src,
            dst_ref=dst,
            send_sem=send_sem,
            recv_sem=recv_sem,
            device_id=device,
            device_id_type=MESH,
        )

    def send(*copy):
        made = remote(*copy)
        made.start()
        pending.append(made)

    def chip_device(q):
        return (q // z.n_x, (q % z.n_x) * 2 + core)

    def other_chip(j):
        return (chip + 1 + j) % z.n_chips

    def own(j, size):
        return rows_at(own0 + j * size, size, 16)

    def column(k):
        return slice(k * z.f, (k + 1) * z.f)

    load_x = pltpu.make_async_copy(x_hbm, s.x.at[rows_at(own0, z.bins, 16)], s.local_sem.at[0])
    load_x.start()
    load_u = pltpu.make_async_copy(cot_hbm, s.u.at[rows_at(own0, z.bins, 16)], s.local_sem.at[1])
    load_u.start()
    own_rows = rows_at(ch * z.share, z.share, 16)
    sources = [point_hbm, taps_hbm.at[0], taps_hbm.at[1], taps_hbm.at[2]]
    load_w = [
        pltpu.make_async_copy(src, s.w.at[p, own_rows], s.local_sem.at[2 + p]) for p, src in enumerate(sources)
    ]
    for made in load_w:
        made.start()

    barrier = pltpu.get_barrier_semaphore()

    def greet(j, carry):
        pl.semaphore_signal(barrier, inc=1, device_id=chip_device(other_chip(j)), device_id_type=MESH)
        return carry

    for i in range(z.n_x):
        across = (seq, ((x_at + i) % z.n_x) * 2 + 1 - core)
        pl.semaphore_signal(barrier, inc=1, device_id=across, device_id_type=MESH)
    lax.fori_loop(0, z.n_chips - 1, greet, 0)

    pair = (seq * z.n_ch + ch) // 2
    window_lengths = [lengths[pair * z.pair_windows + i] for i in range(z.pair_windows)]

    def make_masks(j, total):
        rows = rows_at(j * z.ext_step, z.ext_step, 16)
        at = lax.broadcasted_iota(jnp.int32, (z.ext_step, LANES), 0) + j * z.ext_step
        place = at + core * (z.bins - HALO)
        inside, limit = place, jnp.full(place.shape, window_lengths[0], jnp.int32)
        for i in range(1, z.pair_windows):
            past = place >= i * z.window
            inside = jnp.where(past, place - i * z.window, inside)
            limit = jnp.where(past, window_lengths[i], limit)
        live = (inside < limit).astype(F32)
        mine = ((at >= own0) & (at < own0 + z.bins)).astype(F32)
        s.live[rows] = live
        s.live_own[rows] = live * mine
        s.not_first[rows] = (inside >= DILATION).astype(F32)
        s.not_last[rows] = (inside < z.window - DILATION).astype(F32)
        return total + fold(live * mine)

    live_rows = lax.fori_loop(0, z.ext // z.ext_step, make_masks, jnp.zeros((8, LANES), F32))
    own_count = jnp.maximum(wide(jnp.sum(live_rows, axis=0, keepdims=True), z.f), 1.0)
    bin_total = lax.fori_loop(0, z.n_windows, lambda i, t: t + lengths[i], jnp.int32(0))
    count = jnp.full((1, z.c), bin_total, jnp.int32).astype(F32)
    count_two = count[:, : z.f]
    s.taps[0:PAD] = jnp.zeros((PAD, 3 * z.f), F32)
    s.taps[PAD + z.ext : 2 * PAD + z.ext] = jnp.zeros((PAD, 3 * z.f), F32)

    chosen = lax.broadcasted_iota(jnp.int32, (z.share, z.f), 1) == (
        lax.broadcasted_iota(jnp.int32, (z.share, z.f), 0) + ch * z.share
    )
    both = [v[...].astype(F32).reshape(1, z.share) for v in (gain_two, shift_two)]
    both = jnp.concatenate(both + [jnp.zeros((6, z.share), F32)], axis=0)
    placed = jnp.dot(both.astype(BF16), chosen.astype(BF16), preferred_element_type=F32)
    s.gains[pl.ds(ch, 1)] = placed.reshape(1, 8, z.f)

    load_x.wait()

    def first_act(j, carry):
        rows = own(j, z.own_step)
        v = s.x[rows].astype(F32)
        half, _ = gelu_half(v)
        act = v * half
        s.act[rows] = act
        masked = wide(s.live[rows], z.c) * act
        return carry[0] + fold(masked), carry[1] + fold(masked * act)

    zero = jnp.zeros((8, z.c), F32)
    steps = z.bins // z.own_step
    sums = lax.fori_loop(0, steps // 2, first_act, (zero, zero))

    pl.semaphore_wait(barrier, z.n_chips - 1 + z.n_x)

    near0 = y_at * z.near

    def slot_at(i, c_slot):
        return ((x_at + i) % z.n_x) * 2 + c_slot

    def half_rows(slot, y_half):
        return rows_at(slot * z.share + y_half * z.near, z.near, 16)

    def x_rows(slot, p):
        return half_rows(slot, y_at) if p else rows_at(slot * z.share, z.share, 16)

    def w_copy(kind, i, p, src, rows, to):
        return remote(src, s.w.at[p, rows], s.w_send.at[kind, i, p], s.w_recv.at[kind, i, p], to)

    def w_along(p):
        for i in range(1, z.n_x):
            made = w_copy(
                0,
                i,
                p,
                sources[p].at[rows_at(near0, z.near, 16)] if p else sources[p],
                x_rows(ch, p),
                (seq, slot_at(i, core)),
            )
            made.start()
            pending.append(made)

    def w_across(p):
        made = w_copy(0, 0, p, sources[p], own_rows, partner)
        made.start()
        pending.append(made)

    w_along(1)
    w_along(2)

    def w_pass(kind, p):
        for i in range(1, z.n_x):
            slot = slot_at(z.n_x - i, core)
            rows = x_rows(slot, p) if kind == 0 else half_rows(slot, 1 - y_at)
            here = s.w.at[p, rows]
            w_copy(kind, i, p, here, rows, partner).wait_recv()
            onward = [w_copy(2 + kind, i, p, here, rows, partner)]
            if kind == 0 and p:
                onward.append(w_copy(1, i, p, here, rows, y_peer))
            for made in onward:
                made.start()
                pending.append(made)

    def w_here(p):
        load_w[p].wait()
        whole = rows_at(slot_at(0, 1 - core) * z.share, z.share, 16)
        w_copy(0, 0, p, sources[p], whole, partner).wait_recv()
        for i in range(1, z.n_x):
            slot = slot_at(z.n_x - i, 1 - core)
            for kind in range(2 if p else 1):
                rows = x_rows(slot, p) if kind == 0 else half_rows(slot, 1 - y_at)
                w_copy(2 + kind, i, p, s.w.at[p, rows], rows, partner).wait_recv()

    def reduce_start(i):
        send(own_sum[i], pair_sum[i], s.pair_send.at[i], s.pair_recv.at[i], partner)

    def chip_copy(i, slot, j):
        return remote(
            chip_sum[i].at[slot],
            chip_sum[i].at[slot],
            s.chip_send.at[i, j],
            s.chip_recv.at[i, slot],
            chip_device(other_chip(j)),
        )

    def reduce_spread(i):
        remote(own_sum[i], pair_sum[i], s.pair_send.at[i], s.pair_recv.at[i], partner).wait_recv()
        chip_sum[i][pl.ds(chip, 1)] = (own_sum[i][...] + pair_sum[i][...]).reshape(1, 2, z.c)

        for j in range(z.n_chips - 1):
            made = chip_copy(i, chip, j)
            made.start()
            pending.append(made)

    def reduce_finish(i):
        for j in range(z.n_chips - 1):
            chip_copy(i, other_chip(j), j).wait_recv()
        return jnp.sum(chip_sum[i][...], axis=0)

    sums = lax.fori_loop(steps // 2, steps, first_act, sums)
    own_sum[0][0:1] = jnp.sum(sums[0], axis=0, keepdims=True)
    own_sum[0][1:2] = jnp.sum(sums[1], axis=0, keepdims=True)
    reduce_start(0)

    load_u.wait()

    def first_slope(j, total):
        rows = own(j, z.own_step)
        v = s.x[rows].astype(F32)
        half, square = gelu_half(v)
        s.slope[rows_at(j * z.own_step, z.own_step, 16)] = gelu_slope(v, half, square).astype(BF16)
        masked = s.u[rows].astype(F32) * wide(s.live[rows], z.c)
        s.u[rows] = masked.astype(BF16)
        return total + fold(masked)

    def halo_rows():
        return rows_at((1 - core) * z.bins, HALO, 16)

    reduce_spread(0)
    w_along(3)
    w_along(0)
    w_across(1)
    w_across(2)

    away = (1 - core) * (z.bins - HALO)
    halo_copies = [
        remote(src.at[rows_at(away, HALO, 16)], dst, s.halo_send.at[i], s.halo_recv.at[i], partner)
        for i, (src, dst) in enumerate(((x_hbm, s.x_edge), (cot_hbm, s.u_edge)))
    ]
    for made in halo_copies:
        made.start()
        pending.append(made)
    w_across(3)
    w_across(0)
    for i in range(1, z.n_ch):
        send(
            s.gains.at[pl.ds(ch, 1)],
            s.gains.at[pl.ds(ch, 1)],
            s.gain_send.at[i],
            s.gain_recv.at[ch],
            (seq, (ch + i) % z.n_ch),
        )
    u_sum = lax.fori_loop(0, steps // 2, first_slope, zero)
    w_pass(0, 1)
    w_pass(0, 2)
    u_sum = lax.fori_loop(steps // 2, steps, first_slope, u_sum)
    for made in halo_copies:
        made.wait_recv()
    edge = s.x_edge[...].astype(F32)
    s.act[halo_rows()] = edge * gelu_half(edge)[0]
    s.u[halo_rows()] = (s.u_edge[...].astype(F32) * wide(s.live[halo_rows()], z.c)).astype(BF16)
    w_pass(0, 3)
    w_pass(1, 1)
    u_sum = jnp.sum(u_sum, axis=0, keepdims=True)

    for i in range(1, z.n_ch):
        slot = (ch + i) % z.n_ch
        remote(
            s.gains.at[pl.ds(slot, 1)],
            s.gains.at[pl.ds(slot, 1)],
            s.gain_send.at[i],
            s.gain_recv.at[slot],
            (seq, slot),
        ).wait_recv()
    both = s.gains[0]
    for i in range(1, z.n_ch):
        both = both + s.gains[i]
    whole_gain, whole_shift = both[0:1], both[1:2]

    one = reduce_finish(0)
    mean_one = one[0:1] / count
    inv_one = lax.rsqrt(one[1:2] / count - mean_one * mean_one + EPS)
    scale_one = gain_one[...].astype(F32).reshape(1, z.c) * inv_one
    offset_one = shift_one[...].astype(F32).reshape(1, z.c) - mean_one * scale_one

    def convolve(first, last):
        def step(j, carry):
            s.taps[rows_at(PAD + j * z.ext_block, z.ext_block), first * z.f : last * z.f] = lax.dot_general(
                s.normed[rows_at(j * z.ext_block, z.ext_block, 16)],
                s.w[first + 1 : last + 1].reshape((last - first) * z.f, z.c),
                NT,
                preferred_element_type=F32,
            )
            return carry

        lax.fori_loop(0, 3, step, 0)

    w_pass(1, 2)
    w_here(1)

    def first_norm(j, carry):
        rows = rows_at(j * z.ext_block, z.ext_block, 16)
        normed = (s.act[rows] * scale_one + offset_one).astype(BF16)
        s.normed[rows] = normed
        s.taps[rows_at(PAD + j * z.ext_block, z.ext_block), : z.f] = lax.dot_general(
            normed, s.w[1], NT, preferred_element_type=F32
        )
        return carry

    lax.fori_loop(0, 3, first_norm, 0)
    w_pass(0, 0)
    w_pass(1, 3)
    w_here(2)
    w_here(3)
    convolve(1, 3)
    w_here(0)

    def before(start, size, columns):
        return s.taps[rows_at(start, size + 8), columns][PAD - DILATION : PAD - DILATION + size]

    def after(start, size, columns):
        low = (PAD + DILATION) // 8 * 8
        skip = PAD + DILATION - low
        return s.taps[rows_at(start + low, size + 8), columns][skip : skip + size]

    def second_act(j, carry):
        start, size = j * z.ext_block, z.ext_block
        rows = rows_at(start, size, 16)
        grad = lax.dot_general(s.u[rows], s.w[0], NT, preferred_element_type=F32)
        s.grad_two[rows] = grad
        hidden = (
            s.taps[rows_at(PAD + start, size), column(1)]
            + wide(s.not_first[rows], z.f) * before(start, size, column(0))
            + wide(s.not_last[rows], z.f) * after(start, size, column(2))
        )
        half, square = gelu_half(hidden)
        act = hidden * half
        s.act_two[rows] = act
        s.slope_two[rows] = gelu_slope(hidden, half, square)
        mask = wide(s.live_own[rows], z.f)
        masked, grad = mask * act, mask * grad
        terms = (masked, masked * act, grad, grad * act)
        return tuple(total + fold(term) for total, term in zip(carry, terms))

    zero_two = jnp.zeros((8, z.f), F32)
    sums = lax.fori_loop(0, 3, second_act, (zero_two,) * 4)
    sums = [jnp.sum(v, axis=0, keepdims=True) for v in sums]
    own_sum[1][0:1, : z.f] = sums[0]
    own_sum[1][0:1, z.f :] = sums[1]
    own_sum[1][1:2, : z.f] = sums[2]
    own_sum[1][1:2, z.f :] = sums[3]
    reduce_start(1)
    own_mean = sums[0] / own_count

    def centre(j, carry):
        s.centred[rows_at(j * z.own_step, z.own_step, 16)] = (s.act_two[own(j, z.own_step)] - own_mean).astype(BF16)
        return carry

    lax.fori_loop(0, steps, centre, 0)
    reduce_spread(1)
    own_all = rows_at(own0, z.bins, 16)
    s.point[...] = lax.dot_general(s.centred[...], s.u[own_all], TN, preferred_element_type=F32)
    two = reduce_finish(1)
    mean_two = two[0:1, : z.f] / count_two
    inv_two = lax.rsqrt(two[0:1, z.f :] / count_two - mean_two * mean_two + EPS)
    shift_two_grad = two[1:2, : z.f]
    gain_two_grad = inv_two * (two[1:2, z.f :] - mean_two * shift_two_grad)
    scale_two = whole_gain * inv_two
    offset_two = whole_shift - mean_two * scale_two
    back_b = scale_two * inv_two * gain_two_grad / count_two
    back_a = scale_two * shift_two_grad / count_two - mean_two * back_b

    def second_back(j, carry):
        rows = rows_at(j * z.ext_step, z.ext_step, 16)
        grad = scale_two * s.grad_two[rows] - wide(s.live[rows], z.f) * (back_a + back_b * s.act_two[rows])
        s.taps[rows_at(PAD + j * z.ext_step, z.ext_step), column(2)] = grad * s.slope_two[rows]
        return carry

    def slot_rows(x_slot, c_slot):
        return rows_at((x_slot * 2 + c_slot) * z.share, z.share, 16)

    def launch(made):
        made.start()
        pending.append(made)

    def settle(until=None):
        done = pending[:until]
        del pending[:until]
        for made in done:
            if not isinstance(made, tuple):
                made.wait_send()
        for which in (inner, at_end):
            mine = [made[1] for made in done if isinstance(made, tuple) and made[0] is which]

            @pl.when(which)
            def _():
                for copy in mine:
                    copy().wait_send()

    def hold(p, value):
        for part in range(z.thirds):
            s.part[p, part] = value[:, part * z.third : (part + 1) * z.third].astype(BF16)
        for i in range(z.n_x):
            launch(core_copy(p, i))

    def core_copy(p, i):
        return remote(
            s.part.at[p, :, slot_rows(i, 1 - core)],
            from_core[p].at[i],
            s.core_send.at[p, i],
            s.core_recv.at[p, i],
            partner,
        )

    def chip_part(p, part, to):
        return s.part[p, part, slot_rows(to, core)].astype(F32) + from_core[p][to, part].astype(F32)

    def x_copy(p, part, i):
        return remote(
            s.to_x.at[p, i - 1, part],
            s.from_x.at[p, i - 1, part],
            s.x_send.at[p, part, i],
            s.x_recv.at[p, part, i],
            (seq, slot_at(i, core)),
        )

    def x_stage(p):
        for i in range(z.n_x):
            core_copy(p, i).wait_recv()
        for part in range(z.thirds):
            for i in range(1, z.n_x):
                s.to_x[p, i - 1, part] = chip_part(p, part, (x_at + i) % z.n_x).astype(BF16)
                launch(x_copy(p, part, i))

    def x_sum(p, part):
        value = chip_part(p, part, x_at)
        for i in range(1, z.n_x):
            x_copy(p, part, i).wait_recv()
            value = value + s.from_x[p, i - 1, part].astype(F32)
        return value

    place = slow % LINE
    inner = place * (LINE - 1 - place) > 0
    at_end = place * (LINE - 1 - place) == 0
    beside = (slow + 1 - 2 * (slow % 2)) * 2 + y_at
    swap_with = [(slow + 3 - 2 * place) * 2 + y_at]
    for step in range(z.swaps - 2):
        far = LINE << step
        swap_with.append((slow + far - 2 * far * (slow // far % 2)) * 2 + y_at)
    swap_with.append(slow * 2 + 1 - y_at)

    def inner_copy(p, part):
        return remote(
            s.to_inner.at[p, part],
            s.from_end.at[p, part],
            s.inner_send.at[p, part],
            s.inner_recv.at[p, part],
            (beside, ch),
        )

    def swap_copy(step, p, part):
        return remote(
            s.to_swap.at[step, p, part],
            s.from_swap.at[step, p, part],
            s.swap_send.at[step, p, part],
            s.swap_recv.at[step, p, part],
            (swap_with[step], ch),
        )

    def final_copy(p, part):
        return remote(
            s.final.at[p, part],
            s.final.at[p, part],
            s.final_send.at[p, part],
            s.final_recv.at[p, part],
            (beside, ch),
        )

    def launch_if(which, copy, *at):
        copy(*at).start()
        pending.append((which, functools.partial(copy, *at)))

    def gather_stage(p, part):
        value = x_sum(p, part)

        @pl.when(inner)
        def _():
            s.held[p, part] = value

        @pl.when(at_end)
        def _():
            s.to_inner[p, part] = value.astype(BF16)
            launch_if(at_end, inner_copy, p, part)

    def swapped(step, p, part):
        swap_copy(step, p, part).wait_recv()
        return s.to_swap[step, p, part].astype(F32) + s.from_swap[step, p, part].astype(F32)

    def swap_stage(step, p, part):
        @pl.when(inner)
        def _():
            if step == 0:
                inner_copy(p, part).wait_recv()
                value = s.held[p, part] + s.from_end[p, part].astype(F32)
            else:
                value = swapped(step - 1, p, part)
            s.to_swap[step, p, part] = value.astype(BF16)
            launch_if(inner, swap_copy, step, p, part)

    def keep(p, part):
        w_grad[p, :, part * z.third : (part + 1) * z.third] = s.final[p, part].astype(F32)

    def final_stage(p, part):
        @pl.when(inner)
        def _():
            s.final[p, part] = swapped(z.swaps - 1, p, part).astype(BF16)
            launch_if(inner, final_copy, p, part)
            keep(p, part)

    def last_stage(p, part):
        @pl.when(at_end)
        def _():
            final_copy(p, part).wait_recv()
            keep(p, part)

    def split(value):
        left, right = value[:, : z.half], value[:, z.half :]
        return jnp.where(y_at == 0, left, right), jnp.where(y_at == 0, right, left)

    def side_copy(part):
        return remote(
            s.to_side.at[part], s.from_side.at[part], s.side_send.at[part], s.side_recv.at[part], y_peer
        )

    def side_stage():
        for i in range(z.n_x):
            core_copy(3, i).wait_recv()
        for part in range(z.thirds):
            for i in range(z.n_x):
                own_half, give = split(chip_part(3, part, (x_at + i) % z.n_x))
                s.held_side[part, i] = own_half
                s.to_side[part, i] = give.astype(BF16)
            launch(side_copy(part))

    def far_copy(part, i):
        return remote(
            s.to_far.at[part, i],
            s.from_far.at[part, i],
            s.far_send.at[part, i],
            s.far_recv.at[part, i],
            (seq, slot_at(i, core)),
        )

    def far_stage(part):
        side_copy(part).wait_recv()
        s.held_far[part] = s.held_side[part, 0] + s.from_side[part, 0].astype(F32)
        for i in range(1, z.n_x):
            s.to_far[part, i] = (s.held_side[part, i] + s.from_side[part, i].astype(F32)).astype(BF16)
            launch(far_copy(part, i))

    def z_copy(step, part):
        far = 1 << step
        to = slow + far - 2 * far * (slow // far % 2)
        return remote(
            s.to_z.at[step, part],
            s.from_z.at[step, part],
            s.z_send.at[step, part],
            s.z_recv.at[step, part],
            (to * 2 + y_at, ch),
        )

    def z_sum(step, part):
        z_copy(step, part).wait_recv()
        return s.to_z[step, part].astype(F32) + s.from_z[step, part].astype(F32)

    def z_stage(step, part):
        if step == 0:
            value = s.held_far[part]
            for i in range(1, z.n_x):
                far_copy(part, i).wait_recv()
                value = value + s.from_far[part, i].astype(F32)
        else:
            value = z_sum(step - 1, part)
        s.to_z[step, part] = value.astype(BF16)
        launch(z_copy(step, part))

    def back_copy(part):
        return remote(s.mine.at[part], s.other.at[part], s.back_send.at[part], s.back_recv.at[part], y_peer)

    def back_stage(part):
        s.mine[part] = z_sum(z.doublings - 1, part).astype(BF16)
        launch(back_copy(part))

    def join_stage(part):
        back_copy(part).wait_recv()
        for side, half in ((y_at, s.mine), (1 - y_at, s.other)):
            lanes = rows_at(part * z.third + side * z.half, z.half, LANES)
            w_grad[3, :, lanes] = half[part].astype(F32)

    todo = []
    for n in range(3 * z.thirds):
        p, part = n // z.thirds, n % z.thirds
        at = 5.2 + 1.07 * n
        todo.append((at, functools.partial(gather_stage, p, part)))
        for step in range(z.swaps):
            todo.append((at + 3.6 * (step + 1), functools.partial(swap_stage, step, p, part)))
        todo.append((at + 3.6 * (z.swaps + 1), functools.partial(final_stage, p, part)))
        todo.append((at + 3.6 * (z.swaps + 2), functools.partial(last_stage, p, part)))
    for part in range(z.thirds):
        at = 11.4 + 1.07 * part
        todo.append((at, functools.partial(far_stage, part)))
        for step in range(z.doublings):
            todo.append((at + 3.0 + 3.2 * step, functools.partial(z_stage, step, part)))
        todo.append((at + 4.0 + 3.2 * z.doublings, functools.partial(back_stage, part)))
        todo.append((at + 7.0 + 3.2 * z.doublings, functools.partial(join_stage, part)))
    todo.sort(key=lambda item: item[0])

    def serve(until):
        while todo and todo[0][0] <= until:
            todo.pop(0)[1]()

    def down(row):
        return wide(jnp.transpose(jnp.broadcast_to(row, (LANES, z.f))), z.c)

    hold(0, down(scale_two) * s.point[...] + down(scale_two * (own_mean - mean_two) + whole_shift) * u_sum)
    blocks = z.ext // z.ext_step
    lax.fori_loop(0, blocks // 2, second_back, 0)
    x_stage(0)
    lax.fori_loop(blocks // 2, blocks, second_back, 0)

    def shift_rows(j, carry):
        start, size = own0 + j * z.own_step, z.own_step
        rows = rows_at(start, size, 16)
        to = rows_at(j * size, size, 16)
        later = wide(s.not_last[rows], z.f) * after(start, size, column(2))
        earlier = wide(s.not_first[rows], z.f) * before(start, size, column(2))
        s.shifted[to, column(0)] = later.astype(BF16)
        s.shifted[to, column(1)] = s.taps[rows_at(PAD + start, size), column(2)].astype(BF16)
        s.shifted[to, column(2)] = earlier.astype(BF16)
        return carry

    lax.fori_loop(0, z.bins // z.own_step, shift_rows, 0)
    for k in range(3):
        hold(
            k + 1,
            lax.dot_general(s.shifted[:, column(k)], s.normed[own_all], TN, preferred_element_type=F32),
        )
        if k > 0:
            x_stage(k)
            serve((0.0, 5.3, 6.4)[k])

    offset_back = -mean_one * inv_one

    def first_grad(j, carry):
        rows = rows_at(j * z.own_block, z.own_block, 16)
        grad = jnp.dot(s.shifted[rows], s.w[1:4].reshape(3 * z.f, z.c), preferred_element_type=F32)
        s.taps[rows_at(PAD + j * z.own_block, z.own_block), : z.c] = grad
        centred = s.act[own(j, z.own_block)] * inv_one + offset_back
        return carry[0] + fold(grad), carry[1] + fold(grad * centred)

    sums = (zero, zero)
    sums = lax.fori_loop(0, 1, first_grad, sums)
    side_stage()
    serve(8.0)
    sums = lax.fori_loop(1, 2, first_grad, sums)
    serve(9.2)
    sums = lax.fori_loop(2, 3, first_grad, sums)
    serve(10.3)

    def held(j):
        return rows_at(PAD + j * z.own_step, z.own_step)

    own_sum[2][0:1] = jnp.sum(sums[0], axis=0, keepdims=True)
    own_sum[2][1:2] = jnp.sum(sums[1], axis=0, keepdims=True)
    reduce_start(2)
    reduce_spread(2)
    serve(11.0)
    early = len(pending)

    def block_out(j, carry):
        rows = own(j, z.own_block)
        normed = (s.act_two[rows] * scale_two + offset_two).astype(BF16)
        branch = jnp.dot(normed, s.w[0], preferred_element_type=F32)
        out[rows_at(j * z.own_block, z.own_block, 16)] = (s.x[rows].astype(F32) + branch).astype(BF16)
        return carry

    for j in range(3):
        block_out(j, 0)
        serve(12.0 + j)
    settle(early)
    early = len(pending)
    serve(20.5)

    three = reduce_finish(2)
    shift_one_grad, gain_one_grad = three[0:1], three[1:2]
    stats[0:1] = gain_one_grad
    stats[1:2] = shift_one_grad
    picked = jnp.concatenate([gain_two_grad, shift_two_grad, jnp.zeros((6, z.f), F32)], axis=0)
    stats[2:4, : z.share] = lax.dot_general(
        picked, chosen.astype(F32), NT, precision=lax.Precision.HIGHEST, preferred_element_type=F32
    )[0:2]
    first_b = scale_one * inv_one * gain_one_grad / count
    first_a = scale_one * shift_one_grad / count - mean_one * first_b

    def input_grad(j, carry):
        rows, at = own(j, z.own_step), rows_at(j * z.own_step, z.own_step, 16)
        grad = scale_one * s.taps[held(j), : z.c] - wide(s.live[rows], z.c) * (first_a + first_b * s.act[rows])
        out_grad[at] = (s.u[rows].astype(F32) + grad * s.slope[at].astype(F32)).astype(BF16)
        return carry

    lax.fori_loop(0, steps // 2, input_grad, 0)
    serve(21.5)
    lax.fori_loop(steps // 2, steps, input_grad, 0)
    serve(22.5)
    settle(early)
    early = len(pending)
    serve(28.0)
    settle(early)
    serve(99.0)

    settle()


def write_out(out, out_grad, stats, w_grad, *refs):
    outs, (rows, pieces, sem) = refs[:8], refs[8:]

    def copy(i, src, dst):
        made = pltpu.make_async_copy(src, dst, sem.at[i])
        made.start()
        return made

    pairs = ((out, outs[0]), (out_grad, outs[1]), (w_grad.at[1:4], outs[4]), (w_grad.at[0], outs[7]))
    copies = [copy(i, *pair) for i, pair in enumerate(pairs)]
    channels, share = rows.shape[1], pieces.shape[1]
    for i in range(2):
        rows[i] = stats[i : i + 1].reshape(channels)
        pieces[i] = stats[i + 2 : i + 3, :share].reshape(share)
    small = ((rows.at[0], outs[2]), (rows.at[1], outs[3]), (pieces.at[0], outs[5]), (pieces.at[1], outs[6]))
    copies += [copy(4 + i, *pair) for i, pair in enumerate(small)]
    for made in copies:
        made.wait()


def local(z, block_in, cotangent, lengths, gain_one, shift_one, dilated_w, gain_two, shift_two, point_w):
    names = scratch_of(z)
    hbm = pl.BlockSpec(memory_space=pl.ANY)
    vmem = pl.BlockSpec(memory_space=pltpu.VMEM)
    smem = pl.BlockSpec(memory_space=pltpu.SMEM)
    shape = jax.ShapeDtypeStruct
    big = shape((z.bins, z.c), BF16)
    held = pltpu.VMEM((z.bins, z.c), BF16)
    results = pl.pallas_call(
        functools.partial(kernel, z, tuple(names)),
        out_shape=(held, held, pltpu.VMEM((8, z.c), F32), pltpu.VMEM((4, z.share, z.c), F32)),
        in_specs=[hbm, hbm, smem, vmem, vmem, hbm, vmem, vmem, hbm],
        out_specs=(vmem,) * 4,
        scratch_shapes=list(names.values()),
        compiler_params=pltpu.CompilerParams(
            collective_id=0, has_side_effects=True, vmem_limit_bytes=VMEM_LIMIT
        ),
    )(
        block_in,
        cotangent,
        lengths,
        gain_one,
        shift_one,
        jnp.transpose(dilated_w, (1, 0, 2)),
        gain_two,
        shift_two,
        point_w,
    )
    row, piece = shape((z.c,), F32), shape((z.share,), F32)
    outs = pl.pallas_call(
        write_out,
        out_shape=(big, big, row, row, shape((3, z.share, z.c), F32), piece, piece, shape((z.share, z.c), F32)),
        in_specs=[vmem] * 4,
        out_specs=(hbm,) * 8,
        scratch_shapes=[
            pltpu.VMEM((2, z.c), F32),
            pltpu.VMEM((2, z.share), F32),
            pltpu.SemaphoreType.DMA((8,)),
        ],
        compiler_params=pltpu.CompilerParams(vmem_limit_bytes=2 * 2**20),
    )(*results)
    return (*outs[:4], jnp.transpose(outs[4], (1, 0, 2)), *outs[5:])


def solution(mesh):
    n_seq, n_ch = mesh.shape["seq"], mesh.shape["ch"]

    def run(block_in, cotangent, lengths, gain_one, shift_one, dilated_w, gain_two, shift_two, point_w):
        z = plan(
            n_seq, n_ch, block_in.shape[0], block_in.shape[1], dilated_w.shape[0] * n_ch, lengths.shape[0]
        )
        return local(
            z, block_in, cotangent, lengths, gain_one, shift_one, dilated_w, gain_two, shift_two, point_w
        )

    return jax.shard_map(
        run,
        mesh=mesh,
        in_specs=(
            P(("seq", "ch"), None),
            P(("seq", "ch"), None),
            P(),
            P(),
            P(),
            P("ch", None, None),
            P("ch"),
            P("ch"),
            P("ch", None),
        ),
        out_specs=(
            P(("seq", "ch"), None),
            P(("seq", "ch"), None),
            P(),
            P(),
            P("ch", None, None),
            P("ch"),
            P("ch"),
            P("ch", None),
        ),
        check_vma=False,
    )
```
